32 devices in a mesh: row: 4 (over y, x), col: 8 (over z, core).
Axes of the slice: x: 2, y: 2, z: 4, core: 2. Of those that a mesh axis runs over, the one named last changes fastest.
Arguments:
- ham_tiles: float32 [4, 8, 320, 128, 128], P('row', 'col'), may hold values from -0.0625 to 0.0625
- tile_list: int32 [4, 8, 320, 2], P('row', 'col'), may hold values from 0 to 31, as said below
- tile_count: int32 [4, 8], P('row', 'col'), may hold values from 1 to 320, as said below
- basis_block: float32 [16, 16384], P(None, ('row', 'col')), may hold values from -6 to 6
- residual_block: float32 [16, 16384], P(None, ('row', 'col')), may hold values from -6 to 6
Outputs:
- h_basis: float32 [16, 16384], P(None, ('row', 'col'))
- h_residual: float32 [16, 16384], P(None, ('row', 'col'))
The draws below stay inside these ranges and needn't reach their ends.
Inputs may be any that keep to these rules, and one draw needn't show every extreme that they name: `tile_list`: entry 0 is a block row within the grid row, below 32; entry 1 a block column within the grid column, below 16. Live slots name distinct blocks with global row block at most the global column block; slots past the count name arbitrary blocks in range. `tile_count`: each device's count lies between half and all of its share of 320 in proportion to its upper-triangle slots, never above its distinct upper blocks; devices with the most upper-triangle slots hold exactly 320.
All inputs are finite; a program needn't handle non-finite values.
Results may differ from the reference program's by a relative error of at most 0.0003.
Values sent between devices are 32-bit elements; how exact they have to be, the bound alone decides.
No kernel may reach another device: no remote copies, remote signals or barrier semaphores. Data moves between devices by JAX's collectives and lax.ppermute only.
A program may use at most 128 MiB of HBM per device.

```python
import jax
import jax.numpy as jnp
from jax import lax

TILE = 128
VEC = 16
BP = 4
MAXT = 320
NB = 128
BR = 32
NSTATES = 16384
N_ROW = 4
N_COL = 8


def tile_layout(key):
    slots = BR * N_ROW * BP
    row_ids = jnp.arange(N_ROW, dtype=jnp.int32)[:, None, None, None]
    col_ids = jnp.arange(N_COL, dtype=jnp.int32)[None, :, None, None]
    local_rows = jnp.arange(BR, dtype=jnp.int32)[None, None, :, None]
    local_cols = jnp.arange(N_ROW * BP, dtype=jnp.int32)[None, None, None, :]
    global_row = row_ids * BR + local_rows
    global_col = local_cols // BP * BR + col_ids * BP + local_cols % BP
    upper = (global_row <= global_col).reshape(N_ROW, N_COL, slots)
    valid = jnp.sum(upper.astype(jnp.int32), axis=-1)
    most = jnp.max(valid)
    ceiling = jnp.maximum(1, MAXT * valid // most).astype(jnp.int32)
    floor_count = jnp.maximum(1, ceiling // 2).astype(jnp.int32)
    count_key = jax.random.fold_in(key, 7)
    drawn = jax.random.randint(count_key, (N_ROW, N_COL), floor_count, ceiling + 1, dtype=jnp.int32)
    counts = jnp.where(valid == most, jnp.int32(MAXT), drawn).astype(jnp.int32)
    scores_raw = jax.random.randint(key, (N_ROW, N_COL, slots), 0, 65536, dtype=jnp.int32)
    slot_ids = jnp.arange(slots, dtype=jnp.int32)
    scores = jnp.where(upper, scores_raw * slots + slot_ids, -1 - slot_ids)
    _, chosen = jax.lax.top_k(scores, MAXT)
    chosen = chosen.astype(jnp.int32)
    listing = jnp.stack([chosen // (N_ROW * BP), chosen % (N_ROW * BP)], axis=-1).astype(jnp.int32)
    return (listing, counts)


def draw_tile_list(key, part):
    listing, counts = tile_layout(key)
    return listing


def draw_tile_count(key, part):
    listing, counts = tile_layout(key)
    return counts


def steps_of(stream_key, extent, shards, least, top_value):
    gain = 1.0
    for axis_at, shards_of in shards:
        steps = jax.random.uniform(jax.random.fold_in(jax.random.fold_in(stream_key, 6), axis_at), (shards_of,), jnp.float32, least / len(shards), top_value / len(shards))
        gain = gain * jnp.repeat(jnp.exp(steps), extent[axis_at] // shards_of).reshape((-1,) + (1,) * (len(extent) - 1 - axis_at))
    return gain


def centred(stream_key, shape, deviation, limit, shards=(), kind=jnp.bfloat16):
    level = steps_of(stream_key, shape, shards, -0.22, 0.18) if shards else 1.0
    values = jax.random.normal(stream_key, shape, jnp.float32) * deviation * level
    return jnp.minimum(jnp.maximum(values, -limit), limit).astype(kind)


def setup_inputs(seed: int = 0) -> dict:
    keys = jax.random.split(jax.random.key(seed), 6)
    return {
        "ham_tiles": centred(keys[0], (N_ROW, N_COL, MAXT, TILE, TILE), (TILE * BP * 16) ** -0.5, 0.0625, ((0, 4), (1, 8)), jnp.float32),
        "tile_list": draw_tile_list(jax.random.fold_in(keys[5], 71), 0),
        "tile_count": draw_tile_count(jax.random.fold_in(keys[5], 71), 0),
        "basis_block": centred(keys[3], (VEC, NSTATES), 1.0, 6.0, ((1, 32),), jnp.float32),
        "residual_block": centred(keys[4], (VEC, NSTATES), 1.0, 6.0, ((1, 32),), jnp.float32),
    }


def reference(ham_tiles, tile_list, tile_count, basis_block, residual_block):
    panel = jnp.concatenate([basis_block, residual_block], axis=0)
    width = panel.shape[0]
    blocks = panel.reshape(width, NB, TILE)
    flat_tiles = ham_tiles.reshape(N_ROW * N_COL, MAXT, TILE, TILE)
    flat_list = tile_list.reshape(N_ROW * N_COL, MAXT, 2)
    flat_count = tile_count.reshape(N_ROW * N_COL)
    device_ids = jnp.arange(N_ROW * N_COL, dtype=jnp.int32)

    def step(carry, items):
        tile_data, listing, count, device = items
        row_index = device // N_COL
        col_index = device % N_COL
        local_row = listing[:, 0]
        local_col = listing[:, 1]
        global_row = (row_index * BR + local_row).astype(jnp.int32)
        global_col = ((local_col // BP) * BR + col_index * BP + local_col % BP).astype(jnp.int32)
        live = jnp.arange(MAXT, dtype=jnp.int32) < count
        is_diag = global_row == global_col
        masked = jnp.where(live[:, None, None], tile_data, jnp.float32(0.0))
        forward = jnp.where(is_diag[:, None, None], 0.5 * (masked + jnp.swapaxes(masked, 1, 2)), masked)
        transposed = jnp.where(is_diag[:, None, None], jnp.float32(0.0), masked)
        from_cols = blocks[:, global_col]
        from_rows = blocks[:, global_row]
        fwd_terms = jnp.einsum('vtb,tab->vta', from_cols, forward, precision=lax.Precision.HIGHEST)
        tr_terms = jnp.einsum('vta,tab->vtb', from_rows, transposed, precision=lax.Precision.HIGHEST)
        carry = carry.at[:, global_row].add(fwd_terms)
        carry = carry.at[:, global_col].add(tr_terms)
        return carry, None

    start = jnp.zeros((width, NB, TILE), jnp.float32)
    result, _ = lax.scan(step, start, (flat_tiles, flat_list, flat_count, device_ids))
    result = result.reshape(width, NB * TILE)
    return result[:VEC], result[VEC:]
```

```python
import functools

import jax
import jax.numpy as jnp
from jax import lax
from jax.experimental import pallas as pl
from jax.experimental.pallas import tpu as pltpu
from jax.sharding import PartitionSpec as P

CHUNK = 16
VMEM_LIMIT = 48 * 1024 * 1024


def split(x):
    high = x.astype(jnp.bfloat16)
    low = (x - high.astype(jnp.float32)).astype(jnp.bfloat16)
    return high, low


def product_kernel(forward, per_piece, n_row, n_col, list_ref, count_ref, tiles_ref, *refs):
    n_in, n_out = (n_row, n_col) if forward else (n_col, n_row)
    pieces, outs = refs[:n_in], refs[n_in:n_in + n_out]
    held, vecs, total, sems = refs[n_in + n_out:]
    side = tiles_ref.shape[-1]
    width = pieces[0].shape[0]
    row_at, col_at = lax.axis_index("row"), lax.axis_index("col")
    in_at, out_at = (row_at, col_at) if forward else (col_at, row_at)
    chunks = (count_ref[0, 0] + CHUNK - 1) // CHUNK

    def chunk_copy(k):
        part = pl.ds(k * CHUNK, CHUNK)
        return pltpu.make_async_copy(tiles_ref.at[part], held.at[part], sems.at[k])

    @pl.loop(0, chunks)
    def _(k):
        chunk_copy(k).start()

    for s in range(n_in):
        base = (in_at ^ s) * per_piece
        for b in range(per_piece):
            high, low = split(pieces[s][:, b * side:(b + 1) * side])
            vecs[base + b, :width, :side] = high
            vecs[base + b, :width, side:] = high
            vecs[base + b, width:, :side] = low
            vecs[base + b, width:, side:] = jnp.zeros_like(low)
    total[...] = jnp.zeros_like(total)

    @pl.loop(0, chunks)
    def _(k):
        chunk_copy(k).wait()
        for u in range(CHUNK):
            t = k * CHUNK + u
            i, j = list_ref[0, t], list_ref[1, t]
            row_block = row_at * (n_col * per_piece) + i
            col_block = j // per_piece * (n_col * per_piece) + col_at * per_piece + j % per_piece
            weight = jnp.where(row_block == col_block, 0.5, 1.0)
            weight = jnp.where(t < count_ref[0, 0], weight, 0.0).astype(jnp.float32)
            high, low = split(held[t])
            if forward:
                out = lax.dot_general(
                    vecs[j],
                    jnp.concatenate([high, low], axis=1),
                    (((1,), (1,)), ((), ())),
                    preferred_element_type=jnp.float32,
                )
                at = i
            else:
                out = jnp.dot(
                    vecs[i], jnp.concatenate([high, low], axis=0), preferred_element_type=jnp.float32
                )
                at = j
            total[at] += (out[:width] + out[width:]) * weight

    for s in range(n_out):
        base = (out_at ^ s) * per_piece
        for b in range(per_piece):
            outs[s][:, b * side:(b + 1) * side] = total[base + b]


def product(forward, per_piece, n_row, n_col, listing, count, tiles, pieces):
    slots, side = tiles.shape[0], tiles.shape[-1]
    width = pieces[0].shape[0]
    n_in, n_out = (n_row, n_col) if forward else (n_col, n_row)
    vmem = pl.BlockSpec(memory_space=pltpu.VMEM)
    smem = pl.BlockSpec(memory_space=pltpu.SMEM)
    return pl.pallas_call(
        functools.partial(product_kernel, forward, per_piece, n_row, n_col),
        out_shape=[jax.ShapeDtypeStruct(pieces[0].shape, jnp.float32)] * n_out,
        in_specs=[smem, smem, pl.BlockSpec(memory_space=pl.ANY)] + [vmem] * n_in,
        out_specs=[vmem] * n_out,
        scratch_shapes=[
            pltpu.VMEM((slots, side, side), jnp.float32),
            pltpu.VMEM((n_in * per_piece, 2 * width, 2 * side), jnp.bfloat16),
            pltpu.VMEM((n_out * per_piece, width, side), jnp.float32),
            pltpu.SemaphoreType.DMA((slots // CHUNK,)),
        ],
        compiler_params=pltpu.CompilerParams(vmem_limit_bytes=VMEM_LIMIT),
        cost_estimate=pl.CostEstimate(
            flops=slots * 2 * side * side * width * 3, bytes_accessed=slots * side * side * 4, transcendentals=0
        ),
        name="forward_product" if forward else "transposed_product",
    )(listing, count, tiles, *pieces)


def sum_kernel(vec, *refs):
    ins, (basis_ref, residual_ref) = refs[:-2], refs[-2:]
    total = ins[0][...]
    for ref in ins[1:]:
        total = total + ref[...]
    basis_ref[...] = total[:vec]
    residual_ref[...] = total[vec:]


def exchange(x, axis, offset):
    n = lax.axis_size(axis)
    return lax.ppermute(x, axis, [(a, a ^ offset) for a in range(n)])


def local(ham_tiles, tile_list, tile_count, basis_block, residual_block):
    side = ham_tiles.shape[-1]
    vec, share = basis_block.shape
    per_piece = share // side
    n_row, n_col = lax.axis_size("row"), lax.axis_size("col")
    tiles = ham_tiles[0, 0]
    listing = tile_list[0, 0].T
    own = jnp.concatenate([basis_block, residual_block], axis=0)
    col_pieces = [own] + [exchange(own, "row", s) for s in range(1, n_row)]
    row_pieces = [own] + [exchange(own, "col", s) for s in range(1, n_col)]
    to_rows = product(True, per_piece, n_row, n_col, listing, tile_count, tiles, col_pieces)
    row_sums = [to_rows[0]] + [exchange(to_rows[s], "col", s) for s in range(1, n_col)]
    to_cols = product(False, per_piece, n_row, n_col, listing, tile_count, tiles, row_pieces)
    col_sums = [to_cols[0]] + [exchange(to_cols[s], "row", s) for s in range(1, n_row)]
    out = jax.ShapeDtypeStruct((vec, share), jnp.float32)
    h_basis, h_residual = pl.pallas_call(
        functools.partial(sum_kernel, vec), out_shape=[out, out], name="sum_pieces"
    )(*row_sums, *col_sums)
    return (h_basis, h_residual)


def solution(mesh):
    placed = (
        P("row", "col", None, None, None),
        P("row", "col", None, None),
        P("row", "col"),
        P(None, ("row", "col")),
        P(None, ("row", "col")),
    )
    return jax.shard_map(
        local,
        mesh=mesh,
        in_specs=placed,
        out_specs=(P(None, ("row", "col")), P(None, ("row", "col"))),
        check_vma=False,
    )
```

```python
import functools

import jax
import jax.numpy as jnp
from jax import lax
from jax.experimental import pallas as pl
from jax.experimental.pallas import tpu as pltpu
from jax.sharding import PartitionSpec as P

CHUNK = 16
SLOTS_HELD = 8
MIB = 1024 * 1024
VMEM = pl.BlockSpec(memory_space=pltpu.VMEM)
SMEM = pl.BlockSpec(memory_space=pltpu.SMEM)
ANY = pl.BlockSpec(memory_space=pl.ANY)


def chunks_of(count_ref):
    return (count_ref[0, 0] + CHUNK - 1) // CHUNK


def stack_kernel(basis_ref, residual_ref, out_ref):
    vec = basis_ref.shape[0]
    out_ref[:vec] = basis_ref[...]
    out_ref[vec:] = residual_ref[...]


def split(x):
    high = x.astype(jnp.bfloat16)
    low = (x - high.astype(jnp.float32)).astype(jnp.bfloat16)
    return high, low


def tiles_kernel(per_piece, n_col, list_ref, count_ref, tiles_ref, out_ref, held, sems):
    side = tiles_ref.shape[-1]
    row_at, col_at = lax.axis_index("row"), lax.axis_index("col")
    chunks = chunks_of(count_ref)

    def chunk_copy(k):
        slot = lax.rem(k, SLOTS_HELD)
        return pltpu.make_async_copy(tiles_ref.at[pl.ds(k * CHUNK, CHUNK)], held.at[slot], sems.at[slot])

    @pl.loop(0, jnp.minimum(chunks, SLOTS_HELD))
    def _(k):
        chunk_copy(k).start()

    @pl.loop(0, chunks)
    def _(k):
        chunk_copy(k).wait()
        slot = lax.rem(k, SLOTS_HELD)
        for u in range(CHUNK):
            t = k * CHUNK + u
            i, j = list_ref[0, t], list_ref[1, t]
            row_block = row_at * (n_col * per_piece) + i
            col_block = j // per_piece * (n_col * per_piece) + col_at * per_piece + j % per_piece
            weight = jnp.where(row_block == col_block, 0.5, 1.0)
            weight = jnp.where(t < count_ref[0, 0], weight, 0.0).astype(jnp.float32)
            high, low = split(held[slot, u] * weight)
            out_ref[t, :side] = high
            out_ref[t, side:] = low

        @pl.when(k + SLOTS_HELD < chunks)
        def _():
            chunk_copy(k + SLOTS_HELD).start()


def product_kernel(forward, last, n_pieces, n_out, list_ref, count_ref, tiles_ref, *refs):
    pieces, refs = refs[:n_pieces], refs[n_pieces:]
    side = tiles_ref.shape[-1]
    width, share = pieces[0].shape
    per_piece = share // side
    if last:
        before, _, *outs, vecs, total = refs
    else:
        _, total, vecs = refs
    in_at = lax.axis_index("row" if forward else "col")
    out_at = lax.axis_index("col" if forward else "row")
    chunks = chunks_of(count_ref)
    half = (chunks + 1) // 2
    begin, end = (half, chunks) if last else (0, half)

    for s in range(n_pieces):
        base = (in_at ^ s) * per_piece
        for b in range(per_piece):
            high, low = split(pieces[s][:, b * side:(b + 1) * side])
            vecs[base + b, :width, :side] = high
            vecs[base + b, :width, side:] = high
            vecs[base + b, width:, :side] = low
            vecs[base + b, width:, side:] = jnp.zeros_like(low)
    total[...] = before[...] if last else jnp.zeros_like(total)

    @pl.loop(begin, end)
    def _(k):
        for u in range(CHUNK):
            t = k * CHUNK + u
            i, j = list_ref[0, t], list_ref[1, t]
            if forward:
                out = lax.dot_general(
                    vecs[j],
                    jnp.concatenate([tiles_ref[t, :side], tiles_ref[t, side:]], axis=1),
                    (((1,), (1,)), ((), ())),
                    preferred_element_type=jnp.float32,
                )
                at = i
            else:
                out = jnp.dot(vecs[i], tiles_ref[t], preferred_element_type=jnp.float32)
                at = j
            total[at] += out[:width] + out[width:]

    if last:
        for s in range(n_out):
            base = (out_at ^ s) * per_piece
            out = outs[s % 2].at[s // 2] if forward else outs[s]
            for b in range(per_piece):
                out[:, b * side:(b + 1) * side] = total[base + b]


def product(forward, last, n_out, listing, count, tiles, pieces, before, after):
    slots, side = tiles.shape[0], tiles.shape[-1]
    width, share = pieces[0].shape
    per_piece = share // side
    n_pieces = len(pieces)
    total = (n_out * per_piece, width, side)
    vecs = pltpu.VMEM((n_pieces * per_piece, 2 * width, 2 * side), jnp.bfloat16)
    scratch = [vecs]
    if not last:
        out_shape = jax.ShapeDtypeStruct(total, jnp.float32)
        out_specs = VMEM
        extra, extra_specs = [after], [ANY]
    else:
        scratch.append(pltpu.VMEM(total, jnp.float32))
        if forward:
            out_shape = [jax.ShapeDtypeStruct((n_out // 2, width, share), jnp.float32)] * 2
        else:
            out_shape = [jax.ShapeDtypeStruct((width, share), jnp.float32)] * n_out
        out_specs = [VMEM] * len(out_shape)
        extra, extra_specs = [before, after], [VMEM, ANY]
    return pl.pallas_call(
        functools.partial(product_kernel, forward, last, n_pieces, n_out),
        out_shape=out_shape,
        in_specs=[SMEM, SMEM, VMEM] + [VMEM] * n_pieces + extra_specs,
        out_specs=out_specs,
        scratch_shapes=scratch,
        compiler_params=pltpu.CompilerParams(vmem_limit_bytes=8 * MIB),
        cost_estimate=pl.CostEstimate(
            flops=slots * 2 * side * side * width * 24, bytes_accessed=slots * side * side * 4, transcendentals=0
        ),
        name=("forward" if forward else "transposed") + ("_last" if last else "_first"),
    )(listing, count, tiles, *pieces, *extra)


def add_kernel(kept_ref, came_ref, *outs):
    for q, out in enumerate(outs):
        out[...] = kept_ref[q] + came_ref[q]


def sum_kernel(vec, *refs):
    ins, (basis_ref, residual_ref) = refs[:-2], refs[-2:]
    total = ins[0][...]
    for ref in ins[1:]:
        total = total + ref[...]
    basis_ref[...] = total[:vec]
    residual_ref[...] = total[vec:]


def exchange(x, axis, offset):
    n = lax.axis_size(axis)
    return lax.ppermute(x, axis, [(a, a ^ offset) for a in range(n)])


def local(ham_tiles, tile_list, tile_count, basis_block, residual_block):
    slots, side = ham_tiles.shape[2], ham_tiles.shape[-1]
    vec, share = basis_block.shape
    width = 2 * vec
    per_piece = share // side
    n_row, n_col = lax.axis_size("row"), lax.axis_size("col")
    listing = tile_list[0, 0].T
    piece = jax.ShapeDtypeStruct((width, share), jnp.float32)

    own = pl.pallas_call(
        stack_kernel, out_shape=piece, in_specs=[VMEM] * 2, out_specs=VMEM, name="stack_share"
    )(basis_block, residual_block)
    col_pieces = [own] + [exchange(own, "row", s) for s in range(1, n_row)]
    even = [own] + [exchange(own, "col", s) for s in range(2, n_col, 2)]

    tiles = pl.pallas_call(
        functools.partial(tiles_kernel, per_piece, n_col),
        out_shape=jax.ShapeDtypeStruct((slots, 2 * side, side), jnp.bfloat16),
        in_specs=[SMEM, SMEM, ANY],
        out_specs=VMEM,
        scratch_shapes=[
            pltpu.VMEM((SLOTS_HELD, CHUNK, side, side), jnp.float32),
            pltpu.SemaphoreType.DMA((SLOTS_HELD,)),
        ],
        compiler_params=pltpu.CompilerParams(vmem_limit_bytes=36 * MIB),
        cost_estimate=pl.CostEstimate(flops=0, bytes_accessed=slots * side * side * 4, transcendentals=0),
        name="split_tiles",
    )(listing, tile_count, ham_tiles[0, 0])

    calls = functools.partial(product, listing=listing, count=tile_count, tiles=tiles)
    begun = calls(True, False, n_col, pieces=col_pieces, before=None, after=own)
    even, begun = lax.optimization_barrier((even, begun))
    row_pieces = []
    for q in range(n_col // 2):
        row_pieces += [even[q], exchange(even[q], "col", 1)]
    kept, leaving = calls(True, True, n_col, pieces=col_pieces, before=begun, after=even[-1])
    came = exchange(leaving, "col", 1)
    begun = calls(False, False, n_row, pieces=row_pieces, before=None, after=kept)
    line = pl.pallas_call(
        add_kernel, out_shape=[piece] * (n_col // 2), in_specs=[VMEM] * 2, out_specs=[VMEM] * (n_col // 2),
        name="add_cores",
    )(kept, came)
    row_sums = [line[0]] + [exchange(line[q], "col", 2 * q) for q in range(1, n_col // 2)]
    to_cols = calls(False, True, n_row, pieces=row_pieces, before=begun, after=line[0])
    col_sums = [to_cols[0]] + [exchange(to_cols[s], "row", s) for s in range(1, n_row)]
    out = jax.ShapeDtypeStruct((vec, share), jnp.float32)
    h_basis, h_residual = pl.pallas_call(
        functools.partial(sum_kernel, vec),
        out_shape=[out, out],
        in_specs=[VMEM] * (n_col // 2 + n_row),
        name="sum_pieces",
    )(*row_sums, *col_sums)
    return (h_basis, h_residual)


def solution(mesh):
    placed = (
        P("row", "col", None, None, None),
        P("row", "col", None, None),
        P("row", "col"),
        P(None, ("row", "col")),
        P(None, ("row", "col")),
    )
    return jax.shard_map(
        local,
        mesh=mesh,
        in_specs=placed,
        out_specs=(P(None, ("row", "col")), P(None, ("row", "col"))),
        check_vma=False,
    )
```

```python
import functools

import jax
import jax.numpy as jnp
from jax import lax
from jax.experimental import pallas as pl
from jax.experimental.pallas import tpu as pltpu
from jax.sharding import PartitionSpec as P

CHUNK = 16
SLOTS_HELD = 8
MIB = 1024 * 1024
VMEM = pl.BlockSpec(memory_space=pltpu.VMEM)
SMEM = pl.BlockSpec(memory_space=pltpu.SMEM)
ANY = pl.BlockSpec(memory_space=pl.ANY)


def chunks_of(count_ref):
    return (count_ref[0, 0] + CHUNK - 1) // CHUNK


def stack_kernel(basis_ref, residual_ref, out_ref):
    vec = basis_ref.shape[0]
    out_ref[:vec] = basis_ref[...]
    out_ref[vec:] = residual_ref[...]


def split(x):
    high = x.astype(jnp.bfloat16)
    low = (x - high.astype(jnp.float32)).astype(jnp.bfloat16)
    return high, low


def tiles_kernel(per_piece, n_col, list_ref, count_ref, tiles_ref, out_ref, held, sems):
    side = tiles_ref.shape[-1]
    row_at, col_at = lax.axis_index("row"), lax.axis_index("col")
    chunks = chunks_of(count_ref)

    def chunk_copy(k):
        slot = lax.rem(k, SLOTS_HELD)
        return pltpu.make_async_copy(tiles_ref.at[pl.ds(k * CHUNK, CHUNK)], held.at[slot], sems.at[slot])

    @pl.loop(0, jnp.minimum(chunks, SLOTS_HELD))
    def _(k):
        chunk_copy(k).start()

    @pl.loop(0, chunks)
    def _(k):
        chunk_copy(k).wait()
        slot = lax.rem(k, SLOTS_HELD)
        for u in range(CHUNK):
            t = k * CHUNK + u
            i, j = list_ref[0, t], list_ref[1, t]
            row_block = row_at * (n_col * per_piece) + i
            col_block = j // per_piece * (n_col * per_piece) + col_at * per_piece + j % per_piece
            weight = jnp.where(row_block == col_block, 0.5, 1.0)
            weight = jnp.where(t < count_ref[0, 0], weight, 0.0).astype(jnp.float32)
            high, low = split(held[slot, u] * weight)
            out_ref[t, :side] = high
            out_ref[t, side:] = low

        @pl.when(k + SLOTS_HELD < chunks)
        def _():
            chunk_copy(k + SLOTS_HELD).start()


def product_kernel(forward, last, n_pieces, n_out, list_ref, count_ref, tiles_ref, *refs):
    pieces, refs = refs[:n_pieces], refs[n_pieces:]
    side = tiles_ref.shape[-1]
    width, share = pieces[0].shape
    per_piece = share // side
    if last:
        before, _, *outs, vecs, total = refs
    else:
        _, total, vecs = refs
    in_at = lax.axis_index("row" if forward else "col")
    out_at = lax.axis_index("col" if forward else "row")
    chunks = chunks_of(count_ref)
    half = (chunks + 1) // 2
    begin, end = (half, chunks) if last else (0, half)

    for s in range(n_pieces):
        base = (in_at ^ s) * per_piece
        for b in range(per_piece):
            high, low = split(pieces[s][:, b * side:(b + 1) * side])
            vecs[base + b, :width, :side] = high
            vecs[base + b, :width, side:] = high
            vecs[base + b, width:, :side] = low
            vecs[base + b, width:, side:] = jnp.zeros_like(low)
    total[...] = before[...] if last else jnp.zeros_like(total)

    @pl.loop(begin, end)
    def _(k):
        for u in range(0, CHUNK, 2):
            t = k * CHUNK + u
            blocks = [(list_ref[0, t + h], list_ref[1, t + h]) for h in range(2)]
            if forward:
                ats, froms = [i for i, _ in blocks], [j for _, j in blocks]
            else:
                ats, froms = [j for _, j in blocks], [i for i, _ in blocks]
            rows = jnp.concatenate([vecs[froms[0]], vecs[froms[1]]], axis=0)
            if forward:
                pair = [
                    jnp.concatenate([tiles_ref[t + h, :side], tiles_ref[t + h, side:]], axis=1) for h in range(2)
                ]
                out = lax.dot_general(
                    rows,
                    jnp.concatenate(pair, axis=0),
                    (((1,), (1,)), ((), ())),
                    preferred_element_type=jnp.float32,
                )
            else:
                out = jnp.dot(
                    rows,
                    jnp.concatenate([tiles_ref[t], tiles_ref[t + 1]], axis=1),
                    preferred_element_type=jnp.float32,
                )
            for h in range(2):
                mine = out[2 * width * h:2 * width * (h + 1), side * h:side * (h + 1)]
                total[ats[h]] += mine[:width] + mine[width:]

    if last:
        for s in range(n_out):
            base = (out_at ^ s) * per_piece
            out = outs[s % 2].at[s // 2] if forward else outs[s]
            for b in range(per_piece):
                out[:, b * side:(b + 1) * side] = total[base + b]


def product(forward, last, n_out, listing, count, tiles, pieces, before, after):
    slots, side = tiles.shape[0], tiles.shape[-1]
    width, share = pieces[0].shape
    per_piece = share // side
    n_pieces = len(pieces)
    total = (n_out * per_piece, width, side)
    vecs = pltpu.VMEM((n_pieces * per_piece, 2 * width, 2 * side), jnp.bfloat16)
    scratch = [vecs]
    if not last:
        out_shape = jax.ShapeDtypeStruct(total, jnp.float32)
        out_specs = VMEM
        extra, extra_specs = [after], [ANY]
    else:
        scratch.append(pltpu.VMEM(total, jnp.float32))
        if forward:
            out_shape = [jax.ShapeDtypeStruct((n_out // 2, width, share), jnp.float32)] * 2
        else:
            out_shape = [jax.ShapeDtypeStruct((width, share), jnp.float32)] * n_out
        out_specs = [VMEM] * len(out_shape)
        extra, extra_specs = [before, after], [VMEM, ANY]
    return pl.pallas_call(
        functools.partial(product_kernel, forward, last, n_pieces, n_out),
        out_shape=out_shape,
        in_specs=[SMEM, SMEM, VMEM] + [VMEM] * n_pieces + extra_specs,
        out_specs=out_specs,
        scratch_shapes=scratch,
        compiler_params=pltpu.CompilerParams(vmem_limit_bytes=8 * MIB),
        cost_estimate=pl.CostEstimate(
            flops=slots * 2 * side * side * width * 24, bytes_accessed=slots * side * side * 4, transcendentals=0
        ),
        name=("forward" if forward else "transposed") + ("_last" if last else "_first"),
    )(listing, count, tiles, *pieces, *extra)


def add_kernel(kept_ref, came_ref, *outs):
    for q, out in enumerate(outs):
        out[...] = kept_ref[q] + came_ref[q]


def sum_kernel(vec, *refs):
    ins, (basis_ref, residual_ref) = refs[:-2], refs[-2:]
    total = ins[0][...]
    for ref in ins[1:]:
        total = total + ref[...]
    basis_ref[...] = total[:vec]
    residual_ref[...] = total[vec:]


def exchange(x, axis, offset, keep=lambda source, target: True):
    n = lax.axis_size(axis)
    return lax.ppermute(x, axis, [(a, a ^ offset) for a in range(n) if keep(a, a ^ offset)])


def upward(source, target):
    return source > target


def downward(source, target):
    return source < target


def local(ham_tiles, tile_list, tile_count, basis_block, residual_block):
    slots, side = ham_tiles.shape[2], ham_tiles.shape[-1]
    vec, share = basis_block.shape
    width = 2 * vec
    per_piece = share // side
    n_row, n_col = lax.axis_size("row"), lax.axis_size("col")
    listing = tile_list[0, 0].T
    piece = jax.ShapeDtypeStruct((width, share), jnp.float32)

    own = pl.pallas_call(
        stack_kernel, out_shape=piece, in_specs=[VMEM] * 2, out_specs=VMEM, name="stack_share"
    )(basis_block, residual_block)
    col_pieces = [own] + [exchange(own, "row", s, upward) for s in range(1, n_row)]
    even = [own] + [exchange(own, "col", s) for s in range(2, n_col, 2)]

    tiles = pl.pallas_call(
        functools.partial(tiles_kernel, per_piece, n_col),
        out_shape=jax.ShapeDtypeStruct((slots, 2 * side, side), jnp.bfloat16),
        in_specs=[SMEM, SMEM, ANY],
        out_specs=VMEM,
        scratch_shapes=[
            pltpu.VMEM((SLOTS_HELD, CHUNK, side, side), jnp.float32),
            pltpu.SemaphoreType.DMA((SLOTS_HELD,)),
        ],
        compiler_params=pltpu.CompilerParams(vmem_limit_bytes=24 * MIB),
        cost_estimate=pl.CostEstimate(flops=0, bytes_accessed=slots * side * side * 4, transcendentals=0),
        name="split_tiles",
    )(listing, tile_count, ham_tiles[0, 0])

    calls = functools.partial(product, listing=listing, count=tile_count, tiles=tiles)
    begun = calls(True, False, n_col, pieces=col_pieces, before=None, after=own)
    even, begun = lax.optimization_barrier((even, begun))
    row_pieces = []
    for q in range(n_col // 2):
        row_pieces += [even[q], exchange(even[q], "col", 1)]
    kept, leaving = calls(True, True, n_col, pieces=col_pieces, before=begun, after=even[-1])
    came = exchange(leaving, "col", 1)
    begun = calls(False, False, n_row, pieces=row_pieces, before=None, after=kept)
    line = pl.pallas_call(
        add_kernel, out_shape=[piece] * (n_col // 2), in_specs=[VMEM] * 2, out_specs=[VMEM] * (n_col // 2),
        name="add_cores",
    )(kept, came)
    row_sums = [line[0]] + [exchange(line[q], "col", 2 * q) for q in range(1, n_col // 2)]
    to_cols = calls(False, True, n_row, pieces=row_pieces, before=begun, after=line[0])
    col_sums = [to_cols[0]] + [exchange(to_cols[s], "row", s, downward) for s in range(1, n_row)]
    out = jax.ShapeDtypeStruct((vec, share), jnp.float32)
    h_basis, h_residual = pl.pallas_call(
        functools.partial(sum_kernel, vec),
        out_shape=[out, out],
        in_specs=[VMEM] * (n_col // 2 + n_row),
        name="sum_pieces",
    )(*row_sums, *col_sums)
    return (h_basis, h_residual)


def solution(mesh):
    placed = (
        P("row", "col", None, None, None),
        P("row", "col", None, None),
        P("row", "col"),
        P(None, ("row", "col")),
        P(None, ("row", "col")),
    )
    return jax.shard_map(
        local,
        mesh=mesh,
        in_specs=placed,
        out_specs=(P(None, ("row", "col")), P(None, ("row", "col"))),
        check_vma=False,
    )
```

```python
import functools

import jax
import jax.numpy as jnp
from jax import lax
from jax.experimental import pallas as pl
from jax.experimental.pallas import tpu as pltpu
from jax.sharding import PartitionSpec as P

CHUNK = 16
GROUP = 32
MIB = 1024 * 1024
VMEM = pl.BlockSpec(memory_space=pltpu.VMEM)
SMEM = pl.BlockSpec(memory_space=pltpu.SMEM)
ANY = pl.BlockSpec(memory_space=pl.ANY)
SMALL = pltpu.CompilerParams(vmem_limit_bytes=2 * MIB)


def groups_of(count_ref):
    return (count_ref[0, 0] + GROUP - 1) // GROUP


def stack_kernel(basis_ref, residual_ref, out_ref):
    vec = basis_ref.shape[0]
    out_ref[:vec] = basis_ref[...]
    out_ref[vec:] = residual_ref[...]


def split(x):
    high = x.astype(jnp.bfloat16)
    low = (x - high.astype(jnp.float32)).astype(jnp.bfloat16)
    return high, low


def product_kernel(forward, last, n_pieces, n_out, n_col, list_ref, count_ref, tiles_ref, *refs):
    pieces, refs = refs[:n_pieces], refs[n_pieces:]
    side = tiles_ref.shape[-1]
    width, share = pieces[0].shape
    per_piece = share // side
    loads = forward and not last
    if last:
        before, _, *outs, vecs, total = refs
        held = tiles_ref
    elif loads:
        _, total, held, vecs, sems = refs
    else:
        _, total, vecs = refs
        held = tiles_ref
    row_at, col_at = lax.axis_index("row"), lax.axis_index("col")
    in_at, out_at = (row_at, col_at) if forward else (col_at, row_at)
    groups = groups_of(count_ref)
    half = (groups + 1) // 2
    begin, end = (half, groups) if last else (0, half)
    per_group = GROUP // CHUNK

    def chunk_copy(k):
        part = pl.ds(k * CHUNK, CHUNK)
        return pltpu.make_async_copy(tiles_ref.at[part], held.at[part], sems.at[k])

    if loads:
        @pl.loop(0, groups * per_group)
        def _(k):
            chunk_copy(k).start()

    for s in range(n_pieces):
        base = (in_at ^ s) * per_piece
        for b in range(per_piece):
            high, low = split(pieces[s][:, b * side:(b + 1) * side])
            vecs[base + b, :width, :side] = high
            vecs[base + b, :width, side:] = high
            vecs[base + b, width:, :side] = low
            vecs[base + b, width:, side:] = jnp.zeros_like(low)
    total[...] = before[...] if last else jnp.zeros_like(total)

    @pl.loop(begin, end)
    def _(g):
        if loads:
            for c in range(per_group):
                chunk_copy(g * per_group + c).wait()
        for u in range(GROUP):
            t = g * GROUP + u
            i, j = list_ref[0, t], list_ref[1, t]
            row_block = row_at * (n_col * per_piece) + i
            col_block = j // per_piece * (n_col * per_piece) + col_at * per_piece + j % per_piece
            weight = jnp.where(row_block == col_block, 0.5, 1.0)
            weight = jnp.where(t < count_ref[0, 0], weight, 0.0).astype(jnp.float32)
            high, low = split(held[t])
            if forward:
                out = lax.dot_general(
                    vecs[j],
                    jnp.concatenate([high, low], axis=1),
                    (((1,), (1,)), ((), ())),
                    preferred_element_type=jnp.float32,
                )
                at = i
            else:
                out = jnp.dot(
                    vecs[i], jnp.concatenate([high, low], axis=0), preferred_element_type=jnp.float32
                )
                at = j
            total[at] += (out[:width] + out[width:]) * weight

    if loads:
        @pl.loop(end * per_group, groups * per_group)
        def _(k):
            chunk_copy(k).wait()

    if last:
        for s in range(n_out):
            base = (out_at ^ s) * per_piece
            out = outs[s % 2].at[s // 2] if forward else outs[s]
            for b in range(per_piece):
                out[:, b * side:(b + 1) * side] = total[base + b]


def product(forward, last, n_out, n_col, listing, count, tiles, pieces, before, after):
    slots, side = tiles.shape[0], tiles.shape[-1]
    width, share = pieces[0].shape
    per_piece = share // side
    n_pieces = len(pieces)
    loads = forward and not last
    piece = jax.ShapeDtypeStruct((width, share), jnp.float32)
    total = jax.ShapeDtypeStruct((n_out * per_piece, width, side), jnp.float32)
    scratch = [pltpu.VMEM((n_pieces * per_piece, 2 * width, 2 * side), jnp.bfloat16)]
    extra, extra_specs = ([before, after], [VMEM, ANY]) if last else ([after], [ANY])
    if loads:
        out_shape = [total, jax.ShapeDtypeStruct(tiles.shape, tiles.dtype)]
        scratch.append(pltpu.SemaphoreType.DMA((slots // CHUNK,)))
    elif not last:
        out_shape = [total]
    else:
        scratch.append(pltpu.VMEM(total.shape, total.dtype))
        if forward:
            out_shape = [jax.ShapeDtypeStruct((n_out // 2, width, share), jnp.float32)] * 2
        else:
            out_shape = [piece] * n_out
    return pl.pallas_call(
        functools.partial(product_kernel, forward, last, n_pieces, n_out, n_col),
        out_shape=out_shape,
        in_specs=[SMEM, SMEM, ANY if loads else VMEM] + [VMEM] * n_pieces + extra_specs,
        out_specs=[VMEM] * len(out_shape),
        scratch_shapes=scratch,
        compiler_params=pltpu.CompilerParams(vmem_limit_bytes=(16 if loads else 8) * MIB),
        cost_estimate=pl.CostEstimate(
            flops=slots * 2 * side * side * width * 24, bytes_accessed=slots * side * side * 4, transcendentals=0
        ),
        name=("forward" if forward else "transposed") + ("_last" if last else "_first"),
    )(listing, count, tiles, *pieces, *extra)


def add_kernel(kept_ref, came_ref, *outs):
    for q, out in enumerate(outs):
        out[...] = kept_ref[q] + came_ref[q]


def sum_kernel(vec, *refs):
    ins, (basis_ref, residual_ref) = refs[:-2], refs[-2:]
    total = ins[0][...]
    for ref in ins[1:]:
        total = total + ref[...]
    basis_ref[...] = total[:vec]
    residual_ref[...] = total[vec:]


def exchange(x, axis, offset):
    n = lax.axis_size(axis)
    return lax.ppermute(x, axis, [(a, a ^ offset) for a in range(n)])


def local(ham_tiles, tile_list, tile_count, basis_block, residual_block):
    vec, share = basis_block.shape
    width = 2 * vec
    n_row, n_col = lax.axis_size("row"), lax.axis_size("col")
    listing = tile_list[0, 0].T
    piece = jax.ShapeDtypeStruct((width, share), jnp.float32)

    own = pl.pallas_call(
        stack_kernel,
        out_shape=piece,
        in_specs=[VMEM] * 2,
        out_specs=VMEM,
        compiler_params=SMALL,
        name="stack_share",
    )(basis_block, residual_block)
    col_pieces = [own] + [exchange(own, "row", s) for s in range(1, n_row)]
    even = [own] + [exchange(own, "col", s) for s in range(2, n_col, 2)]

    calls = functools.partial(product, n_col=n_col, listing=listing, count=tile_count)
    begun, tiles = calls(True, False, n_col, tiles=ham_tiles[0, 0], pieces=col_pieces, before=None, after=own)
    even, begun = lax.optimization_barrier((even, begun))
    row_pieces = []
    for q in range(n_col // 2):
        row_pieces += [even[q], exchange(even[q], "col", 1)]
    kept, leaving = calls(
        True, True, n_col, tiles=tiles, pieces=col_pieces, before=begun, after=even[-1]
    )
    came = exchange(leaving, "col", 1)
    (begun,) = calls(False, False, n_row, tiles=tiles, pieces=row_pieces, before=None, after=kept)
    line = pl.pallas_call(
        add_kernel,
        out_shape=[piece] * (n_col // 2),
        in_specs=[VMEM] * 2,
        out_specs=[VMEM] * (n_col // 2),
        compiler_params=SMALL,
        name="add_cores",
    )(kept, came)
    row_sums = [line[0]] + [exchange(line[q], "col", 2 * q) for q in range(1, n_col // 2)]
    to_cols = calls(False, True, n_row, tiles=tiles, pieces=row_pieces, before=begun, after=line[0])
    col_sums = [to_cols[0]] + [exchange(to_cols[s], "row", s) for s in range(1, n_row)]
    out = jax.ShapeDtypeStruct((vec, share), jnp.float32)
    h_basis, h_residual = pl.pallas_call(
        functools.partial(sum_kernel, vec),
        out_shape=[out, out],
        in_specs=[VMEM] * (n_col // 2 + n_row),
        compiler_params=SMALL,
        name="sum_pieces",
    )(*row_sums, *col_sums)
    return (h_basis, h_residual)


def solution(mesh):
    placed = (
        P("row", "col", None, None, None),
        P("row", "col", None, None),
        P("row", "col"),
        P(None, ("row", "col")),
        P(None, ("row", "col")),
    )
    return jax.shard_map(
        local,
        mesh=mesh,
        in_specs=placed,
        out_specs=(P(None, ("row", "col")), P(None, ("row", "col"))),
        check_vma=False,
    )
```

```python
import functools

import jax
import jax.numpy as jnp
from jax import lax
from jax.experimental import pallas as pl
from jax.experimental.pallas import tpu as pltpu
from jax.sharding import PartitionSpec as P

CHUNK = 16
GROUP = 32
MIB = 1024 * 1024
VMEM = pl.BlockSpec(memory_space=pltpu.VMEM)
SMEM = pl.BlockSpec(memory_space=pltpu.SMEM)
ANY = pl.BlockSpec(memory_space=pl.ANY)


def small(kernel, out_shape, name, *args, in_specs=None):
    single = not isinstance(out_shape, list)
    return pl.pallas_call(
        kernel,
        out_shape=out_shape,
        in_specs=in_specs or [VMEM] * len(args),
        out_specs=VMEM if single else [VMEM] * len(out_shape),
        compiler_params=pltpu.CompilerParams(vmem_limit_bytes=2 * MIB),
        name=name,
    )(*args)


def f32(*shape):
    return jax.ShapeDtypeStruct(shape, jnp.float32)


def stack_kernel(basis_ref, residual_ref, out_ref):
    vec = basis_ref.shape[0]
    out_ref[0, :vec] = basis_ref[...]
    out_ref[0, vec:] = residual_ref[...]


def interleave_kernel(own_ref, came_ref, out_ref):
    for q in range(own_ref.shape[0]):
        out_ref[2 * q] = own_ref[q]
        out_ref[2 * q + 1] = came_ref[q]


def split(x):
    high = x.astype(jnp.bfloat16)
    low = (x - high.astype(jnp.float32)).astype(jnp.bfloat16)
    return high, low


def prepare_kernel(axis, *refs):
    *ins, out_ref = refs
    pieces = [ref.at[q] for ref in ins for q in range(ref.shape[0])]
    side = out_ref.shape[-1]
    width, share = pieces[0].shape
    for s, piece in enumerate(pieces):
        base = (lax.axis_index(axis) ^ s) * (share // side)
        for b in range(share // side):
            high, low = split(piece[:, b * side:(b + 1) * side])
            out_ref[base + b, :width] = high
            out_ref[base + b, width:] = low


def chunk_copies(start, slots, count_ref, tiles_ref, held_ref, sems):
    live = jnp.clip(count_ref[0, 0] - start, 0, slots)
    chunks = (live + GROUP - 1) // GROUP * (GROUP // CHUNK)

    def chunk_copy(k):
        return pltpu.make_async_copy(
            tiles_ref.at[pl.ds(start + k * CHUNK, CHUNK)], held_ref.at[pl.ds(k * CHUNK, CHUNK)], sems.at[k]
        )

    return chunks, chunk_copy


def start_all(chunks, chunk_copy):
    @pl.loop(0, chunks)
    def _(k):
        chunk_copy(k).start()


def wait_all(chunks, chunk_copy):
    @pl.loop(0, chunks)
    def _(k):
        chunk_copy(k).wait()


def load_kernel(count_ref, tiles_ref, held_ref, sems):
    chunks, chunk_copy = chunk_copies(0, held_ref.shape[0], count_ref, tiles_ref, held_ref, sems)
    start_all(chunks, chunk_copy)
    wait_all(chunks, chunk_copy)


def add_products(forward, n_col, per_piece, start, begin, end, list_ref, count_ref, held_ref, vecs_ref, total_ref):
    side = held_ref.shape[-1]
    width = total_ref.shape[1]
    row_at, col_at = lax.axis_index("row"), lax.axis_index("col")
    live = jnp.clip(count_ref[0, 0] - start, 0, end)

    @pl.loop(begin // GROUP, (live + GROUP - 1) // GROUP)
    def _(g):
        for u in range(GROUP):
            h = g * GROUP + u
            t = start + h
            i, j = list_ref[0, t], list_ref[1, t]
            row_block = row_at * (n_col * per_piece) + i
            col_block = j // per_piece * (n_col * per_piece) + col_at * per_piece + j % per_piece
            weight = jnp.where(row_block == col_block, 0.5, 1.0)
            weight = jnp.where(t < count_ref[0, 0], weight, 0.0).astype(jnp.float32)
            high, low = split(held_ref[h])
            if forward:
                out = lax.dot_general(
                    vecs_ref[j],
                    jnp.concatenate([high, low], axis=0),
                    (((1,), (1,)), ((), ())),
                    preferred_element_type=jnp.float32,
                )
                at = i
            else:
                out = jnp.dot(
                    vecs_ref[i], jnp.concatenate([high, low], axis=1), preferred_element_type=jnp.float32
                )
                at = j
            total_ref[at] += (out[:width, :side] + out[width:, :side] + out[:width, side:]) * weight


def first_kernel(forward, n_col, per_piece, list_ref, count_ref, *refs):
    if forward:
        tiles_ref, held_ref, vecs_ref, _, total_ref, next_ref, sems = refs
        chunks, chunk_copy = chunk_copies(held_ref.shape[0], next_ref.shape[0], count_ref, tiles_ref, next_ref, sems)
        start_all(chunks, chunk_copy)
    else:
        held_ref, vecs_ref, _, total_ref = refs
    total_ref[...] = jnp.zeros_like(total_ref)
    add_products(
        forward, n_col, per_piece, 0, 0, held_ref.shape[0], list_ref, count_ref, held_ref, vecs_ref, total_ref
    )
    if forward:
        wait_all(chunks, chunk_copy)


def later_kernel(forward, n_col, per_piece, start, begin, end, list_ref, count_ref, held_ref, vecs_ref, _, total_ref):
    add_products(
        forward, n_col, per_piece, start, begin, end, list_ref, count_ref, held_ref, vecs_ref, total_ref
    )


def route_rows_kernel(total_ref, kept_ref, leaving_ref):
    n = 2 * kept_ref.shape[0]
    per_piece = total_ref.shape[0] // n
    side = total_ref.shape[-1]
    for s in range(n):
        base = (lax.axis_index("col") ^ s) * per_piece
        out = (leaving_ref if s % 2 else kept_ref).at[s // 2]
        for b in range(per_piece):
            out[:, b * side:(b + 1) * side] = total_ref[base + b]


def route_cols_kernel(total_ref, out_ref):
    n = out_ref.shape[0]
    per_piece = total_ref.shape[0] // n
    side = total_ref.shape[-1]
    for r in range(n):
        for b in range(per_piece):
            out_ref[r, :, b * side:(b + 1) * side] = total_ref[r * per_piece + b]


def halve_kernel(kept_ref, came_ref, even_ref, odd_ref):
    for q in range(even_ref.shape[0]):
        even_ref[q] = kept_ref[2 * q] + came_ref[2 * q]
        odd_ref[q] = kept_ref[2 * q + 1] + came_ref[2 * q + 1]


def sum_kernel(kept_ref, came_ref, cols_ref, basis_ref, residual_ref):
    vec = basis_ref.shape[0]
    total = kept_ref[0] + came_ref[0]
    for r in range(cols_ref.shape[0]):
        total = total + cols_ref[r]
    basis_ref[...] = total[:vec]
    residual_ref[...] = total[vec:]


def exchange(x, axis, offset):
    n = lax.axis_size(axis)
    return lax.ppermute(x, axis, [(a, a ^ offset) for a in range(n)])


def local(ham_tiles, tile_list, tile_count, basis_block, residual_block):
    slots, side = ham_tiles.shape[2], ham_tiles.shape[-1]
    vec, share = basis_block.shape
    width = 2 * vec
    per_piece = share // side
    n_row, n_col = lax.axis_size("row"), lax.axis_size("col")
    tiles = ham_tiles[0, 0]
    listing = tile_list[0, 0].T
    half = slots // 2 // GROUP * GROUP
    rest = slots - half
    cut = (rest // GROUP + 1) // 2 * GROUP
    bits = [1 << k for k in range(n_col.bit_length() - 1)]
    cost = pl.CostEstimate(
        flops=slots * 2 * side * side * width * 24, bytes_accessed=half * side * side * 4, transcendentals=0
    )
    params = pltpu.CompilerParams(vmem_limit_bytes=16 * MIB)

    def first(forward, held, vecs, after):
        blocks = (n_col if forward else n_row) * per_piece
        totals = f32(blocks, width, side)
        loads = [tiles] if forward else []
        return pl.pallas_call(
            functools.partial(first_kernel, forward, n_col, per_piece),
            out_shape=[totals] + ([f32(rest, side, side)] if forward else []),
            in_specs=[SMEM, SMEM] + [ANY] * len(loads) + [VMEM, VMEM, ANY],
            out_specs=[VMEM] * (1 + len(loads)),
            scratch_shapes=[pltpu.SemaphoreType.DMA((rest // CHUNK,))] * len(loads),
            compiler_params=params,
            cost_estimate=cost,
            name="forward_first" if forward else "transposed_first",
        )(listing, tile_count, *loads, held, vecs, after)

    def later(forward, begin, end, held, vecs, total, name):
        return pl.pallas_call(
            functools.partial(later_kernel, forward, n_col, per_piece, half, begin, end),
            out_shape=f32(*total.shape),
            in_specs=[SMEM, SMEM, VMEM, VMEM, VMEM],
            out_specs=VMEM,
            input_output_aliases={4: 0},
            compiler_params=params,
            cost_estimate=cost,
            name=name,
        )(listing, tile_count, held, vecs, total)

    def doubled(x, bit):
        came = exchange(x, "col", bit)
        return small(interleave_kernel, f32(2 * x.shape[0], width, share), "interleave", x, came)

    own = small(stack_kernel, f32(1, width, share), "stack_share", basis_block, residual_block)
    col_pieces = [own] + [exchange(own, "row", s) for s in range(1, n_row)]
    panel = doubled(own, bits[-1])
    held = pl.pallas_call(
        load_kernel,
        out_shape=f32(half, side, side),
        in_specs=[SMEM, ANY],
        out_specs=VMEM,
        scratch_shapes=[pltpu.SemaphoreType.DMA((half // CHUNK,))],
        compiler_params=pltpu.CompilerParams(vmem_limit_bytes=28 * MIB),
        cost_estimate=pl.CostEstimate(flops=0, bytes_accessed=half * side * side * 4, transcendentals=0),
        name="load_half",
    )(tile_count, tiles)
    vecs = small(
        functools.partial(prepare_kernel, "row"),
        jax.ShapeDtypeStruct((n_row * per_piece, 2 * width, side), jnp.bfloat16),
        "prepare_columns",
        *col_pieces,
    )
    total, held_rest = first(True, held, vecs, own)
    panel, total = lax.optimization_barrier((panel, total))
    for bit in bits[-2:-1]:
        panel = doubled(panel, bit)
    total = later(True, 0, cut, held_rest, vecs, total, "forward_middle")
    panel, total = lax.optimization_barrier((panel, total))
    for bit in reversed(bits[:-2]):
        panel = doubled(panel, bit)
    total = later(True, cut, rest, held_rest, vecs, total, "forward_last")
    kept, leaving = small(route_rows_kernel, [f32(n_col // 2, width, share)] * 2, "route_rows", total)
    came = exchange(leaving, "col", 1)

    vecs = small(
        functools.partial(prepare_kernel, "col"),
        jax.ShapeDtypeStruct((n_col * per_piece, 2 * width, side), jnp.bfloat16),
        "prepare_rows",
        panel,
    )
    (total,) = first(False, held, vecs, kept)
    for bit in bits[1:]:
        came, total = lax.optimization_barrier((came, total))
        m = kept.shape[0] // 2
        kept, leaving = small(halve_kernel, [f32(m, width, share)] * 2, "halve", kept, came)
        leaving, total = lax.optimization_barrier((leaving, total))
        came = exchange(leaving, "col", bit)
        if bit == 2:
            total = later(False, 0, cut, held_rest, vecs, total, "transposed_middle")
    total = later(False, cut, rest, held_rest, vecs, total, "transposed_last")
    cols = small(route_cols_kernel, f32(n_row, width, share), "route_columns", total)
    cols = lax.all_to_all(cols, "row", 0, 0, tiled=True)
    h_basis, h_residual = small(sum_kernel, [f32(vec, share)] * 2, "sum_pieces", kept, came, cols)
    return (h_basis, h_residual)


def solution(mesh):
    placed = (
        P("row", "col", None, None, None),
        P("row", "col", None, None),
        P("row", "col"),
        P(None, ("row", "col")),
        P(None, ("row", "col")),
    )
    return jax.shard_map(
        local,
        mesh=mesh,
        in_specs=placed,
        out_specs=(P(None, ("row", "col")), P(None, ("row", "col"))),
        check_vma=False,
    )
```

```python
import functools

import jax
import jax.numpy as jnp
from jax import lax
from jax.experimental import pallas as pl
from jax.experimental.pallas import tpu as pltpu
from jax.sharding import PartitionSpec as P

CHUNK = 16
GROUP = 32
MIB = 1024 * 1024
VMEM = pl.BlockSpec(memory_space=pltpu.VMEM)
SMEM = pl.BlockSpec(memory_space=pltpu.SMEM)
ANY = pl.BlockSpec(memory_space=pl.ANY)


def small(kernel, out_shape, name, *args, in_specs=None):
    single = not isinstance(out_shape, list)
    return pl.pallas_call(
        kernel,
        out_shape=out_shape,
        in_specs=in_specs or [VMEM] * len(args),
        out_specs=VMEM if single else [VMEM] * len(out_shape),
        compiler_params=pltpu.CompilerParams(vmem_limit_bytes=2 * MIB),
        name=name,
    )(*args)


def f32(*shape):
    return jax.ShapeDtypeStruct(shape, jnp.float32)


def stack_kernel(basis_ref, residual_ref, out_ref, sems):
    vec = basis_ref.shape[0]
    copies = [
        pltpu.make_async_copy(basis_ref, out_ref.at[0, :vec], sems.at[0]),
        pltpu.make_async_copy(residual_ref, out_ref.at[0, vec:], sems.at[1]),
    ]
    for copy in copies:
        copy.start()
    for copy in copies:
        copy.wait()


def interleave_kernel(own_ref, came_ref, out_ref):
    for q in range(own_ref.shape[0]):
        out_ref[2 * q] = own_ref[q]
        out_ref[2 * q + 1] = came_ref[q]


def split(x):
    high = x.astype(jnp.bfloat16)
    low = (x - high.astype(jnp.float32)).astype(jnp.bfloat16)
    return high, low


def prepare(forward, at, pieces, vecs_ref):
    blocks = vecs_ref.shape[0] // 2
    side = vecs_ref.shape[-1]
    width, share = pieces[0].shape
    per_piece = share // side
    for s, piece in enumerate(pieces):
        base = (at ^ s) * per_piece
        for b in range(per_piece):
            x = piece[:, b * side:(b + 1) * side]
            high = x.astype(jnp.bfloat16).astype(jnp.float32)
            rows = [high, x - high]
            if forward:
                rows = jnp.concatenate(rows + [jnp.zeros((side - 2 * width, side), jnp.float32)], axis=0).T
                rows = jnp.concatenate([rows, rows], axis=0)
            else:
                rows = jnp.concatenate(rows, axis=0)
            vecs_ref[base + b] = rows.astype(jnp.bfloat16)
            vecs_ref[blocks + base + b] = (rows * 0.5).astype(jnp.bfloat16)
    vecs_ref[2 * blocks] = jnp.zeros_like(vecs_ref[2 * blocks])


def chunk_copies(start, slots, count_ref, tiles_ref, held_ref, sems):
    live = jnp.clip(count_ref[0, 0] - start, 0, slots)
    chunks = (live + GROUP - 1) // GROUP * (GROUP // CHUNK)

    def chunk_copy(k):
        return pltpu.make_async_copy(
            tiles_ref.at[pl.ds(start + k * CHUNK, CHUNK)], held_ref.at[pl.ds(k * CHUNK, CHUNK)], sems.at[k]
        )

    return chunks, chunk_copy


def start_all(chunks, chunk_copy):
    @pl.loop(0, chunks)
    def _(k):
        chunk_copy(k).start()


def wait_all(chunks, chunk_copy):
    @pl.loop(0, chunks)
    def _(k):
        chunk_copy(k).wait()


def load_kernel(count_ref, tiles_ref, held_ref, sems):
    chunks, chunk_copy = chunk_copies(0, held_ref.shape[0], count_ref, tiles_ref, held_ref, sems)
    start_all(chunks, chunk_copy)
    wait_all(chunks, chunk_copy)


def add_products(forward, per_piece, start, begin, end, list_ref, count_ref, held_ref, vecs_ref, total_ref, arrive=None):
    blocks = vecs_ref.shape[0] // 2
    width = vecs_ref.shape[1] // 2
    side = held_ref.shape[-1]
    row_base, col_base = lax.axis_index("row") * per_piece, lax.axis_index("col") * per_piece
    live = jnp.clip(count_ref[0, 0] - start, 0, end)

    @pl.loop(begin // GROUP, (live + GROUP - 1) // GROUP)
    def _(g):
        if arrive is not None:
            for c in range(GROUP // CHUNK):
                arrive(g * (GROUP // CHUNK) + c).wait()
        for u in range(GROUP):
            h = g * GROUP + u
            t = start + h
            i, j = list_ref[0, t], list_ref[1, t]
            within = i - col_base
            diagonal = (within == j - row_base) & (within >= 0) & (within < per_piece)
            source, at = (j, i) if forward else (i, j)
            source = jnp.where(diagonal, blocks + source, source)
            source = jnp.where(t < count_ref[0, 0], source, 2 * blocks)
            high, low = split(held_ref[h])
            if forward:
                total_ref[at] += jnp.dot(
                    jnp.concatenate([high, low], axis=1), vecs_ref[source], preferred_element_type=jnp.float32
                )
            else:
                out = jnp.dot(
                    vecs_ref[source], jnp.concatenate([high, low], axis=1), preferred_element_type=jnp.float32
                )
                total_ref[at] += out[:width, :side] + out[width:, :side] + out[:width, side:]


def forward_first_kernel(per_piece, cut, list_ref, count_ref, tiles_ref, held_ref, *refs):
    *pieces, total_ref, vecs_ref, rest_ref, sems = refs
    chunks, chunk_copy = chunk_copies(held_ref.shape[0], rest_ref.shape[0], count_ref, tiles_ref, rest_ref, sems)
    start_all(chunks, chunk_copy)
    prepare(True, lax.axis_index("row"), [ref.at[0] for ref in pieces], vecs_ref)
    total_ref[...] = jnp.zeros_like(total_ref)
    head = held_ref.shape[0]
    add_products(True, per_piece, 0, 0, head, list_ref, count_ref, held_ref, vecs_ref, total_ref)
    add_products(True, per_piece, head, 0, cut, list_ref, count_ref, rest_ref, vecs_ref, total_ref, chunk_copy)

    @pl.loop(jnp.minimum(chunks, cut // CHUNK), chunks)
    def _(k):
        chunk_copy(k).wait()


def forward_last_kernel(per_piece, head, cut, list_ref, count_ref, rest_ref, vecs_ref, _, total_ref):
    add_products(
        True, per_piece, head, cut, rest_ref.shape[0], list_ref, count_ref, rest_ref, vecs_ref, total_ref
    )


def transposed_first_kernel(per_piece, list_ref, count_ref, held_ref, own_ref, came_ref, _, total_ref, vecs_ref):
    pieces = [ref.at[q] for q in range(own_ref.shape[0]) for ref in (own_ref, came_ref)]
    prepare(False, lax.axis_index("col"), pieces, vecs_ref)
    total_ref[...] = jnp.zeros_like(total_ref)
    add_products(
        False, per_piece, 0, 0, held_ref.shape[0], list_ref, count_ref, held_ref, vecs_ref, total_ref
    )


def transposed_last_kernel(per_piece, head, list_ref, count_ref, rest_ref, vecs_ref, _, total_ref):
    add_products(
        False, per_piece, head, 0, rest_ref.shape[0], list_ref, count_ref, rest_ref, vecs_ref, total_ref
    )


def route_rows_kernel(total_ref, kept_ref, leaving_ref):
    n = 2 * kept_ref.shape[0]
    per_piece = total_ref.shape[0] // n
    width = kept_ref.shape[1]
    side = total_ref.shape[-1]
    for s in range(n):
        base = (lax.axis_index("col") ^ s) * per_piece
        out = (leaving_ref if s % 2 else kept_ref).at[s // 2]
        for b in range(per_piece):
            turned = total_ref[base + b].T
            out[:, b * side:(b + 1) * side] = turned[:width] + turned[width:2 * width]


def route_cols_kernel(total_ref, out_ref):
    n = out_ref.shape[0]
    per_piece = total_ref.shape[0] // n
    side = total_ref.shape[-1]
    for r in range(n):
        for b in range(per_piece):
            out_ref[r, :, b * side:(b + 1) * side] = total_ref[r * per_piece + b]


def add_kernel(kept_ref, came_ref, *outs):
    for q, out in enumerate(outs):
        out[...] = kept_ref[q] + came_ref[q]


def sum_kernel(*refs):
    *lines, cols_ref, basis_ref, residual_ref = refs
    vec = basis_ref.shape[0]
    total = cols_ref[0]
    for r in range(1, cols_ref.shape[0]):
        total = total + cols_ref[r]
    for line in lines:
        total = total + line[...]
    basis_ref[...] = total[:vec]
    residual_ref[...] = total[vec:]


def exchange(x, axis, offset):
    n = lax.axis_size(axis)
    return lax.ppermute(x, axis, [(a, a ^ offset) for a in range(n)])


def local(ham_tiles, tile_list, tile_count, basis_block, residual_block):
    slots, side = ham_tiles.shape[2], ham_tiles.shape[-1]
    vec, share = basis_block.shape
    width = 2 * vec
    per_piece = share // side
    n_row, n_col = lax.axis_size("row"), lax.axis_size("col")
    row_blocks, col_blocks = n_col * per_piece, n_row * per_piece
    tiles = ham_tiles[0, 0]
    listing = tile_list[0, 0].T
    head = slots * 2 // 5 // GROUP * GROUP
    rest = slots - head
    cut = rest // 3 // GROUP * GROUP
    bits = [1 << k for k in range(n_col.bit_length() - 1)]

    def call(kernel, name, out_shape, in_specs, operands, scratch=(), grant=16, share_of=1.0, aliases=None):
        single = not isinstance(out_shape, list)
        return pl.pallas_call(
            kernel,
            out_shape=out_shape,
            in_specs=in_specs,
            out_specs=VMEM if single else [VMEM] * len(out_shape),
            scratch_shapes=list(scratch),
            input_output_aliases=aliases or {},
            compiler_params=pltpu.CompilerParams(vmem_limit_bytes=grant * MIB),
            cost_estimate=pl.CostEstimate(
                flops=int(share_of * slots * 2 * side * side * width * 24),
                bytes_accessed=int(share_of * slots * side * side * 4),
                transcendentals=0,
            ),
            name=name,
        )(*operands)

    def doubled(x, bit):
        came = exchange(x, "col", bit)
        return small(interleave_kernel, f32(2 * x.shape[0], width, share), "interleave", x, came)

    own = pl.pallas_call(
        stack_kernel,
        out_shape=f32(1, width, share),
        in_specs=[ANY] * 2,
        out_specs=VMEM,
        scratch_shapes=[pltpu.SemaphoreType.DMA((2,))],
        compiler_params=pltpu.CompilerParams(vmem_limit_bytes=2 * MIB),
        name="stack_share",
    )(basis_block, residual_block)
    col_pieces = [own] + [exchange(own, "row", s) for s in range(1, n_row)]
    panel = doubled(own, bits[-1])
    held = call(
        load_kernel,
        "load_head",
        f32(head, side, side),
        [SMEM, ANY],
        (tile_count, tiles),
        [pltpu.SemaphoreType.DMA((head // CHUNK,))],
        grant=28,
        share_of=0.4,
    )
    total, vecs, held_rest = call(
        functools.partial(forward_first_kernel, per_piece, cut),
        "forward_first",
        [
            f32(row_blocks, side, side),
            jax.ShapeDtypeStruct((2 * col_blocks + 1, 2 * side, side), jnp.bfloat16),
            f32(rest, side, side),
        ],
        [SMEM, SMEM, ANY] + [VMEM] * (1 + n_row),
        (listing, tile_count, tiles, held, *col_pieces),
        [pltpu.SemaphoreType.DMA((rest // CHUNK,))],
        share_of=0.6,
    )
    panel, total = lax.optimization_barrier((panel, total))
    for bit in bits[-2:-1]:
        panel = doubled(panel, bit)
    total = call(
        functools.partial(forward_last_kernel, per_piece, head, cut),
        "forward_last",
        f32(*total.shape),
        [SMEM, SMEM, VMEM, VMEM, VMEM],
        (listing, tile_count, held_rest, vecs, total),
        share_of=0.4,
        aliases={4: 0},
    )
    panel, total = lax.optimization_barrier((panel, total))
    for bit in reversed(bits[1:-2]):
        panel = doubled(panel, bit)
    other = exchange(panel, "col", 1)
    kept, leaving = small(route_rows_kernel, [f32(n_col // 2, width, share)] * 2, "route_rows", total)
    came = exchange(leaving, "col", 1)

    total, vecs = call(
        functools.partial(transposed_first_kernel, per_piece),
        "transposed_first",
        [
            f32(col_blocks, width, side),
            jax.ShapeDtypeStruct((2 * row_blocks + 1, 2 * width, side), jnp.bfloat16),
        ],
        [SMEM, SMEM, VMEM, VMEM, VMEM, ANY],
        (listing, tile_count, held, panel, other, kept),
        share_of=0.4,
    )
    came, total = lax.optimization_barrier((came, total))
    line = small(add_kernel, [f32(width, share)] * (n_col // 2), "add_cores", kept, came)
    *line, total = lax.optimization_barrier((*line, total))
    lines = [line[0]] + [exchange(line[q], "col", 2 * q) for q in range(1, n_col // 2)]
    total = call(
        functools.partial(transposed_last_kernel, per_piece, head),
        "transposed_last",
        f32(*total.shape),
        [SMEM, SMEM, VMEM, VMEM, VMEM],
        (listing, tile_count, held_rest, vecs, total),
        share_of=0.6,
        aliases={4: 0},
    )
    cols = small(route_cols_kernel, f32(n_row, width, share), "route_columns", total)
    *lines, cols = lax.optimization_barrier((*lines, cols))
    cols = lax.all_to_all(cols, "row", 0, 0, tiled=True)
    h_basis, h_residual = small(sum_kernel, [f32(vec, share)] * 2, "sum_pieces", *lines, cols)
    return (h_basis, h_residual)


def solution(mesh):
    placed = (
        P("row", "col", None, None, None),
        P("row", "col", None, None),
        P("row", "col"),
        P(None, ("row", "col")),
        P(None, ("row", "col")),
    )
    return jax.shard_map(
        local,
        mesh=mesh,
        in_specs=placed,
        out_specs=(P(None, ("row", "col")), P(None, ("row", "col"))),
        check_vma=False,
    )
```

```python
import functools

import jax
import jax.numpy as jnp
from jax import lax
from jax.experimental import pallas as pl
from jax.experimental.pallas import tpu as pltpu
from jax.sharding import PartitionSpec as P

CHUNK = 16
GROUP = 32
MIB = 1024 * 1024
VMEM = pl.BlockSpec(memory_space=pltpu.VMEM)
SMEM = pl.BlockSpec(memory_space=pltpu.SMEM)
ANY = pl.BlockSpec(memory_space=pl.ANY)


def small(kernel, out_shape, name, *args, in_specs=None):
    single = not isinstance(out_shape, list)
    return pl.pallas_call(
        kernel,
        out_shape=out_shape,
        in_specs=in_specs or [VMEM] * len(args),
        out_specs=VMEM if single else [VMEM] * len(out_shape),
        compiler_params=pltpu.CompilerParams(vmem_limit_bytes=2 * MIB),
        name=name,
    )(*args)


def f32(*shape):
    return jax.ShapeDtypeStruct(shape, jnp.float32)


def interleave_kernel(own_ref, came_ref, out_ref):
    for q in range(own_ref.shape[0]):
        out_ref[2 * q] = own_ref[q]
        out_ref[2 * q + 1] = came_ref[q]


def split(x):
    high = x.astype(jnp.bfloat16)
    low = (x - high.astype(jnp.float32)).astype(jnp.bfloat16)
    return high, low


def prepare(forward, at, pieces, vecs_ref):
    blocks = vecs_ref.shape[0] // 2
    side = vecs_ref.shape[-1]
    width, share = pieces[0].shape
    per_piece = share // side
    for s, piece in enumerate(pieces):
        base = (at ^ s) * per_piece
        for b in range(per_piece):
            x = piece[:, b * side:(b + 1) * side]
            high = x.astype(jnp.bfloat16).astype(jnp.float32)
            rows = [high, x - high]
            if forward:
                rows = jnp.concatenate(rows + [jnp.zeros((side - 2 * width, side), jnp.float32)], axis=0).T
                rows = jnp.concatenate([rows, rows], axis=0)
            else:
                rows = jnp.concatenate(rows, axis=0)
            vecs_ref[base + b] = rows.astype(jnp.bfloat16)
            vecs_ref[blocks + base + b] = (rows * 0.5).astype(jnp.bfloat16)
    vecs_ref[2 * blocks] = jnp.zeros_like(vecs_ref[2 * blocks])


def chunk_copies(count_ref, tiles_ref, held_ref, sems):
    chunks = (count_ref[0, 0] + GROUP - 1) // GROUP * (GROUP // CHUNK)

    def chunk_copy(k):
        part = pl.ds(k * CHUNK, CHUNK)
        return pltpu.make_async_copy(tiles_ref.at[part], held_ref.at[part], sems.at[k])

    return chunks, chunk_copy


def source_of(per_piece, blocks, block, i, j):
    within = i - lax.axis_index("col") * per_piece
    diagonal = (within == j - lax.axis_index("row") * per_piece) & (within >= 0) & (within < per_piece)
    return jnp.where(diagonal, blocks + block, block)


def load_kernel(per_piece, row_blocks, col_blocks, head, list_ref, count_ref, tiles_ref, held_ref, order_ref, sems):
    chunks, chunk_copy = chunk_copies(count_ref, tiles_ref, held_ref, sems)
    chunks = jnp.minimum(chunks, head // CHUNK)

    @pl.loop(0, chunks)
    def _(k):
        chunk_copy(k).start()

    def place(t, counts):
        upper, lower = counts
        i, j = list_ref[0, t], list_ref[1, t]
        is_upper = j >= col_blocks // 2
        row = jnp.where(is_upper, 0, 3)
        at = jnp.where(is_upper, upper, lower)
        order_ref[row, at] = t
        order_ref[row + 1, at] = source_of(per_piece, row_blocks, i, i, j)
        order_ref[row + 2, at] = j
        step = is_upper.astype(jnp.int32)
        return upper + step, lower + 1 - step

    counts = lax.fori_loop(0, count_ref[0, 0], place, (jnp.int32(0), jnp.int32(0)))
    for side, count in enumerate(counts):
        groups = (count + GROUP - 1) // GROUP
        order_ref[6, side] = groups

        @pl.loop(count, groups * GROUP)
        def _(at):
            order_ref[3 * side, at] = 0
            order_ref[3 * side + 1, at] = 2 * row_blocks
            order_ref[3 * side + 2, at] = 0

    @pl.loop(0, chunks)
    def _(k):
        chunk_copy(k).wait()


def add_forward(per_piece, begin, end, list_ref, count_ref, held_ref, vecs_ref, total_ref, arrive=None):
    blocks = vecs_ref.shape[0] // 2
    live = jnp.minimum(count_ref[0, 0], end)

    @pl.loop(begin // GROUP, (live + GROUP - 1) // GROUP)
    def _(g):
        if arrive is not None:
            for c in range(GROUP // CHUNK):
                arrive(g * (GROUP // CHUNK) + c).wait()
        for u in range(GROUP):
            t = g * GROUP + u
            i, j = list_ref[0, t], list_ref[1, t]
            source = source_of(per_piece, blocks, j, i, j)
            source = jnp.where(t < count_ref[0, 0], source, 2 * blocks)
            high, low = split(held_ref[t])
            total_ref[i] += jnp.dot(
                jnp.concatenate([high, low], axis=1), vecs_ref[source], preferred_element_type=jnp.float32
            )


def forward_first_kernel(per_piece, head, cut, list_ref, count_ref, tiles_ref, _, *refs):
    *pieces, total_ref, vecs_ref, held_ref, sems = refs
    chunks, chunk_copy = chunk_copies(count_ref, tiles_ref, held_ref, sems)

    @pl.loop(head // CHUNK, chunks)
    def _(k):
        chunk_copy(k).start()

    prepare(True, lax.axis_index("row"), pieces, vecs_ref)
    total_ref[...] = jnp.zeros_like(total_ref)
    add_forward(per_piece, 0, head, list_ref, count_ref, held_ref, vecs_ref, total_ref)
    add_forward(per_piece, head, cut, list_ref, count_ref, held_ref, vecs_ref, total_ref, chunk_copy)

    @pl.loop(jnp.minimum(chunks, cut // CHUNK), chunks)
    def _(k):
        chunk_copy(k).wait()


def forward_last_kernel(per_piece, cut, list_ref, count_ref, held_ref, vecs_ref, _, total_ref):
    add_forward(per_piece, cut, held_ref.shape[0], list_ref, count_ref, held_ref, vecs_ref, total_ref)


def add_transposed(part, order_ref, held_ref, vecs_ref, total_ref):
    width, side = total_ref.shape[1:]

    @pl.loop(0, order_ref[6, part])
    def _(g):
        for u in range(GROUP):
            at = g * GROUP + u
            slot, source, block = (order_ref[3 * part + row, at] for row in range(3))
            high, low = split(held_ref[slot])
            out = jnp.dot(
                vecs_ref[source], jnp.concatenate([high, low], axis=1), preferred_element_type=jnp.float32
            )
            total_ref[block] += out[:width, :side] + out[width:, :side] + out[:width, side:]


def transposed_first_kernel(order_ref, held_ref, own_ref, came_ref, _, total_ref, vecs_ref):
    pieces = [ref.at[q] for q in range(own_ref.shape[0]) for ref in (own_ref, came_ref)]
    prepare(False, lax.axis_index("col"), pieces, vecs_ref)
    total_ref[...] = jnp.zeros_like(total_ref)
    add_transposed(0, order_ref, held_ref, vecs_ref, total_ref)


def transposed_last_kernel(order_ref, held_ref, vecs_ref, _, total_ref):
    add_transposed(1, order_ref, held_ref, vecs_ref, total_ref)


def route_rows_kernel(total_ref, kept_ref, leaving_ref):
    n = 2 * kept_ref.shape[0]
    per_piece = total_ref.shape[0] // n
    width = kept_ref.shape[1]
    side = total_ref.shape[-1]
    for s in range(n):
        base = (lax.axis_index("col") ^ s) * per_piece
        out = (leaving_ref if s % 2 else kept_ref).at[s // 2]
        for b in range(per_piece):
            turned = total_ref[base + b].T
            out[:, b * side:(b + 1) * side] = turned[:width] + turned[width:2 * width]


def route_cols_kernel(offsets, total_ref, *outs):
    width, share = outs[0].shape
    side = total_ref.shape[-1]
    for s, out in zip(offsets, outs):
        base = (lax.axis_index("row") ^ s) * (share // side)
        for b in range(share // side):
            out[:, b * side:(b + 1) * side] = total_ref[base + b]


def add_kernel(kept_ref, came_ref, *outs):
    for q, out in enumerate(outs):
        out[...] = kept_ref[q] + came_ref[q]


def sum_kernel(*refs):
    *ins, basis_ref, residual_ref = refs
    vec = basis_ref.shape[0]
    total = ins[0][...]
    for ref in ins[1:]:
        total = total + ref[...]
    basis_ref[...] = total[:vec]
    residual_ref[...] = total[vec:]


def exchange(x, axis, offset):
    n = lax.axis_size(axis)
    return lax.ppermute(x, axis, [(a, a ^ offset) for a in range(n)])


def local(ham_tiles, tile_list, tile_count, basis_block, residual_block):
    slots, side = ham_tiles.shape[2], ham_tiles.shape[-1]
    vec, share = basis_block.shape
    width = 2 * vec
    per_piece = share // side
    n_row, n_col = lax.axis_size("row"), lax.axis_size("col")
    row_blocks, col_blocks = n_col * per_piece, n_row * per_piece
    tiles = ham_tiles[0, 0]
    listing = tile_list[0, 0].T
    head = slots * 2 // 5 // GROUP * GROUP
    cut = slots // 2 // GROUP * GROUP
    bits = [1 << k for k in range(n_col.bit_length() - 1)]

    def call(kernel, name, out_shape, in_specs, operands, scratch=(), grant=16, share_of=1.0, aliases=None):
        single = not isinstance(out_shape, list)
        return pl.pallas_call(
            kernel,
            out_shape=out_shape,
            in_specs=in_specs,
            out_specs=VMEM if single else [VMEM] * len(out_shape),
            scratch_shapes=list(scratch),
            input_output_aliases=aliases or {},
            compiler_params=pltpu.CompilerParams(vmem_limit_bytes=grant * MIB),
            cost_estimate=pl.CostEstimate(
                flops=int(share_of * slots * 2 * side * side * width * 24),
                bytes_accessed=int(share_of * slots * side * side * 4),
                transcendentals=0,
            ),
            name=name,
        )(*operands)

    own = lax.pad(basis_block, 0.0, ((0, vec, 0), (0, 0, 0))) + lax.pad(residual_block, 0.0, ((vec, 0, 0), (0, 0, 0)))
    col_pieces = [own] + [exchange(own, "row", s) for s in range(1, n_row)]
    panel = own.reshape(1, width, share)
    came = exchange(panel, "col", bits[-1])
    chunk_sems = pltpu.SemaphoreType.DMA((slots // CHUNK,))
    held, order = pl.pallas_call(
        functools.partial(load_kernel, per_piece, row_blocks, col_blocks, head),
        out_shape=[f32(slots, side, side), jax.ShapeDtypeStruct((8, slots), jnp.int32)],
        in_specs=[SMEM, SMEM, ANY],
        out_specs=[VMEM, SMEM],
        scratch_shapes=[chunk_sems],
        compiler_params=pltpu.CompilerParams(vmem_limit_bytes=16 * MIB),
        cost_estimate=pl.CostEstimate(flops=0, bytes_accessed=head * side * side * 4, transcendentals=0),
        name="load_head",
    )(listing, tile_count, tiles)
    total, vecs, held = call(
        functools.partial(forward_first_kernel, per_piece, head, cut),
        "forward_first",
        [
            f32(row_blocks, side, side),
            jax.ShapeDtypeStruct((2 * col_blocks + 1, 2 * side, side), jnp.bfloat16),
            f32(slots, side, side),
        ],
        [SMEM, SMEM, ANY] + [VMEM] * (1 + n_row),
        (listing, tile_count, tiles, held, *col_pieces),
        [chunk_sems],
        share_of=0.5,
        aliases={3: 2},
    )
    for bit in bits[-2:-1]:
        came, total = lax.optimization_barrier((came, total))
        panel = small(interleave_kernel, f32(2 * panel.shape[0], width, share), "interleave", panel, came)
        came = exchange(panel, "col", bit)
    total = call(
        functools.partial(forward_last_kernel, per_piece, cut),
        "forward_last",
        f32(*total.shape),
        [SMEM, SMEM, VMEM, VMEM, VMEM],
        (listing, tile_count, held, vecs, total),
        share_of=0.5,
        aliases={4: 0},
    )
    for bit in reversed(bits[:-2]):
        came, total = lax.optimization_barrier((came, total))
        panel = small(interleave_kernel, f32(2 * panel.shape[0], width, share), "interleave", panel, came)
        came = exchange(panel, "col", bit)
    kept, leaving = small(route_rows_kernel, [f32(n_col // 2, width, share)] * 2, "route_rows", total)
    from_core = exchange(leaving, "col", 1)

    total, vecs = call(
        transposed_first_kernel,
        "transposed_first",
        [
            f32(col_blocks, width, side),
            jax.ShapeDtypeStruct((2 * row_blocks + 1, 2 * width, side), jnp.bfloat16),
        ],
        [SMEM, VMEM, VMEM, VMEM, ANY],
        (order, held, panel, came, kept),
        share_of=0.5,
    )
    piece = f32(width, share)
    upper = list(range(n_row // 2, n_row))
    lower = list(range(n_row // 2))
    from_core, total = lax.optimization_barrier((from_core, total))
    line = small(add_kernel, [piece] * (n_col // 2), "add_cores", kept, from_core)
    away = small(functools.partial(route_cols_kernel, upper), [piece] * len(upper), "route_upper", total)
    *line, total = lax.optimization_barrier((*line, total))
    lines = [line[0]] + [exchange(line[q], "col", 2 * q) for q in range(1, n_col // 2)]
    cols = [exchange(x, "row", s) for s, x in zip(upper, away)]
    total = call(
        transposed_last_kernel,
        "transposed_last",
        f32(*total.shape),
        [SMEM, VMEM, VMEM, VMEM],
        (order, held, vecs, total),
        share_of=0.5,
        aliases={3: 0},
    )
    *ready, total = lax.optimization_barrier((*lines, *cols, total))
    lines, cols = ready[:len(lines)], ready[len(lines):]
    away = small(functools.partial(route_cols_kernel, lower), [piece] * len(lower), "route_lower", total)
    cols += [away[0]] + [exchange(x, "row", s) for s, x in zip(lower[1:], away[1:])]
    h_basis, h_residual = small(sum_kernel, [f32(vec, share)] * 2, "sum_pieces", *lines, *cols)
    return (h_basis, h_residual)


def solution(mesh):
    placed = (
        P("row", "col", None, None, None),
        P("row", "col", None, None),
        P("row", "col"),
        P(None, ("row", "col")),
        P(None, ("row", "col")),
    )
    return jax.shard_map(
        local,
        mesh=mesh,
        in_specs=placed,
        out_specs=(P(None, ("row", "col")), P(None, ("row", "col"))),
        check_vma=False,
    )
```

```python
import functools

import jax
import jax.numpy as jnp
from jax import lax
from jax.experimental import pallas as pl
from jax.experimental.pallas import tpu as pltpu
from jax.sharding import PartitionSpec as P

CHUNK = 16
GROUP = 32
SHIFT = 10
MIB = 1024 * 1024
VMEM = pl.BlockSpec(memory_space=pltpu.VMEM)
SMEM = pl.BlockSpec(memory_space=pltpu.SMEM)
ANY = pl.BlockSpec(memory_space=pl.ANY)


def small(kernel, out_shape, name, *args, in_specs=None):
    single = not isinstance(out_shape, list)
    return pl.pallas_call(
        kernel,
        out_shape=out_shape,
        in_specs=in_specs or [VMEM] * len(args),
        out_specs=VMEM if single else [VMEM] * len(out_shape),
        compiler_params=pltpu.CompilerParams(vmem_limit_bytes=2 * MIB),
        name=name,
    )(*args)


def f32(*shape):
    return jax.ShapeDtypeStruct(shape, jnp.float32)


def gather_kernel(*refs):
    *ins, out_ref = refs
    for q, ref in enumerate(ins):
        out_ref[q] = ref[...]


def split(x):
    high = x.astype(jnp.bfloat16)
    low = (x - high.astype(jnp.float32)).astype(jnp.bfloat16)
    return high, low


def prepare(forward, at, pieces, vecs_ref):
    blocks = vecs_ref.shape[0] // 2
    side = vecs_ref.shape[-1]
    width, share = pieces[0].shape
    per_piece = share // side
    for s, piece in enumerate(pieces):
        base = (at ^ s) * per_piece
        for b in range(per_piece):
            x = piece[:, b * side:(b + 1) * side]
            high = x.astype(jnp.bfloat16).astype(jnp.float32)
            rows = [high, x - high]
            if forward:
                rows = jnp.concatenate(rows + [jnp.zeros((side - 2 * width, side), jnp.float32)], axis=0).T
                rows = jnp.concatenate([rows, rows], axis=0)
            else:
                rows = jnp.concatenate(rows, axis=0)
            vecs_ref[base + b] = rows.astype(jnp.bfloat16)
            vecs_ref[blocks + base + b] = (rows * 0.5).astype(jnp.bfloat16)
    vecs_ref[2 * blocks] = jnp.zeros_like(vecs_ref[2 * blocks])


def source_of(per_piece, blocks, block, i, j):
    within = i - lax.axis_index("col") * per_piece
    diagonal = (within == j - lax.axis_index("row") * per_piece) & (within >= 0) & (within < per_piece)
    return jnp.where(diagonal, blocks + block, block)


def forward_kernel(per_piece, list_ref, count_ref, tiles_ref, *refs):
    *pieces, total_ref, held_ref, order_ref, vecs_ref, places_ref, list_sem, sems = refs
    count = count_ref[0, 0]
    groups = (count + GROUP - 1) // GROUP
    per_group = GROUP // CHUNK
    blocks = vecs_ref.shape[0] // 2
    row_blocks = total_ref.shape[0]

    def chunk_copy(k):
        part = pl.ds(k * CHUNK, CHUNK)
        return pltpu.make_async_copy(tiles_ref.at[part], held_ref.at[part], sems.at[k])

    @pl.loop(0, groups * per_group)
    def _(k):
        chunk_copy(k).start()

    list_copy = pltpu.make_async_copy(list_ref, places_ref, list_sem)
    list_copy.start()
    prepare(True, lax.axis_index("row"), pieces, vecs_ref)
    total_ref[...] = jnp.zeros_like(total_ref)
    list_copy.wait()

    def group(g, counts):
        upper, lower = counts
        for c in range(per_group):
            chunk_copy(g * per_group + c).wait()
        for u in range(GROUP):
            t = g * GROUP + u
            i, j = places_ref[0, t], places_ref[1, t]
            live = t < count
            source = jnp.where(live, source_of(per_piece, blocks, j, i, j), 2 * blocks)
            high, low = split(held_ref[t])
            total_ref[i] += jnp.dot(
                jnp.concatenate([high, low], axis=1), vecs_ref[source], preferred_element_type=jnp.float32
            )
            is_upper = j >= blocks // 2
            word = t + (source_of(per_piece, row_blocks, i, i, j) << SHIFT) + (j << (2 * SHIFT))
            order_ref[jnp.where(is_upper, 0, 1), jnp.where(is_upper, upper, lower)] = word
            upper += jnp.where(live & is_upper, 1, 0)
            lower += jnp.where(live & ~is_upper, 1, 0)
        return upper, lower

    upper, lower = lax.fori_loop(0, groups, group, (jnp.int32(0), jnp.int32(0)))
    order_ref[2, 0] = upper
    order_ref[2, 1] = lower


def add_transposed(part, order_ref, held_ref, vecs_ref, total_ref):
    width, side = total_ref.shape[1:]
    count = order_ref[2, part]
    mask = (1 << SHIFT) - 1
    nothing = vecs_ref.shape[0] // 2 * 2 << SHIFT

    @pl.loop(0, (count + GROUP - 1) // GROUP)
    def _(g):
        for u in range(GROUP):
            at = g * GROUP + u
            word = jnp.where(at < count, order_ref[part, at], nothing)
            slot, source, block = word & mask, (word >> SHIFT) & mask, word >> (2 * SHIFT)
            high, low = split(held_ref[slot])
            out = jnp.dot(
                vecs_ref[source], jnp.concatenate([high, low], axis=1), preferred_element_type=jnp.float32
            )
            total_ref[block] += out[:width, :side] + out[width:, :side] + out[:width, side:]


def transposed_first_kernel(order_ref, held_ref, own_ref, came_ref, _, total_ref, vecs_ref):
    pieces = [ref.at[q] for q in range(own_ref.shape[0]) for ref in (own_ref, came_ref)]
    prepare(False, lax.axis_index("col"), pieces, vecs_ref)
    total_ref[...] = jnp.zeros_like(total_ref)
    add_transposed(0, order_ref, held_ref, vecs_ref, total_ref)


def transposed_last_kernel(order_ref, held_ref, vecs_ref, _, total_ref):
    add_transposed(1, order_ref, held_ref, vecs_ref, total_ref)


def route_rows_kernel(total_ref, kept_ref, leaving_ref):
    n = 2 * kept_ref.shape[0]
    per_piece = total_ref.shape[0] // n
    width = kept_ref.shape[1]
    side = total_ref.shape[-1]
    for s in range(n):
        base = (lax.axis_index("col") ^ s) * per_piece
        out = (leaving_ref if s % 2 else kept_ref).at[s // 2]
        for b in range(per_piece):
            turned = total_ref[base + b].T
            out[:, b * side:(b + 1) * side] = turned[:width] + turned[width:2 * width]


def route_cols_kernel(offsets, total_ref, *outs):
    width, share = outs[0].shape
    side = total_ref.shape[-1]
    for s, out in zip(offsets, outs):
        base = (lax.axis_index("row") ^ s) * (share // side)
        for b in range(share // side):
            out[:, b * side:(b + 1) * side] = total_ref[base + b]


def add_kernel(kept_ref, came_ref, *outs):
    for q, out in enumerate(outs):
        out[...] = kept_ref[q] + came_ref[q]


def sum_kernel(*refs):
    *ins, basis_ref, residual_ref = refs
    vec = basis_ref.shape[0]
    total = ins[0][...]
    for ref in ins[1:]:
        total = total + ref[...]
    basis_ref[...] = total[:vec]
    residual_ref[...] = total[vec:]


def exchange(x, axis, offset):
    n = lax.axis_size(axis)
    return lax.ppermute(x, axis, [(a, a ^ offset) for a in range(n)])


def local(ham_tiles, tile_list, tile_count, basis_block, residual_block):
    slots, side = ham_tiles.shape[2], ham_tiles.shape[-1]
    vec, share = basis_block.shape
    width = 2 * vec
    per_piece = share // side
    n_row, n_col = lax.axis_size("row"), lax.axis_size("col")
    row_blocks, col_blocks = n_col * per_piece, n_row * per_piece
    tiles = ham_tiles[0, 0]
    listing = tile_list[0, 0].T
    def cost(part):
        return pl.CostEstimate(
            flops=int(part * slots * 2 * side * side * width * 24),
            bytes_accessed=int(part * slots * side * side * 4),
            transcendentals=0,
        )

    def call(kernel, name, out_shape, in_specs, operands, aliases=None):
        single = not isinstance(out_shape, list)
        return pl.pallas_call(
            kernel,
            out_shape=out_shape,
            in_specs=in_specs,
            out_specs=VMEM if single else [VMEM] * len(out_shape),
            input_output_aliases=aliases or {},
            compiler_params=pltpu.CompilerParams(vmem_limit_bytes=16 * MIB),
            cost_estimate=cost(0.5),
            name=name,
        )(*operands)

    own = lax.pad(basis_block, 0.0, ((0, vec, 0), (0, 0, 0))) + lax.pad(residual_block, 0.0, ((vec, 0, 0), (0, 0, 0)))
    col_pieces = [own] + [exchange(own, "row", s) for s in range(1, n_row)]
    line = [own] + [exchange(own, "col", s) for s in range(2, n_col, 2)]
    total, held, order = pl.pallas_call(
        functools.partial(forward_kernel, per_piece),
        out_shape=[
            f32(row_blocks, side, side),
            f32(slots, side, side),
            jax.ShapeDtypeStruct((4, slots), jnp.int32),
        ],
        in_specs=[ANY, SMEM, ANY] + [VMEM] * n_row,
        out_specs=[VMEM, VMEM, SMEM],
        scratch_shapes=[
            pltpu.VMEM((2 * col_blocks + 1, 2 * side, side), jnp.bfloat16),
            pltpu.SMEM(listing.shape, jnp.int32),
            pltpu.SemaphoreType.DMA(()),
            pltpu.SemaphoreType.DMA((slots // CHUNK,)),
        ],
        compiler_params=pltpu.CompilerParams(vmem_limit_bytes=16 * MIB),
        cost_estimate=cost(1.0),
        name="forward_product",
    )(listing, tile_count, tiles, *col_pieces)
    *line, total = lax.optimization_barrier((*line, total))
    panel = small(gather_kernel, f32(n_col // 2, width, share), "gather_line", *line)
    came = exchange(panel, "col", 1)
    kept, leaving = small(route_rows_kernel, [f32(n_col // 2, width, share)] * 2, "route_rows", total)
    from_core = exchange(leaving, "col", 1)

    total, vecs = call(
        transposed_first_kernel,
        "transposed_first",
        [
            f32(col_blocks, width, side),
            jax.ShapeDtypeStruct((2 * row_blocks + 1, 2 * width, side), jnp.bfloat16),
        ],
        [SMEM, VMEM, VMEM, VMEM, ANY],
        (order, held, panel, came, kept),
    )
    piece = f32(width, share)
    upper = list(range(n_row // 2, n_row))
    lower = list(range(n_row // 2))
    from_core, total = lax.optimization_barrier((from_core, total))
    line = small(add_kernel, [piece] * (n_col // 2), "add_cores", kept, from_core)
    away = small(functools.partial(route_cols_kernel, upper), [piece] * len(upper), "route_upper", total)
    *line, total = lax.optimization_barrier((*line, total))
    lines = [line[0]] + [exchange(line[q], "col", 2 * q) for q in range(1, n_col // 2)]
    cols = [exchange(x, "row", s) for s, x in zip(upper, away)]
    total = call(
        transposed_last_kernel,
        "transposed_last",
        f32(*total.shape),
        [SMEM, VMEM, VMEM, VMEM],
        (order, held, vecs, total),
        aliases={3: 0},
    )
    *ready, total = lax.optimization_barrier((*lines, *cols, total))
    lines, cols = ready[:len(lines)], ready[len(lines):]
    away = small(functools.partial(route_cols_kernel, lower), [piece] * len(lower), "route_lower", total)
    cols += [away[0]] + [exchange(x, "row", s) for s, x in zip(lower[1:], away[1:])]
    h_basis, h_residual = small(sum_kernel, [f32(vec, share)] * 2, "sum_pieces", *lines, *cols)
    return (h_basis, h_residual)


def solution(mesh):
    placed = (
        P("row", "col", None, None, None),
        P("row", "col", None, None),
        P("row", "col"),
        P(None, ("row", "col")),
        P(None, ("row", "col")),
    )
    return jax.shard_map(
        local,
        mesh=mesh,
        in_specs=placed,
        out_specs=(P(None, ("row", "col")), P(None, ("row", "col"))),
        check_vma=False,
    )
```

```python
import functools

import jax
import jax.numpy as jnp
from jax import lax
from jax.experimental import pallas as pl
from jax.experimental.pallas import tpu as pltpu
from jax.sharding import PartitionSpec as P

CHUNK = 16
GROUP = 32
SHIFT = 10
MIB = 1024 * 1024
VMEM = pl.BlockSpec(memory_space=pltpu.VMEM)
SMEM = pl.BlockSpec(memory_space=pltpu.SMEM)
ANY = pl.BlockSpec(memory_space=pl.ANY)


def small(kernel, out_shape, name, *args, in_specs=None):
    single = not isinstance(out_shape, list)
    return pl.pallas_call(
        kernel,
        out_shape=out_shape,
        in_specs=in_specs or [VMEM] * len(args),
        out_specs=VMEM if single else [VMEM] * len(out_shape),
        compiler_params=pltpu.CompilerParams(vmem_limit_bytes=2 * MIB),
        name=name,
    )(*args)


def f32(*shape):
    return jax.ShapeDtypeStruct(shape, jnp.float32)


def gather_kernel(*refs):
    *ins, out_ref = refs
    for q, ref in enumerate(ins):
        out_ref[q] = ref[...]


def split(x):
    high = x.astype(jnp.bfloat16)
    low = (x - high.astype(jnp.float32)).astype(jnp.bfloat16)
    return high, low


def prepare(forward, origins, pieces, vecs_ref):
    blocks = vecs_ref.shape[0] // 2
    side = vecs_ref.shape[-1]
    width, share = pieces[0].shape
    per_piece = share // side
    for origin, piece in zip(origins, pieces):
        base = origin * per_piece
        for b in range(per_piece):
            x = piece[:, b * side:(b + 1) * side]
            high = x.astype(jnp.bfloat16).astype(jnp.float32)
            rows = [high, x - high]
            if forward:
                rows = jnp.concatenate(rows + [jnp.zeros((side - 2 * width, side), jnp.float32)], axis=0).T
                rows = jnp.concatenate([rows, rows], axis=0)
            else:
                rows = jnp.concatenate(rows, axis=0)
            vecs_ref[base + b] = rows.astype(jnp.bfloat16)
            vecs_ref[blocks + base + b] = (rows * 0.5).astype(jnp.bfloat16)
    vecs_ref[2 * blocks] = jnp.zeros_like(vecs_ref[2 * blocks])


def shifted(steps, n):
    return lax.rem(lax.axis_index("col") + steps % n, n)


def is_diagonal(per_piece, i, j):
    row_base, col_base = lax.axis_index("row") * per_piece, lax.axis_index("col") * per_piece
    return (i - j == col_base - row_base) & (j >= row_base) & (j < row_base + per_piece)


def load_kernel(head, count_ref, tiles_ref, _, held_ref, sems):
    chunks = jnp.minimum((count_ref[0, 0] + GROUP - 1) // GROUP * GROUP, head) // CHUNK

    def chunk_copy(k):
        part = pl.ds(k * CHUNK, CHUNK)
        return pltpu.make_async_copy(tiles_ref.at[part], held_ref.at[part], sems.at[k])

    @pl.loop(0, chunks)
    def _(k):
        chunk_copy(k).start()

    @pl.loop(0, chunks)
    def _(k):
        chunk_copy(k).wait()


def forward_kernel(per_piece, head, list_ref, count_ref, tiles_ref, _, *refs):
    *pieces, total_ref, held_ref, order_ref, vecs_ref, places_ref, list_sem, sems = refs
    count = count_ref[0, 0]
    groups = (count + GROUP - 1) // GROUP
    per_group = GROUP // CHUNK
    blocks = vecs_ref.shape[0] // 2
    row_blocks = total_ref.shape[0]

    def chunk_copy(k):
        part = pl.ds(k * CHUNK, CHUNK)
        return pltpu.make_async_copy(tiles_ref.at[part], held_ref.at[part], sems.at[k])

    @pl.loop(head // CHUNK, groups * per_group)
    def _(k):
        chunk_copy(k).start()

    list_copy = pltpu.make_async_copy(list_ref, places_ref, list_sem)
    list_copy.start()
    row_at = lax.axis_index("row")
    prepare(True, [row_at ^ s for s in range(len(pieces))], pieces, vecs_ref)
    total_ref[...] = jnp.zeros_like(total_ref)
    list_copy.wait()

    def group(wait, g, upper):
        if wait:
            for c in range(per_group):
                chunk_copy(g * per_group + c).wait()
        for u in range(GROUP):
            t = g * GROUP + u
            i, j = places_ref[0, t], places_ref[1, t]
            live = t < count
            half = is_diagonal(per_piece, i, j)
            source = jnp.where(live, jnp.where(half, j + blocks, j), 2 * blocks)
            high, low = split(held_ref[t])
            total_ref[i] += jnp.dot(
                jnp.concatenate([high, low], axis=1), vecs_ref[source], preferred_element_type=jnp.float32
            )
            word = (jnp.where(half, i + row_blocks, i) << SHIFT) + ((j << (2 * SHIFT)) + t)
            order_ref[0, upper] = word
            order_ref[1, t - upper] = word
            upper += jnp.where(live & (j >= blocks // 2), 1, 0)
        return upper

    mine = jnp.minimum(groups, head // GROUP)
    upper = lax.fori_loop(0, mine, functools.partial(group, False), jnp.int32(0))
    upper = lax.fori_loop(mine, groups, functools.partial(group, True), upper)
    order_ref[2, 0] = upper
    order_ref[2, 1] = count - upper


def add_transposed(part, order_ref, held_ref, vecs_ref, total_ref):
    width, side = total_ref.shape[1:]
    count = order_ref[2, part]
    mask = (1 << SHIFT) - 1
    nothing = vecs_ref.shape[0] // 2 * 2 << SHIFT

    @pl.loop(0, (count + GROUP - 1) // GROUP)
    def _(g):
        for u in range(GROUP):
            at = g * GROUP + u
            word = jnp.where(at < count, order_ref[part, at], nothing)
            slot, source, block = word & mask, (word >> SHIFT) & mask, word >> (2 * SHIFT)
            high, low = split(held_ref[slot])
            out = jnp.dot(
                vecs_ref[source], jnp.concatenate([high, low], axis=1), preferred_element_type=jnp.float32
            )
            total_ref[block] += out[:width, :side] + out[width:, :side] + out[:width, side:]


def transposed_first_kernel(order_ref, held_ref, own_ref, came_ref, _, total_ref, vecs_ref):
    half = own_ref.shape[0]
    origins = [shifted(-2 * q, 2 * half) for q in range(half)]
    prepare(
        False,
        origins + [origin ^ 1 for origin in origins],
        [ref.at[q] for ref in (own_ref, came_ref) for q in range(half)],
        vecs_ref,
    )
    total_ref[...] = jnp.zeros_like(total_ref)
    add_transposed(0, order_ref, held_ref, vecs_ref, total_ref)


def transposed_last_kernel(order_ref, held_ref, vecs_ref, _, total_ref):
    add_transposed(1, order_ref, held_ref, vecs_ref, total_ref)


def route_rows_kernel(total_ref, kept_ref, leaving_ref):
    n = 2 * kept_ref.shape[0]
    per_piece = total_ref.shape[0] // n
    width = kept_ref.shape[1]
    side = total_ref.shape[-1]
    for s in range(n):
        base = (shifted(s // 2 * 2, n) ^ (s % 2)) * per_piece
        out = (leaving_ref if s % 2 else kept_ref).at[s // 2]
        for b in range(per_piece):
            turned = total_ref[base + b].T
            out[:, b * side:(b + 1) * side] = turned[:width] + turned[width:2 * width]


def route_cols_kernel(offsets, total_ref, *outs):
    width, share = outs[0].shape
    side = total_ref.shape[-1]
    for s, out in zip(offsets, outs):
        base = (lax.axis_index("row") ^ s) * (share // side)
        for b in range(share // side):
            out[:, b * side:(b + 1) * side] = total_ref[base + b]


def add_kernel(kept_ref, came_ref, *outs):
    for q, out in enumerate(outs):
        out[...] = kept_ref[q] + came_ref[q]


def sum_kernel(*refs):
    *ins, basis_ref, residual_ref = refs
    vec = basis_ref.shape[0]
    total = ins[0][...]
    for ref in ins[1:]:
        total = total + ref[...]
    basis_ref[...] = total[:vec]
    residual_ref[...] = total[vec:]


def exchange(x, axis, offset):
    n = lax.axis_size(axis)
    return lax.ppermute(x, axis, [(a, a ^ offset) for a in range(n)])


def shift(x, steps):
    n = lax.axis_size("col")
    return lax.ppermute(x, "col", [(a, (a + steps) % n) for a in range(n)])


def local(ham_tiles, tile_list, tile_count, basis_block, residual_block):
    slots, side = ham_tiles.shape[2], ham_tiles.shape[-1]
    vec, share = basis_block.shape
    width = 2 * vec
    per_piece = share // side
    n_row, n_col = lax.axis_size("row"), lax.axis_size("col")
    row_blocks, col_blocks = n_col * per_piece, n_row * per_piece
    tiles = ham_tiles[0, 0]
    listing = tile_list[0, 0].T
    def cost(part):
        return pl.CostEstimate(
            flops=int(part * slots * 2 * side * side * width * 24),
            bytes_accessed=int(part * slots * side * side * 4),
            transcendentals=0,
        )

    def call(kernel, name, out_shape, in_specs, operands, aliases=None):
        single = not isinstance(out_shape, list)
        return pl.pallas_call(
            kernel,
            out_shape=out_shape,
            in_specs=in_specs,
            out_specs=VMEM if single else [VMEM] * len(out_shape),
            input_output_aliases=aliases or {},
            compiler_params=pltpu.CompilerParams(vmem_limit_bytes=16 * MIB),
            cost_estimate=cost(0.5),
            name=name,
        )(*operands)

    own = lax.pad(basis_block, 0.0, ((0, vec, 0), (0, 0, 0))) + lax.pad(residual_block, 0.0, ((vec, 0, 0), (0, 0, 0)))
    col_pieces = [own] + [exchange(own, "row", s) for s in range(1, n_row)]
    line = [own] + [shift(own, s) for s in range(2, n_col, 2)]
    params = pltpu.CompilerParams(vmem_limit_bytes=16 * MIB)
    chunk_sems = pltpu.SemaphoreType.DMA((slots // CHUNK,))
    head = slots // 5 // GROUP * GROUP
    held = pl.pallas_call(
        functools.partial(load_kernel, head),
        out_shape=f32(slots, side, side),
        in_specs=[SMEM, ANY, ANY],
        out_specs=VMEM,
        scratch_shapes=[chunk_sems],
        compiler_params=params,
        cost_estimate=cost(0.2),
        name="load_head",
    )(tile_count, tiles, listing)
    total, held, order = pl.pallas_call(
        functools.partial(forward_kernel, per_piece, head),
        out_shape=[
            f32(row_blocks, side, side),
            f32(slots, side, side),
            jax.ShapeDtypeStruct((4, slots), jnp.int32),
        ],
        in_specs=[ANY, SMEM, ANY, VMEM] + [VMEM] * n_row,
        out_specs=[VMEM, VMEM, SMEM],
        scratch_shapes=[
            pltpu.VMEM((2 * col_blocks + 1, 2 * side, side), jnp.bfloat16),
            pltpu.SMEM(listing.shape, jnp.int32),
            pltpu.SemaphoreType.DMA(()),
            chunk_sems,
        ],
        input_output_aliases={3: 1},
        compiler_params=params,
        cost_estimate=cost(1.0),
        name="forward_product",
    )(listing, tile_count, tiles, held, *col_pieces)
    *line, total = lax.optimization_barrier((*line, total))
    panel = small(gather_kernel, f32(n_col // 2, width, share), "gather_line", *line)
    came = exchange(panel, "col", 1)
    kept, leaving = small(route_rows_kernel, [f32(n_col // 2, width, share)] * 2, "route_rows", total)
    from_core = exchange(leaving, "col", 1)

    total, vecs = call(
        transposed_first_kernel,
        "transposed_first",
        [
            f32(col_blocks, width, side),
            jax.ShapeDtypeStruct((2 * row_blocks + 1, 2 * width, side), jnp.bfloat16),
        ],
        [SMEM, VMEM, VMEM, VMEM, ANY],
        (order, held, panel, came, kept),
    )
    piece = f32(width, share)
    upper = list(range(n_row // 2, n_row))
    lower = list(range(n_row // 2))
    from_core, total = lax.optimization_barrier((from_core, total))
    line = small(add_kernel, [piece] * (n_col // 2), "add_cores", kept, from_core)
    away = small(functools.partial(route_cols_kernel, upper), [piece] * len(upper), "route_upper", total)
    *line, total = lax.optimization_barrier((*line, total))
    lines = [line[0]] + [shift(line[q], 2 * q) for q in range(1, n_col // 2)]
    cols = [exchange(x, "row", s) for s, x in zip(upper, away)]
    total = call(
        transposed_last_kernel,
        "transposed_last",
        f32(*total.shape),
        [SMEM, VMEM, VMEM, VMEM],
        (order, held, vecs, total),
        aliases={3: 0},
    )
    *ready, total = lax.optimization_barrier((*lines, *cols, total))
    lines, cols = ready[:len(lines)], ready[len(lines):]
    away = small(functools.partial(route_cols_kernel, lower), [piece] * len(lower), "route_lower", total)
    cols += [away[0]] + [exchange(x, "row", s) for s, x in zip(lower[1:], away[1:])]
    h_basis, h_residual = small(sum_kernel, [f32(vec, share)] * 2, "sum_pieces", *lines, *cols)
    return (h_basis, h_residual)


def solution(mesh):
    placed = (
        P("row", "col", None, None, None),
        P("row", "col", None, None),
        P("row", "col"),
        P(None, ("row", "col")),
        P(None, ("row", "col")),
    )
    return jax.shard_map(
        local,
        mesh=mesh,
        in_specs=placed,
        out_specs=(P(None, ("row", "col")), P(None, ("row", "col"))),
        check_vma=False,
    )
```

```python
import functools

import jax
import jax.numpy as jnp
from jax import lax
from jax.experimental import pallas as pl
from jax.experimental.pallas import tpu as pltpu
from jax.sharding import PartitionSpec as P

CHUNK = 16
GROUP = 32
MIB = 1024 * 1024
VMEM = pl.BlockSpec(memory_space=pltpu.VMEM)
SMEM = pl.BlockSpec(memory_space=pltpu.SMEM)
ANY = pl.BlockSpec(memory_space=pl.ANY)


def small(kernel, out_shape, name, *args, in_specs=None):
    single = not isinstance(out_shape, list)
    return pl.pallas_call(
        kernel,
        out_shape=out_shape,
        in_specs=in_specs or [VMEM] * len(args),
        out_specs=VMEM if single else [VMEM] * len(out_shape),
        compiler_params=pltpu.CompilerParams(vmem_limit_bytes=2 * MIB),
        name=name,
    )(*args)


def f32(*shape):
    return jax.ShapeDtypeStruct(shape, jnp.float32)


def gather_kernel(*refs):
    *ins, out_ref = refs
    for q, ref in enumerate(ins):
        out_ref[q] = ref[...]


def split(x):
    high = x.astype(jnp.bfloat16)
    low = (x - high.astype(jnp.float32)).astype(jnp.bfloat16)
    return high, low


def prepare(forward, origins, pieces, vecs_ref):
    side = vecs_ref.shape[-1]
    width, share = pieces[0].shape
    per_piece = share // side
    blocks = len(pieces) * per_piece
    for s, (origin, piece) in enumerate(zip(origins, pieces)):
        for b in range(per_piece):
            x = piece[:, b * side:(b + 1) * side]
            high = x.astype(jnp.bfloat16).astype(jnp.float32)
            rows = [high, x - high]
            if forward:
                rows = jnp.concatenate(rows + [jnp.zeros((side - 2 * width, side), jnp.float32)], axis=0).T
                rows = jnp.concatenate([rows, rows], axis=0)
            else:
                rows = jnp.concatenate(rows, axis=0)
            vecs_ref[origin * per_piece + b] = rows.astype(jnp.bfloat16)
            if s == 0:
                vecs_ref[blocks + b] = (rows * 0.5).astype(jnp.bfloat16)
    vecs_ref[blocks + per_piece] = jnp.zeros_like(vecs_ref[0])


def shifted(steps, n):
    return lax.rem(lax.axis_index("col") + steps % n, n)


def add_products(forward, per_piece, arrive, places_ref, count, held_ref, vecs_ref, total_ref):
    side = held_ref.shape[-1]
    blocks = vecs_ref.shape[0] - per_piece - 1
    row_base, col_base = lax.axis_index("row") * per_piece, lax.axis_index("col") * per_piece

    @pl.loop(0, (count + GROUP - 1) // GROUP)
    def _(g):
        if arrive is not None:
            for c in range(GROUP // CHUNK):
                arrive(g * (GROUP // CHUNK) + c).wait()
        for u in range(GROUP):
            t = g * GROUP + u
            i, j = places_ref[0, t], places_ref[1, t]
            diagonal = (i - j == col_base - row_base) & (j >= row_base) & (j < row_base + per_piece)
            source, at, base = (j, i, row_base) if forward else (i, j, col_base)
            source = jnp.where(diagonal, source + (blocks - base), source)
            source = jnp.where(t < count, source, blocks + per_piece)
            high, low = split(held_ref[t])
            both = jnp.concatenate([high, low], axis=1)
            if forward:
                total_ref[at] += jnp.dot(both, vecs_ref[source], preferred_element_type=jnp.float32)
            else:
                out = jnp.dot(vecs_ref[source], both, preferred_element_type=jnp.float32)
                width = out.shape[0] // 2
                total_ref[at] += out[:width, :side] + out[width:, :side] + out[:width, side:]


def forward_kernel(per_piece, list_ref, count_ref, tiles_ref, *refs):
    *pieces, total_ref, held_ref, vecs_ref, places_ref, list_sem, sems = refs
    count = count_ref[0, 0]

    def chunk_copy(k):
        part = pl.ds(k * CHUNK, CHUNK)
        return pltpu.make_async_copy(tiles_ref.at[part], held_ref.at[part], sems.at[k])

    @pl.loop(0, (count + GROUP - 1) // GROUP * (GROUP // CHUNK))
    def _(k):
        chunk_copy(k).start()

    list_copy = pltpu.make_async_copy(list_ref, places_ref, list_sem)
    list_copy.start()
    row_at = lax.axis_index("row")
    prepare(True, [row_at ^ s for s in range(len(pieces))], pieces, vecs_ref)
    total_ref[...] = jnp.zeros_like(total_ref)
    list_copy.wait()
    add_products(True, per_piece, chunk_copy, places_ref, count, held_ref, vecs_ref, total_ref)


def transposed_kernel(
    per_piece, list_ref, count_ref, held_ref, own_ref, came_ref, _, total_ref, vecs_ref, places_ref, list_sem
):
    list_copy = pltpu.make_async_copy(list_ref, places_ref, list_sem)
    list_copy.start()
    half = own_ref.shape[0]
    origins = [shifted(-2 * q, 2 * half) for q in range(half)]
    prepare(
        False,
        origins + [origin ^ 1 for origin in origins],
        [ref.at[q] for ref in (own_ref, came_ref) for q in range(half)],
        vecs_ref,
    )
    total_ref[...] = jnp.zeros_like(total_ref)
    list_copy.wait()
    add_products(False, per_piece, None, places_ref, count_ref[0, 0], held_ref, vecs_ref, total_ref)


def route_rows_kernel(total_ref, kept_ref, leaving_ref):
    n = 2 * kept_ref.shape[0]
    per_piece = total_ref.shape[0] // n
    width = kept_ref.shape[1]
    side = total_ref.shape[-1]
    for s in range(n):
        base = (shifted(s // 2 * 2, n) ^ (s % 2)) * per_piece
        out = (leaving_ref if s % 2 else kept_ref).at[s // 2]
        for b in range(per_piece):
            turned = total_ref[base + b].T
            out[:, b * side:(b + 1) * side] = turned[:width] + turned[width:2 * width]


def route_cols_kernel(total_ref, *outs):
    width, share = outs[0].shape
    side = total_ref.shape[-1]
    for s, out in enumerate(outs):
        base = (lax.axis_index("row") ^ s) * (share // side)
        for b in range(share // side):
            out[:, b * side:(b + 1) * side] = total_ref[base + b]


def add_kernel(kept_ref, came_ref, *outs):
    for q, out in enumerate(outs):
        out[...] = kept_ref[q] + came_ref[q]


def sum_kernel(*refs):
    *ins, basis_ref, residual_ref = refs
    vec = basis_ref.shape[0]
    total = ins[0][...]
    for ref in ins[1:]:
        total = total + ref[...]
    basis_ref[...] = total[:vec]
    residual_ref[...] = total[vec:]


def exchange(x, axis, offset):
    n = lax.axis_size(axis)
    return lax.ppermute(x, axis, [(a, a ^ offset) for a in range(n)])


def shift(x, steps):
    n = lax.axis_size("col")
    return lax.ppermute(x, "col", [(a, (a + steps) % n) for a in range(n)])


def local(ham_tiles, tile_list, tile_count, basis_block, residual_block):
    slots, side = ham_tiles.shape[2], ham_tiles.shape[-1]
    vec, share = basis_block.shape
    width = 2 * vec
    per_piece = share // side
    n_row, n_col = lax.axis_size("row"), lax.axis_size("col")
    row_blocks, col_blocks = n_col * per_piece, n_row * per_piece
    tiles = ham_tiles[0, 0]
    listing = tile_list[0, 0].T
    def cost(part):
        return pl.CostEstimate(
            flops=int(part * slots * 2 * side * side * width * 24),
            bytes_accessed=int(part * slots * side * side * 4),
            transcendentals=0,
        )

    own = lax.pad(basis_block, 0.0, ((0, vec, 0), (0, 0, 0))) + lax.pad(residual_block, 0.0, ((vec, 0, 0), (0, 0, 0)))
    col_pieces = [own] + [exchange(own, "row", s) for s in range(1, n_row)]
    line = [own] + [shift(own, s) for s in range(2, n_col, 2)]
    params = pltpu.CompilerParams(vmem_limit_bytes=16 * MIB)
    total, held = pl.pallas_call(
        functools.partial(forward_kernel, per_piece),
        out_shape=[f32(row_blocks, side, side), f32(slots, side, side)],
        in_specs=[ANY, SMEM, ANY] + [VMEM] * n_row,
        out_specs=[VMEM] * 2,
        scratch_shapes=[
            pltpu.VMEM((col_blocks + per_piece + 1, 2 * side, side), jnp.bfloat16),
            pltpu.SMEM(listing.shape, jnp.int32),
            pltpu.SemaphoreType.DMA(()),
            pltpu.SemaphoreType.DMA((slots // CHUNK,)),
        ],
        compiler_params=params,
        cost_estimate=cost(1.0),
        name="forward_product",
    )(listing, tile_count, tiles, *col_pieces)
    *line, total = lax.optimization_barrier((*line, total))
    panel = small(gather_kernel, f32(n_col // 2, width, share), "gather_line", *line)
    came = exchange(panel, "col", 1)
    kept, leaving = small(route_rows_kernel, [f32(n_col // 2, width, share)] * 2, "route_rows", total)
    from_core = exchange(leaving, "col", 1)

    piece = f32(width, share)
    line = small(add_kernel, [piece] * (n_col // 2), "add_cores", kept, from_core)
    total = pl.pallas_call(
        functools.partial(transposed_kernel, per_piece),
        out_shape=f32(col_blocks, width, side),
        in_specs=[ANY, SMEM, VMEM, VMEM, VMEM, ANY],
        out_specs=VMEM,
        scratch_shapes=[
            pltpu.VMEM((row_blocks + per_piece + 1, 2 * width, side), jnp.bfloat16),
            pltpu.SMEM(listing.shape, jnp.int32),
            pltpu.SemaphoreType.DMA(()),
        ],
        compiler_params=params,
        cost_estimate=cost(1.0),
        name="transposed_product",
    )(listing, tile_count, held, panel, came, line[0])
    lines = [line[0]] + [shift(line[q], 2 * q) for q in range(1, n_col // 2)]
    *lines, total = lax.optimization_barrier((*lines, total))
    away = small(route_cols_kernel, [piece] * n_row, "route_columns", total)
    cols = [away[0]] + [exchange(away[s], "row", s) for s in range(1, n_row)]
    h_basis, h_residual = small(sum_kernel, [f32(vec, share)] * 2, "sum_pieces", *lines, *cols)
    return (h_basis, h_residual)


def solution(mesh):
    placed = (
        P("row", "col", None, None, None),
        P("row", "col", None, None),
        P("row", "col"),
        P(None, ("row", "col")),
        P(None, ("row", "col")),
    )
    return jax.shard_map(
        local,
        mesh=mesh,
        in_specs=placed,
        out_specs=(P(None, ("row", "col")), P(None, ("row", "col"))),
        check_vma=False,
    )
```

```python
import functools

import jax
import jax.numpy as jnp
from jax import lax
from jax.experimental import pallas as pl
from jax.experimental.pallas import tpu as pltpu
from jax.sharding import PartitionSpec as P

CHUNK = 16
GROUP = 32
MIB = 1024 * 1024
VMEM = pl.BlockSpec(memory_space=pltpu.VMEM)
SMEM = pl.BlockSpec(memory_space=pltpu.SMEM)
ANY = pl.BlockSpec(memory_space=pl.ANY)


def small(kernel, out_shape, name, *args, in_specs=None):
    single = not isinstance(out_shape, list)
    return pl.pallas_call(
        kernel,
        out_shape=out_shape,
        in_specs=in_specs or [VMEM] * len(args),
        out_specs=VMEM if single else [VMEM] * len(out_shape),
        compiler_params=pltpu.CompilerParams(vmem_limit_bytes=2 * MIB),
        name=name,
    )(*args)


def f32(*shape):
    return jax.ShapeDtypeStruct(shape, jnp.float32)


def gather_kernel(*refs):
    *ins, out_ref = refs
    for q, ref in enumerate(reversed(ins)):
        out_ref[q] = ref[...]


def split(x):
    high = x.astype(jnp.bfloat16)
    low = (x - high.astype(jnp.float32)).astype(jnp.bfloat16)
    return high, low


def prepare(forward, origins, pieces, vecs_ref):
    side = vecs_ref.shape[-1]
    width, share = pieces[0].shape
    per_piece = share // side
    blocks = len(pieces) * per_piece
    for s, (origin, piece) in enumerate(zip(origins, pieces)):
        for b in range(per_piece):
            x = piece[:, b * side:(b + 1) * side]
            high = x.astype(jnp.bfloat16).astype(jnp.float32)
            rows = [high, x - high]
            if forward:
                rows = jnp.concatenate(rows + [jnp.zeros((side - 2 * width, side), jnp.float32)], axis=0).T
                rows = jnp.concatenate([rows, rows], axis=0)
            else:
                rows = jnp.concatenate(rows, axis=0)
            vecs_ref[origin * per_piece + b] = rows.astype(jnp.bfloat16)
            if s == 0:
                vecs_ref[blocks + b] = (rows * 0.5).astype(jnp.bfloat16)
    vecs_ref[blocks + per_piece] = jnp.zeros_like(vecs_ref[0])


def shifted(axis, steps, n):
    return lax.rem(lax.axis_index(axis) + steps % n, n)


def add_products(forward, per_piece, arrive, places_ref, count, held_ref, vecs_ref, total_ref):
    side = held_ref.shape[-1]
    blocks = vecs_ref.shape[0] - per_piece - 1
    row_base, col_base = lax.axis_index("row") * per_piece, lax.axis_index("col") * per_piece

    @pl.loop(0, (count + GROUP - 1) // GROUP)
    def _(g):
        if arrive is not None:
            for c in range(GROUP // CHUNK):
                arrive(g * (GROUP // CHUNK) + c).wait()
        for u in range(GROUP):
            t = g * GROUP + u
            i, j = places_ref[0, t], places_ref[1, t]
            diagonal = (i - j == col_base - row_base) & (j >= row_base) & (j < row_base + per_piece)
            source, at, base = (j, i, row_base) if forward else (i, j, col_base)
            source = jnp.where(diagonal, source + (blocks - base), source)
            source = jnp.where(t < count, source, blocks + per_piece)
            high, low = split(held_ref[t])
            both = jnp.concatenate([high, low], axis=1)
            if forward:
                total_ref[at] += jnp.dot(both, vecs_ref[source], preferred_element_type=jnp.float32)
            else:
                out = jnp.dot(vecs_ref[source], both, preferred_element_type=jnp.float32)
                width = out.shape[0] // 2
                total_ref[at] += out[:width, :side] + out[width:, :side] + out[:width, side:]


def forward_kernel(per_piece, list_ref, count_ref, tiles_ref, *refs):
    *pieces, total_ref, held_ref, vecs_ref, places_ref, list_sem, sems = refs
    pieces = pieces[::-1]
    count = count_ref[0, 0]

    def chunk_copy(k):
        part = pl.ds(k * CHUNK, CHUNK)
        return pltpu.make_async_copy(tiles_ref.at[part], held_ref.at[part], sems.at[k])

    @pl.loop(0, (count + GROUP - 1) // GROUP * (GROUP // CHUNK))
    def _(k):
        chunk_copy(k).start()

    list_copy = pltpu.make_async_copy(list_ref, places_ref, list_sem)
    list_copy.start()
    n = len(pieces)
    prepare(True, [shifted("row", -s, n) for s in range(n)], pieces, vecs_ref)
    total_ref[...] = jnp.zeros_like(total_ref)
    list_copy.wait()
    add_products(True, per_piece, chunk_copy, places_ref, count, held_ref, vecs_ref, total_ref)


def transposed_kernel(
    per_piece, list_ref, count_ref, held_ref, own_ref, came_ref, _, total_ref, vecs_ref, places_ref, list_sem
):
    list_copy = pltpu.make_async_copy(list_ref, places_ref, list_sem)
    list_copy.start()
    half = own_ref.shape[0]
    origins = [shifted("col", -2 * q, 2 * half) for q in range(half)]
    prepare(
        False,
        origins + [origin ^ 1 for origin in origins],
        [ref.at[q] for ref in (own_ref, came_ref) for q in range(half)],
        vecs_ref,
    )
    total_ref[...] = jnp.zeros_like(total_ref)
    list_copy.wait()
    add_products(False, per_piece, None, places_ref, count_ref[0, 0], held_ref, vecs_ref, total_ref)


def route_rows_kernel(total_ref, kept_ref, leaving_ref):
    n = 2 * kept_ref.shape[0]
    per_piece = total_ref.shape[0] // n
    width = kept_ref.shape[1]
    side = total_ref.shape[-1]
    for s in range(n):
        base = (shifted("col", s // 2 * 2, n) ^ (s % 2)) * per_piece
        out = (leaving_ref if s % 2 else kept_ref).at[s // 2]
        for b in range(per_piece):
            turned = total_ref[base + b].T
            out[:, b * side:(b + 1) * side] = turned[:width] + turned[width:2 * width]


def route_cols_kernel(total_ref, *outs):
    n = len(outs)
    width, share = outs[0].shape
    side = total_ref.shape[-1]
    for s, out in enumerate(outs):
        base = shifted("row", s, n) * (share // side)
        for b in range(share // side):
            out[:, b * side:(b + 1) * side] = total_ref[base + b]


def add_kernel(kept_ref, came_ref, *outs):
    for q, out in enumerate(outs):
        out[...] = kept_ref[q] + came_ref[q]


def sum_kernel(*refs):
    *ins, basis_ref, residual_ref = refs
    vec = basis_ref.shape[0]
    total = ins[0][...]
    for ref in ins[1:]:
        total = total + ref[...]
    basis_ref[...] = total[:vec]
    residual_ref[...] = total[vec:]


def to_other_core(x):
    return lax.ppermute(x, "col", [(a, a ^ 1) for a in range(lax.axis_size("col"))])


def shift(x, axis, steps):
    n = lax.axis_size(axis)
    return lax.ppermute(x, axis, [(a, (a + steps) % n) for a in range(n)])


def local(ham_tiles, tile_list, tile_count, basis_block, residual_block):
    slots, side = ham_tiles.shape[2], ham_tiles.shape[-1]
    vec, share = basis_block.shape
    width = 2 * vec
    per_piece = share // side
    n_row, n_col = lax.axis_size("row"), lax.axis_size("col")
    row_blocks, col_blocks = n_col * per_piece, n_row * per_piece
    tiles = ham_tiles[0, 0]
    listing = tile_list[0, 0].T
    def cost(part):
        return pl.CostEstimate(
            flops=int(part * slots * 2 * side * side * width * 24),
            bytes_accessed=int(part * slots * side * side * 4),
            transcendentals=0,
        )

    own = lax.pad(basis_block, 0.0, ((0, vec, 0), (0, 0, 0))) + lax.pad(residual_block, 0.0, ((vec, 0, 0), (0, 0, 0)))
    col_pieces = [own] + [shift(own, "row", s) for s in reversed(range(1, n_row))][::-1]
    line = [own] + [shift(own, "col", s) for s in reversed(range(2, n_col, 2))][::-1]
    params = pltpu.CompilerParams(vmem_limit_bytes=16 * MIB)
    total, held = pl.pallas_call(
        functools.partial(forward_kernel, per_piece),
        out_shape=[f32(row_blocks, side, side), f32(slots, side, side)],
        in_specs=[ANY, SMEM, ANY] + [VMEM] * n_row,
        out_specs=[VMEM] * 2,
        scratch_shapes=[
            pltpu.VMEM((col_blocks + per_piece + 1, 2 * side, side), jnp.bfloat16),
            pltpu.SMEM(listing.shape, jnp.int32),
            pltpu.SemaphoreType.DMA(()),
            pltpu.SemaphoreType.DMA((slots // CHUNK,)),
        ],
        compiler_params=params,
        cost_estimate=cost(1.0),
        name="forward_product",
    )(listing, tile_count, tiles, *col_pieces[::-1])
    *line, total = lax.optimization_barrier((*line[::-1], total))
    panel = small(gather_kernel, f32(n_col // 2, width, share), "gather_line", *line)
    came = to_other_core(panel)
    kept, leaving = small(route_rows_kernel, [f32(n_col // 2, width, share)] * 2, "route_rows", total)
    from_core = to_other_core(leaving)

    piece = f32(width, share)
    line = small(add_kernel, [piece] * (n_col // 2), "add_cores", kept, from_core)
    total = pl.pallas_call(
        functools.partial(transposed_kernel, per_piece),
        out_shape=f32(col_blocks, width, side),
        in_specs=[ANY, SMEM, VMEM, VMEM, VMEM, ANY],
        out_specs=VMEM,
        scratch_shapes=[
            pltpu.VMEM((row_blocks + per_piece + 1, 2 * width, side), jnp.bfloat16),
            pltpu.SMEM(listing.shape, jnp.int32),
            pltpu.SemaphoreType.DMA(()),
        ],
        compiler_params=params,
        cost_estimate=cost(1.0),
        name="transposed_product",
    )(listing, tile_count, held, panel, came, line[0])
    lines = [line[0]] + [shift(line[q], "col", 2 * q) for q in range(1, n_col // 2)]
    *lines, total = lax.optimization_barrier((*lines, total))
    away = small(route_cols_kernel, [piece] * n_row, "route_columns", total)
    cols = [away[0]] + [shift(away[s], "row", s) for s in reversed(range(1, n_row))]
    h_basis, h_residual = small(sum_kernel, [f32(vec, share)] * 2, "sum_pieces", *lines, *cols)
    return (h_basis, h_residual)


def solution(mesh):
    placed = (
        P("row", "col", None, None, None),
        P("row", "col", None, None),
        P("row", "col"),
        P(None, ("row", "col")),
        P(None, ("row", "col")),
    )
    return jax.shard_map(
        local,
        mesh=mesh,
        in_specs=placed,
        out_specs=(P(None, ("row", "col")), P(None, ("row", "col"))),
        check_vma=False,
    )
```

```python
import functools

import jax
import jax.numpy as jnp
from jax import lax
from jax.experimental import pallas as pl
from jax.experimental.pallas import tpu as pltpu
from jax.sharding import PartitionSpec as P

GROUP = 32
MIB = 1024 * 1024
VMEM = pl.BlockSpec(memory_space=pltpu.VMEM)
SMEM = pl.BlockSpec(memory_space=pltpu.SMEM)
ANY = pl.BlockSpec(memory_space=pl.ANY)


def small(kernel, out_shape, name, *args, in_specs=None):
    single = not isinstance(out_shape, list)
    return pl.pallas_call(
        kernel,
        out_shape=out_shape,
        in_specs=in_specs or [VMEM] * len(args),
        out_specs=VMEM if single else [VMEM] * len(out_shape),
        compiler_params=pltpu.CompilerParams(vmem_limit_bytes=2 * MIB),
        name=name,
    )(*args)


def f32(*shape):
    return jax.ShapeDtypeStruct(shape, jnp.float32)


def pass_kernel(in_ref, out_ref):
    out_ref[...] = in_ref[...]


def gather_kernel(*refs):
    *ins, out_ref = refs
    for q, ref in enumerate(reversed(ins)):
        out_ref[q] = ref[...]


def split(x):
    high = x.astype(jnp.bfloat16)
    low = (x - high.astype(jnp.float32)).astype(jnp.bfloat16)
    return high, low


def prepare(forward, origins, pieces, vecs_ref):
    side = vecs_ref.shape[-1]
    width, share = pieces[0].shape
    per_piece = share // side
    blocks = len(pieces) * per_piece
    for s, (origin, piece) in enumerate(zip(origins, pieces)):
        for b in range(per_piece):
            x = piece[:, b * side:(b + 1) * side]
            high = x.astype(jnp.bfloat16).astype(jnp.float32)
            rows = [high, x - high]
            if forward:
                rows = jnp.concatenate(rows + [jnp.zeros((side - 2 * width, side), jnp.float32)], axis=0).T
                rows = jnp.concatenate([rows, rows], axis=0)
            else:
                rows = jnp.concatenate(rows, axis=0)
            vecs_ref[origin * per_piece + b] = rows.astype(jnp.bfloat16)
            if s == 0:
                vecs_ref[blocks + b] = (rows * 0.5).astype(jnp.bfloat16)
    vecs_ref[blocks + per_piece] = jnp.zeros_like(vecs_ref[0])


def shifted(steps, n):
    return lax.rem(lax.axis_index("col") + steps % n, n)


def add_products(forward, per_piece, places_ref, count, held_ref, vecs_ref, total_ref):
    side = held_ref.shape[-1]
    blocks = vecs_ref.shape[0] - per_piece - 1
    row_base, col_base = lax.axis_index("row") * per_piece, lax.axis_index("col") * per_piece

    @pl.loop(0, (count + GROUP - 1) // GROUP)
    def _(g):
        for u in range(GROUP):
            t = g * GROUP + u
            i, j = places_ref[0, t], places_ref[1, t]
            diagonal = (i - j == col_base - row_base) & (j >= row_base) & (j < row_base + per_piece)
            source, at, base = (j, i, row_base) if forward else (i, j, col_base)
            source = jnp.where(diagonal, source + (blocks - base), source)
            source = jnp.where(t < count, source, blocks + per_piece)
            high, low = split(held_ref[t])
            both = jnp.concatenate([high, low], axis=1)
            if forward:
                total_ref[at] += jnp.dot(both, vecs_ref[source], preferred_element_type=jnp.float32)
            else:
                out = jnp.dot(vecs_ref[source], both, preferred_element_type=jnp.float32)
                width = out.shape[0] // 2
                total_ref[at] += out[:width, :side] + out[width:, :side] + out[:width, side:]


def forward_kernel(per_piece, list_ref, count_ref, held_ref, *refs):
    *pieces, total_ref, vecs_ref, places_ref, list_sem = refs
    list_copy = pltpu.make_async_copy(list_ref, places_ref, list_sem)
    list_copy.start()
    row_at = lax.axis_index("row")
    prepare(True, [row_at ^ s for s in range(len(pieces))], pieces, vecs_ref)
    total_ref[...] = jnp.zeros_like(total_ref)
    list_copy.wait()
    add_products(True, per_piece, places_ref, count_ref[0, 0], held_ref, vecs_ref, total_ref)


def transposed_kernel(
    per_piece, list_ref, count_ref, held_ref, own_ref, came_ref, _, total_ref, vecs_ref, places_ref, list_sem
):
    list_copy = pltpu.make_async_copy(list_ref, places_ref, list_sem)
    list_copy.start()
    half = own_ref.shape[0]
    origins = [shifted(-2 * q, 2 * half) for q in range(half)]
    prepare(
        False,
        origins + [origin ^ 1 for origin in origins],
        [ref.at[q] for ref in (own_ref, came_ref) for q in range(half)],
        vecs_ref,
    )
    total_ref[...] = jnp.zeros_like(total_ref)
    list_copy.wait()
    add_products(False, per_piece, places_ref, count_ref[0, 0], held_ref, vecs_ref, total_ref)


def route_rows_kernel(total_ref, kept_ref, leaving_ref):
    n = 2 * kept_ref.shape[0]
    per_piece = total_ref.shape[0] // n
    width = kept_ref.shape[1]
    side = total_ref.shape[-1]
    for s in range(n):
        base = (shifted(s // 2 * 2, n) ^ (s % 2)) * per_piece
        out = (leaving_ref if s % 2 else kept_ref).at[s // 2]
        for b in range(per_piece):
            turned = total_ref[base + b].T
            out[:, b * side:(b + 1) * side] = turned[:width] + turned[width:2 * width]


def route_cols_kernel(total_ref, *outs):
    width, share = outs[0].shape
    side = total_ref.shape[-1]
    for s, out in enumerate(outs):
        base = (lax.axis_index("row") ^ s) * (share // side)
        for b in range(share // side):
            out[:, b * side:(b + 1) * side] = total_ref[base + b]


def add_kernel(kept_ref, came_ref, *outs):
    for q, out in enumerate(outs):
        out[...] = kept_ref[q] + came_ref[q]


def sum_kernel(*refs):
    *ins, basis_ref, residual_ref = refs
    vec = basis_ref.shape[0]
    total = ins[0][...]
    for ref in ins[1:]:
        total = total + ref[...]
    basis_ref[...] = total[:vec]
    residual_ref[...] = total[vec:]


def exchange(x, axis, offset):
    return lax.ppermute(x, axis, [(a, a ^ offset) for a in range(lax.axis_size(axis))])


def shift(x, steps):
    n = lax.axis_size("col")
    return lax.ppermute(x, "col", [(a, (a + steps) % n) for a in range(n)])


def local(ham_tiles, tile_list, tile_count, basis_block, residual_block):
    slots, side = ham_tiles.shape[2], ham_tiles.shape[-1]
    vec, share = basis_block.shape
    width = 2 * vec
    per_piece = share // side
    n_row, n_col = lax.axis_size("row"), lax.axis_size("col")
    row_blocks, col_blocks = n_col * per_piece, n_row * per_piece
    tiles = ham_tiles[0, 0]
    listing = tile_list[0, 0].T
    def cost(part):
        return pl.CostEstimate(
            flops=int(part * slots * 2 * side * side * width * 24),
            bytes_accessed=int(part * slots * side * side * 4),
            transcendentals=0,
        )

    stacked = lax.pad(basis_block, 0.0, ((0, vec, 0), (0, 0, 0))) + lax.pad(
        residual_block, 0.0, ((vec, 0, 0), (0, 0, 0))
    )
    own = pl.pallas_call(
        pass_kernel,
        out_shape=f32(width, share),
        in_specs=[VMEM],
        out_specs=VMEM,
        compiler_params=pltpu.CompilerParams(vmem_limit_bytes=2 * MIB),
        cost_estimate=cost(4.0),
        name="own_share",
    )(stacked)
    col_pieces = [own] + [exchange(own, "row", s) for s in range(1, n_row)]
    line = [own] + [shift(own, s) for s in reversed(range(2, n_col, 2))][::-1]
    params = pltpu.CompilerParams(vmem_limit_bytes=16 * MIB)
    total = pl.pallas_call(
        functools.partial(forward_kernel, per_piece),
        out_shape=f32(row_blocks, side, side),
        in_specs=[ANY, SMEM, VMEM] + [VMEM] * n_row,
        out_specs=VMEM,
        scratch_shapes=[
            pltpu.VMEM((col_blocks + per_piece + 1, 2 * side, side), jnp.bfloat16),
            pltpu.SMEM(listing.shape, jnp.int32),
            pltpu.SemaphoreType.DMA(()),
        ],
        compiler_params=params,
        cost_estimate=cost(1.0),
        name="forward_product",
    )(listing, tile_count, tiles, *col_pieces)
    *line, total = lax.optimization_barrier((*line[::-1], total))
    panel = small(gather_kernel, f32(n_col // 2, width, share), "gather_line", *line)
    came = exchange(panel, "col", 1)
    kept, leaving = small(route_rows_kernel, [f32(n_col // 2, width, share)] * 2, "route_rows", total)
    from_core = exchange(leaving, "col", 1)

    piece = f32(width, share)
    line = small(add_kernel, [piece] * (n_col // 2), "add_cores", kept, from_core)
    total = pl.pallas_call(
        functools.partial(transposed_kernel, per_piece),
        out_shape=f32(col_blocks, width, side),
        in_specs=[ANY, SMEM, VMEM, VMEM, VMEM, ANY],
        out_specs=VMEM,
        scratch_shapes=[
            pltpu.VMEM((row_blocks + per_piece + 1, 2 * width, side), jnp.bfloat16),
            pltpu.SMEM(listing.shape, jnp.int32),
            pltpu.SemaphoreType.DMA(()),
        ],
        compiler_params=params,
        cost_estimate=cost(1.0),
        name="transposed_product",
    )(listing, tile_count, tiles, panel, came, line[0])
    lines = [line[0]] + [shift(line[q], 2 * q) for q in range(1, n_col // 2)]
    *lines, total = lax.optimization_barrier((*lines, total))
    away = small(route_cols_kernel, [piece] * n_row, "route_columns", total)
    cols = [away[0]] + [exchange(away[s], "row", s) for s in reversed(range(1, n_row))]
    h_basis, h_residual = small(sum_kernel, [f32(vec, share)] * 2, "sum_pieces", *lines, *cols)
    return (h_basis, h_residual)


def solution(mesh):
    placed = (
        P("row", "col", None, None, None),
        P("row", "col", None, None),
        P("row", "col"),
        P(None, ("row", "col")),
        P(None, ("row", "col")),
    )
    return jax.shard_map(
        local,
        mesh=mesh,
        in_specs=placed,
        out_specs=(P(None, ("row", "col")), P(None, ("row", "col"))),
        check_vma=False,
    )
```

```python
import functools

import jax
import jax.numpy as jnp
from jax import lax
from jax.experimental import pallas as pl
from jax.experimental.pallas import tpu as pltpu
from jax.sharding import PartitionSpec as P

GROUP = 32
MIB = 1024 * 1024
VMEM = pl.BlockSpec(memory_space=pltpu.VMEM)
SMEM = pl.BlockSpec(memory_space=pltpu.SMEM)
ANY = pl.BlockSpec(memory_space=pl.ANY)


def small(kernel, out_shape, name, *args, in_specs=None):
    single = not isinstance(out_shape, list)
    return pl.pallas_call(
        kernel,
        out_shape=out_shape,
        in_specs=in_specs or [VMEM] * len(args),
        out_specs=VMEM if single else [VMEM] * len(out_shape),
        compiler_params=pltpu.CompilerParams(vmem_limit_bytes=2 * MIB),
        name=name,
    )(*args)


def f32(*shape):
    return jax.ShapeDtypeStruct(shape, jnp.float32)


def pass_kernel(in_ref, out_ref):
    out_ref[...] = in_ref[...]


def gather_kernel(*refs):
    *ins, out_ref = refs
    for q, ref in enumerate(reversed(ins)):
        out_ref[q] = ref[...]


def split(x):
    high = x.astype(jnp.bfloat16)
    low = (x - high.astype(jnp.float32)).astype(jnp.bfloat16)
    return high, low


def turned_vectors(x, vecs_ref, at, weight=1.0):
    width, side = x.shape
    high = x.astype(jnp.bfloat16).astype(jnp.float32)
    both = jnp.concatenate([high, x - high] * (side // (2 * width)), axis=0).T * weight
    column = lax.broadcasted_iota(jnp.int32, both.shape, 1)
    vecs_ref[0, at] = jnp.where(column < side // 2, both, 0.0).astype(jnp.bfloat16)
    vecs_ref[1, at] = jnp.where(column < side // 2, 0.0, both).astype(jnp.bfloat16)


def plain_vectors(x, vecs_ref, at, weight=1.0):
    high = x.astype(jnp.bfloat16).astype(jnp.float32)
    vecs_ref[0, at] = (jnp.concatenate([high, x - high], axis=0) * weight).astype(jnp.bfloat16)


def prepare(store, origins, pieces, vecs_ref):
    side = vecs_ref.shape[-1]
    per_piece = pieces[0].shape[1] // side
    blocks = len(pieces) * per_piece
    for s, (origin, piece) in enumerate(zip(origins, pieces)):
        for b in range(per_piece):
            x = piece[:, b * side:(b + 1) * side]
            store(x, vecs_ref, origin * per_piece + b)
            if s == 0:
                store(x, vecs_ref, blocks + b, 0.5)
    for form in range(vecs_ref.shape[0]):
        vecs_ref[form, blocks + per_piece] = jnp.zeros_like(vecs_ref[0, 0])


def shifted(steps, n):
    return lax.rem(lax.axis_index("col") + steps % n, n)


def find_slot(forward, per_piece, t, places_ref, count, vecs_ref):
    blocks = vecs_ref.shape[1] - per_piece - 1
    row_base, col_base = lax.axis_index("row") * per_piece, lax.axis_index("col") * per_piece
    i, j = places_ref[0, t], places_ref[1, t]
    diagonal = (i - j == col_base - row_base) & (j >= row_base) & (j < row_base + per_piece)
    source, at, base = (j, i, row_base) if forward else (i, j, col_base)
    source = jnp.where(diagonal, source + (blocks - base), source)
    return jnp.where(t < count, source, blocks + per_piece), at


def forward_kernel(per_piece, list_ref, count_ref, held_ref, *refs):
    *pieces, total_ref, vecs_ref, places_ref, list_sem = refs
    list_copy = pltpu.make_async_copy(list_ref, places_ref, list_sem)
    list_copy.start()
    row_at = lax.axis_index("row")
    prepare(turned_vectors, [row_at ^ s for s in range(len(pieces))], pieces, vecs_ref)
    total_ref[...] = jnp.zeros_like(total_ref)
    list_copy.wait()
    count = count_ref[0, 0]
    side = held_ref.shape[-1]
    step = 16

    @pl.loop(0, (count + GROUP - 1) // GROUP)
    def _(g):
        for u in range(0, GROUP, 2):
            slots = [g * GROUP + u + h for h in range(2)]
            found = [find_slot(True, per_piece, t, places_ref, count, vecs_ref) for t in slots]
            rows = []
            for t in slots:
                high, low = split(held_ref[t])
                for r in range(0, side, step):
                    rows += [high[r:r + step], low[r:r + step]]
            out = jnp.dot(
                jnp.concatenate(rows, axis=0),
                vecs_ref[0, found[0][0]] + vecs_ref[1, found[1][0]],
                preferred_element_type=jnp.float32,
            )
            for h in range(2):
                at = found[h][1]
                for r in range(0, side, step):
                    lies = 2 * (side * h + r)
                    total_ref[h, at, r:r + step] += out[lies:lies + step] + out[lies + step:lies + 2 * step]


def transposed_kernel(
    per_piece, list_ref, count_ref, held_ref, own_ref, came_ref, _, total_ref, vecs_ref, places_ref, list_sem
):
    list_copy = pltpu.make_async_copy(list_ref, places_ref, list_sem)
    list_copy.start()
    half = own_ref.shape[0]
    origins = [shifted(-2 * q, 2 * half) for q in range(half)]
    prepare(
        plain_vectors,
        origins + [origin ^ 1 for origin in origins],
        [ref.at[q] for ref in (own_ref, came_ref) for q in range(half)],
        vecs_ref,
    )
    total_ref[...] = jnp.zeros_like(total_ref)
    list_copy.wait()
    count = count_ref[0, 0]
    width, side = total_ref.shape[1:]

    @pl.loop(0, (count + GROUP - 1) // GROUP)
    def _(g):
        for u in range(GROUP):
            t = g * GROUP + u
            source, at = find_slot(False, per_piece, t, places_ref, count, vecs_ref)
            out = jnp.dot(
                vecs_ref[0, source],
                jnp.concatenate(split(held_ref[t]), axis=1),
                preferred_element_type=jnp.float32,
            )
            total_ref[at] += out[:width, :side] + out[width:, :side] + out[:width, side:]


def route_rows_kernel(other, total_ref, out_ref):
    n = 2 * out_ref.shape[0]
    per_piece = total_ref.shape[1] // n
    width = out_ref.shape[1]
    side = total_ref.shape[-1]
    column = lax.broadcasted_iota(jnp.int32, (side, side), 1)
    for q in range(n // 2):
        base = (shifted(2 * q, n) ^ other) * per_piece
        for b in range(per_piece):
            turned = jnp.where(column < side // 2, total_ref[0, base + b], total_ref[1, base + b]).T
            block = turned[:width]
            for v in range(width, side, width):
                block = block + turned[v:v + width]
            out_ref[q, :, b * side:(b + 1) * side] = block


def route_cols_kernel(total_ref, *outs):
    width, share = outs[0].shape
    side = total_ref.shape[-1]
    for s, out in enumerate(outs):
        base = (lax.axis_index("row") ^ s) * (share // side)
        for b in range(share // side):
            out[:, b * side:(b + 1) * side] = total_ref[base + b]


def add_kernel(kept_ref, came_ref, *outs):
    for q, out in enumerate(outs):
        out[...] = kept_ref[q] + came_ref[q]


def sum_kernel(*refs):
    *ins, basis_ref, residual_ref = refs
    vec = basis_ref.shape[0]
    total = ins[0][...]
    for ref in ins[1:]:
        total = total + ref[...]
    basis_ref[...] = total[:vec]
    residual_ref[...] = total[vec:]


def exchange(x, axis, offset):
    return lax.ppermute(x, axis, [(a, a ^ offset) for a in range(lax.axis_size(axis))])


def shift(x, steps):
    n = lax.axis_size("col")
    return lax.ppermute(x, "col", [(a, (a + steps) % n) for a in range(n)])


def local(ham_tiles, tile_list, tile_count, basis_block, residual_block):
    slots, side = ham_tiles.shape[2], ham_tiles.shape[-1]
    vec, share = basis_block.shape
    width = 2 * vec
    per_piece = share // side
    n_row, n_col = lax.axis_size("row"), lax.axis_size("col")
    row_blocks, col_blocks = n_col * per_piece, n_row * per_piece
    tiles = ham_tiles[0, 0]
    listing = tile_list[0, 0].T
    def cost(part):
        return pl.CostEstimate(
            flops=int(part * slots * 2 * side * side * width * 24),
            bytes_accessed=int(part * slots * side * side * 4),
            transcendentals=0,
        )

    stacked = lax.pad(basis_block, 0.0, ((0, vec, 0), (0, 0, 0))) + lax.pad(
        residual_block, 0.0, ((vec, 0, 0), (0, 0, 0))
    )
    own = pl.pallas_call(
        pass_kernel,
        out_shape=f32(width, share),
        in_specs=[VMEM],
        out_specs=VMEM,
        compiler_params=pltpu.CompilerParams(vmem_limit_bytes=2 * MIB),
        cost_estimate=cost(4.0),
        name="own_share",
    )(stacked)
    col_pieces = [own] + [exchange(own, "row", s) for s in range(1, n_row)]
    line = [own] + [shift(own, s) for s in reversed(range(2, n_col, 2))][::-1]
    params = pltpu.CompilerParams(vmem_limit_bytes=16 * MIB)
    total = pl.pallas_call(
        functools.partial(forward_kernel, per_piece),
        out_shape=f32(2, row_blocks, side, side),
        in_specs=[ANY, SMEM, VMEM] + [VMEM] * n_row,
        out_specs=VMEM,
        scratch_shapes=[
            pltpu.VMEM((2, col_blocks + per_piece + 1, side, side), jnp.bfloat16),
            pltpu.SMEM(listing.shape, jnp.int32),
            pltpu.SemaphoreType.DMA(()),
        ],
        compiler_params=params,
        cost_estimate=cost(1.0),
        name="forward_product",
    )(listing, tile_count, tiles, *col_pieces)
    *line, total = lax.optimization_barrier((*line[::-1], total))
    panel = small(gather_kernel, f32(n_col // 2, width, share), "gather_line", *line)
    came = exchange(panel, "col", 1)
    pieces = f32(n_col // 2, width, share)
    leaving = small(functools.partial(route_rows_kernel, 1), pieces, "route_leaving", total)
    from_core = exchange(leaving, "col", 1)
    leaving, total = lax.optimization_barrier((leaving, total))
    kept = small(functools.partial(route_rows_kernel, 0), pieces, "route_kept", total)
    piece = f32(width, share)
    line = small(add_kernel, [piece] * (n_col // 2), "add_cores", kept, from_core)
    total = pl.pallas_call(
        functools.partial(transposed_kernel, per_piece),
        out_shape=f32(col_blocks, width, side),
        in_specs=[ANY, SMEM, VMEM, VMEM, VMEM, ANY],
        out_specs=VMEM,
        scratch_shapes=[
            pltpu.VMEM((1, row_blocks + per_piece + 1, 2 * width, side), jnp.bfloat16),
            pltpu.SMEM(listing.shape, jnp.int32),
            pltpu.SemaphoreType.DMA(()),
        ],
        compiler_params=params,
        cost_estimate=cost(1.0),
        name="transposed_product",
    )(listing, tile_count, tiles, panel, came, line[0])
    lines = [line[0]] + [shift(line[q], 2 * q) for q in range(1, n_col // 2)]
    *lines, total = lax.optimization_barrier((*lines, total))
    away = small(route_cols_kernel, [piece] * n_row, "route_columns", total)
    cols = [away[0]] + [exchange(away[s], "row", s) for s in reversed(range(1, n_row))]
    h_basis, h_residual = small(sum_kernel, [f32(vec, share)] * 2, "sum_pieces", *lines, *cols)
    return (h_basis, h_residual)


def solution(mesh):
    placed = (
        P("row", "col", None, None, None),
        P("row", "col", None, None),
        P("row", "col"),
        P(None, ("row", "col")),
        P(None, ("row", "col")),
    )
    return jax.shard_map(
        local,
        mesh=mesh,
        in_specs=placed,
        out_specs=(P(None, ("row", "col")), P(None, ("row", "col"))),
        check_vma=False,
    )
```

```python
import functools

import jax
import jax.numpy as jnp
from jax import lax
from jax.experimental import pallas as pl
from jax.experimental.pallas import tpu as pltpu
from jax.sharding import PartitionSpec as P

GROUP = 32
MIB = 1024 * 1024
VMEM = pl.BlockSpec(memory_space=pltpu.VMEM)
SMEM = pl.BlockSpec(memory_space=pltpu.SMEM)
ANY = pl.BlockSpec(memory_space=pl.ANY)


def small(kernel, out_shape, name, *args, in_specs=None):
    single = not isinstance(out_shape, list)
    return pl.pallas_call(
        kernel,
        out_shape=out_shape,
        in_specs=in_specs or [VMEM] * len(args),
        out_specs=VMEM if single else [VMEM] * len(out_shape),
        compiler_params=pltpu.CompilerParams(vmem_limit_bytes=2 * MIB),
        name=name,
    )(*args)


def f32(*shape):
    return jax.ShapeDtypeStruct(shape, jnp.float32)


def pass_kernel(in_ref, out_ref):
    out_ref[...] = in_ref[...]


def gather_kernel(*refs):
    *ins, out_ref = refs
    for q, ref in enumerate(reversed(ins)):
        out_ref[q] = ref[...]


def split(x):
    high = x.astype(jnp.bfloat16)
    low = (x - high.astype(jnp.float32)).astype(jnp.bfloat16)
    return high, low


def turned_vectors(x, vecs_ref, at, weight=1.0):
    width, side = x.shape
    high = x.astype(jnp.bfloat16).astype(jnp.float32)
    both = jnp.concatenate([high, x - high] * (side // (2 * width)), axis=0).T * weight
    column = lax.broadcasted_iota(jnp.int32, both.shape, 1)
    vecs_ref[0, at] = jnp.where(column < side // 2, both, 0.0).astype(jnp.bfloat16)
    vecs_ref[1, at] = jnp.where(column < side // 2, 0.0, both).astype(jnp.bfloat16)


def plain_vectors(x, vecs_ref, at, weight=1.0):
    high = x.astype(jnp.bfloat16).astype(jnp.float32)
    vecs_ref[0, at] = (jnp.concatenate([high, x - high], axis=0) * weight).astype(jnp.bfloat16)


def prepare(store, origins, pieces, vecs_ref):
    side = vecs_ref.shape[-1]
    per_piece = pieces[0].shape[1] // side
    blocks = len(pieces) * per_piece
    for s, (origin, piece) in enumerate(zip(origins, pieces)):
        for b in range(per_piece):
            x = piece[:, b * side:(b + 1) * side]
            store(x, vecs_ref, origin * per_piece + b)
            if s == 0:
                store(x, vecs_ref, blocks + b, 0.5)
    for form in range(vecs_ref.shape[0]):
        vecs_ref[form, blocks + per_piece] = jnp.zeros_like(vecs_ref[0, 0])


def shifted(steps, n):
    return lax.rem(lax.axis_index("col") + steps % n, n)


def find_slot(forward, per_piece, t, places_ref, count, vecs_ref):
    blocks = vecs_ref.shape[1] - per_piece - 1
    row_base, col_base = lax.axis_index("row") * per_piece, lax.axis_index("col") * per_piece
    i, j = places_ref[0, t], places_ref[1, t]
    diagonal = (i - j == col_base - row_base) & (j >= row_base) & (j < row_base + per_piece)
    source, at, base = (j, i, row_base) if forward else (i, j, col_base)
    source = jnp.where(diagonal, source + (blocks - base), source)
    return jnp.where(t < count, source, blocks + per_piece), at


def forward_kernel(per_piece, list_ref, count_ref, held_ref, *refs):
    *pieces, first_ref, second_ref, vecs_ref, places_ref, list_sem = refs
    list_copy = pltpu.make_async_copy(list_ref, places_ref, list_sem)
    list_copy.start()
    row_at = lax.axis_index("row")
    prepare(turned_vectors, [row_at ^ s for s in range(len(pieces))], pieces, vecs_ref)
    for total_ref in (first_ref, second_ref):
        total_ref[...] = jnp.zeros_like(total_ref)
    list_copy.wait()
    count = count_ref[0, 0]
    side = held_ref.shape[-1]
    step = 16

    @pl.loop(0, (count + GROUP - 1) // GROUP)
    def _(g):
        for u in range(0, GROUP, 2):
            slots = [g * GROUP + u + h for h in range(2)]
            found = [find_slot(True, per_piece, t, places_ref, count, vecs_ref) for t in slots]
            rows = []
            for t in slots:
                high, low = split(held_ref[t])
                for r in range(0, side, step):
                    rows += [high[r:r + step], low[r:r + step]]
            out = jnp.dot(
                jnp.concatenate(rows, axis=0),
                vecs_ref[0, found[0][0]] + vecs_ref[1, found[1][0]],
                preferred_element_type=jnp.float32,
            )
            for h, total_ref in enumerate((first_ref, second_ref)):
                at = found[h][1]
                for r in range(0, side, step):
                    lies = 2 * (side * h + r)
                    total_ref[at, r:r + step] += out[lies:lies + step] + out[lies + step:lies + 2 * step]


def transposed_kernel(
    per_piece, list_ref, count_ref, held_ref, own_ref, came_ref, _, total_ref, vecs_ref, places_ref, list_sem, *others
):
    list_copy = pltpu.make_async_copy(list_ref, places_ref, list_sem)
    list_copy.start()
    half = own_ref.shape[0]
    origins = [shifted(-2 * q, 2 * half) for q in range(half)]
    prepare(
        plain_vectors,
        origins + [origin ^ 1 for origin in origins],
        [ref.at[q] for ref in (own_ref, came_ref) for q in range(half)],
        vecs_ref,
    )
    totals = [total_ref, *others]
    for ref in totals:
        ref[...] = jnp.zeros_like(ref)
    list_copy.wait()
    count = count_ref[0, 0]
    width, side = total_ref.shape[1:]

    @pl.loop(0, (count + GROUP - 1) // GROUP)
    def _(g):
        for u in range(GROUP):
            t = g * GROUP + u
            source, at = find_slot(False, per_piece, t, places_ref, count, vecs_ref)
            out = jnp.dot(
                vecs_ref[0, source],
                jnp.concatenate(split(held_ref[t]), axis=1),
                preferred_element_type=jnp.float32,
            )
            totals[u % len(totals)][at] += out[:width, :side] + out[width:, :side] + out[:width, side:]

    for ref in others:
        total_ref[...] += ref[...]


def route_rows_kernel(other, first_ref, second_ref, out_ref):
    n = 2 * out_ref.shape[0]
    per_piece = first_ref.shape[0] // n
    width = out_ref.shape[1]
    side = first_ref.shape[-1]
    column = lax.broadcasted_iota(jnp.int32, (side, side), 1)
    for q in range(n // 2):
        base = (shifted(2 * q, n) ^ other) * per_piece
        for b in range(per_piece):
            turned = jnp.where(column < side // 2, first_ref[base + b], second_ref[base + b]).T
            block = turned[:width]
            for v in range(width, side, width):
                block = block + turned[v:v + width]
            out_ref[q, :, b * side:(b + 1) * side] = block


def route_cols_kernel(total_ref, *outs):
    width, share = outs[0].shape
    side = total_ref.shape[-1]
    for s, out in enumerate(outs):
        base = (lax.axis_index("row") ^ s) * (share // side)
        for b in range(share // side):
            out[:, b * side:(b + 1) * side] = total_ref[base + b]


def add_kernel(kept_ref, came_ref, *outs):
    for q, out in enumerate(outs):
        out[...] = kept_ref[q] + came_ref[q]


def sum_kernel(*refs):
    *ins, basis_ref, residual_ref = refs
    vec = basis_ref.shape[0]
    total = ins[0][...]
    for ref in ins[1:]:
        total = total + ref[...]
    basis_ref[...] = total[:vec]
    residual_ref[...] = total[vec:]


def exchange(x, axis, offset):
    return lax.ppermute(x, axis, [(a, a ^ offset) for a in range(lax.axis_size(axis))])


def shift(x, steps):
    n = lax.axis_size("col")
    return lax.ppermute(x, "col", [(a, (a + steps) % n) for a in range(n)])


def local(ham_tiles, tile_list, tile_count, basis_block, residual_block):
    slots, side = ham_tiles.shape[2], ham_tiles.shape[-1]
    vec, share = basis_block.shape
    width = 2 * vec
    per_piece = share // side
    n_row, n_col = lax.axis_size("row"), lax.axis_size("col")
    row_blocks, col_blocks = n_col * per_piece, n_row * per_piece
    tiles = ham_tiles[0, 0]
    listing = tile_list[0, 0].T
    def cost(part):
        return pl.CostEstimate(
            flops=int(part * slots * 2 * side * side * width * 24),
            bytes_accessed=int(part * slots * side * side * 4),
            transcendentals=0,
        )

    stacked = lax.pad(basis_block, 0.0, ((0, vec, 0), (0, 0, 0))) + lax.pad(
        residual_block, 0.0, ((vec, 0, 0), (0, 0, 0))
    )
    own = pl.pallas_call(
        pass_kernel,
        out_shape=f32(width, share),
        in_specs=[VMEM],
        out_specs=VMEM,
        compiler_params=pltpu.CompilerParams(vmem_limit_bytes=2 * MIB),
        cost_estimate=cost(4.0),
        name="own_share",
    )(stacked)
    col_pieces = [own] + [exchange(own, "row", s) for s in range(1, n_row)]
    line = [own] + [shift(own, s) for s in reversed(range(2, n_col, 2))][::-1]
    params = pltpu.CompilerParams(vmem_limit_bytes=16 * MIB)
    total, second = pl.pallas_call(
        functools.partial(forward_kernel, per_piece),
        out_shape=[f32(row_blocks, side, side)] * 2,
        in_specs=[ANY, SMEM, VMEM] + [VMEM] * n_row,
        out_specs=[VMEM] * 2,
        scratch_shapes=[
            pltpu.VMEM((2, col_blocks + per_piece + 1, side, side), jnp.bfloat16),
            pltpu.SMEM(listing.shape, jnp.int32),
            pltpu.SemaphoreType.DMA(()),
        ],
        compiler_params=params,
        cost_estimate=cost(1.0),
        name="forward_product",
    )(listing, tile_count, tiles, *col_pieces)
    *line, total = lax.optimization_barrier((*line[::-1], total))
    panel = small(gather_kernel, f32(n_col // 2, width, share), "gather_line", *line)
    came = exchange(panel, "col", 1)
    pieces = f32(n_col // 2, width, share)
    leaving = small(functools.partial(route_rows_kernel, 1), pieces, "route_leaving", total, second)
    from_core = exchange(leaving, "col", 1)
    leaving, total = lax.optimization_barrier((leaving, total))
    kept = small(functools.partial(route_rows_kernel, 0), pieces, "route_kept", total, second)
    piece = f32(width, share)
    line = small(add_kernel, [piece] * (n_col // 2), "add_cores", kept, from_core)
    total = pl.pallas_call(
        functools.partial(transposed_kernel, per_piece),
        out_shape=f32(col_blocks, width, side),
        in_specs=[ANY, SMEM, VMEM, VMEM, VMEM, ANY],
        out_specs=VMEM,
        scratch_shapes=[
            pltpu.VMEM((1, row_blocks + per_piece + 1, 2 * width, side), jnp.bfloat16),
            pltpu.SMEM(listing.shape, jnp.int32),
            pltpu.SemaphoreType.DMA(()),
        ]
        + [pltpu.VMEM((col_blocks, width, side), jnp.float32)] * 3,
        compiler_params=params,
        cost_estimate=cost(1.0),
        name="transposed_product",
    )(listing, tile_count, tiles, panel, came, line[0])
    lines = [line[0]] + [shift(line[q], 2 * q) for q in range(1, n_col // 2)]
    *lines, total = lax.optimization_barrier((*lines, total))
    away = small(route_cols_kernel, [piece] * n_row, "route_columns", total)
    cols = [away[0]] + [exchange(away[s], "row", s) for s in reversed(range(1, n_row))]
    h_basis, h_residual = small(sum_kernel, [f32(vec, share)] * 2, "sum_pieces", *lines, *cols)
    return (h_basis, h_residual)


def solution(mesh):
    placed = (
        P("row", "col", None, None, None),
        P("row", "col", None, None),
        P("row", "col"),
        P(None, ("row", "col")),
        P(None, ("row", "col")),
    )
    return jax.shard_map(
        local,
        mesh=mesh,
        in_specs=placed,
        out_specs=(P(None, ("row", "col")), P(None, ("row", "col"))),
        check_vma=False,
    )
```

```python
import functools

import jax
import jax.numpy as jnp
from jax import lax
from jax.experimental import pallas as pl
from jax.experimental.pallas import tpu as pltpu
from jax.sharding import PartitionSpec as P

GROUP = 32
LONG_GROUP = 64
MIB = 1024 * 1024
VMEM = pl.BlockSpec(memory_space=pltpu.VMEM)
SMEM = pl.BlockSpec(memory_space=pltpu.SMEM)
ANY = pl.BlockSpec(memory_space=pl.ANY)


def small(kernel, out_shape, name, *args, in_specs=None):
    single = not isinstance(out_shape, list)
    return pl.pallas_call(
        kernel,
        out_shape=out_shape,
        in_specs=in_specs or [VMEM] * len(args),
        out_specs=VMEM if single else [VMEM] * len(out_shape),
        compiler_params=pltpu.CompilerParams(vmem_limit_bytes=2 * MIB),
        name=name,
    )(*args)


def f32(*shape):
    return jax.ShapeDtypeStruct(shape, jnp.float32)


def pass_kernel(in_ref, out_ref):
    out_ref[...] = in_ref[...]


def gather_kernel(*refs):
    *ins, out_ref = refs
    for q, ref in enumerate(reversed(ins)):
        out_ref[q] = ref[...]


def split(x):
    high = x.astype(jnp.bfloat16)
    low = (x - high.astype(jnp.float32)).astype(jnp.bfloat16)
    return high, low


def turned_vectors(x, vecs_ref, at, weight=1.0):
    width, side = x.shape
    high = x.astype(jnp.bfloat16).astype(jnp.float32)
    both = jnp.concatenate([high, x - high] * (side // (2 * width)), axis=0).T * weight
    column = lax.broadcasted_iota(jnp.int32, both.shape, 1)
    vecs_ref[0, at] = jnp.where(column < side // 2, both, 0.0).astype(jnp.bfloat16)
    vecs_ref[1, at] = jnp.where(column < side // 2, 0.0, both).astype(jnp.bfloat16)


def plain_vectors(x, vecs_ref, at, weight=1.0):
    high = x.astype(jnp.bfloat16).astype(jnp.float32)
    vecs_ref[0, at] = (jnp.concatenate([high, x - high], axis=0) * weight).astype(jnp.bfloat16)


def prepare(store, origins, pieces, vecs_ref):
    side = vecs_ref.shape[-1]
    per_piece = pieces[0].shape[1] // side
    blocks = len(pieces) * per_piece
    for s, (origin, piece) in enumerate(zip(origins, pieces)):
        for b in range(per_piece):
            x = piece[:, b * side:(b + 1) * side]
            store(x, vecs_ref, origin * per_piece + b)
            if s == 0:
                store(x, vecs_ref, blocks + b, 0.5)
    for form in range(vecs_ref.shape[0]):
        vecs_ref[form, blocks + per_piece] = jnp.zeros_like(vecs_ref[0, 0])


def shifted(steps, n):
    return lax.rem(lax.axis_index("col") + steps % n, n)


def find_slot(forward, per_piece, t, places_ref, count, vecs_ref):
    blocks = vecs_ref.shape[1] - per_piece - 1
    row_base, col_base = lax.axis_index("row") * per_piece, lax.axis_index("col") * per_piece
    i, j = places_ref[0, t], places_ref[1, t]
    diagonal = (i - j == col_base - row_base) & (j >= row_base) & (j < row_base + per_piece)
    source, at, base = (j, i, row_base) if forward else (i, j, col_base)
    source = jnp.where(diagonal, source + (blocks - base), source)
    return jnp.where(t < count, source, blocks + per_piece), at


def forward_kernel(per_piece, list_ref, count_ref, held_ref, *refs):
    *pieces, first_ref, second_ref, vecs_ref, places_ref, list_sem = refs
    list_copy = pltpu.make_async_copy(list_ref, places_ref, list_sem)
    list_copy.start()
    row_at = lax.axis_index("row")
    prepare(turned_vectors, [row_at ^ s for s in range(len(pieces))], pieces, vecs_ref)
    for total_ref in (first_ref, second_ref):
        total_ref[...] = jnp.zeros_like(total_ref)
    list_copy.wait()
    count = count_ref[0, 0]
    side = held_ref.shape[-1]

    @pl.loop(0, (count + GROUP - 1) // GROUP)
    def _(g):
        for u in range(0, GROUP, 2):
            slots = [g * GROUP + u + h for h in range(2)]
            found = [find_slot(True, per_piece, t, places_ref, count, vecs_ref) for t in slots]
            rows = [jnp.concatenate(split(held_ref[t]), axis=1) for t in slots]
            both = vecs_ref[0, found[0][0]] + vecs_ref[1, found[1][0]]
            out = jnp.dot(
                jnp.concatenate(rows, axis=0),
                jnp.concatenate([both, both], axis=0),
                preferred_element_type=jnp.float32,
            )
            for h, total_ref in enumerate((first_ref, second_ref)):
                total_ref[found[h][1]] += out[side * h:side * (h + 1)]


def transposed_kernel(
    per_piece, list_ref, count_ref, held_ref, own_ref, came_ref, _, total_ref, vecs_ref, places_ref, list_sem, *others
):
    list_copy = pltpu.make_async_copy(list_ref, places_ref, list_sem)
    list_copy.start()
    half = own_ref.shape[0]
    origins = [shifted(-2 * q, 2 * half) for q in range(half)]
    prepare(
        plain_vectors,
        origins + [origin ^ 1 for origin in origins],
        [ref.at[q] for ref in (own_ref, came_ref) for q in range(half)],
        vecs_ref,
    )
    totals = [total_ref, *others]
    for ref in totals:
        ref[...] = jnp.zeros_like(ref)
    list_copy.wait()
    count = count_ref[0, 0]
    width, side = total_ref.shape[1:]

    @pl.loop(0, (count + LONG_GROUP - 1) // LONG_GROUP)
    def _(g):
        for u in range(LONG_GROUP):
            t = g * LONG_GROUP + u
            source, at = find_slot(False, per_piece, t, places_ref, count, vecs_ref)
            out = jnp.dot(
                vecs_ref[0, source],
                jnp.concatenate(split(held_ref[t]), axis=1),
                preferred_element_type=jnp.float32,
            )
            totals[u % len(totals)][at] += out[:width, :side] + out[width:, :side] + out[:width, side:]

    for ref in others:
        total_ref[...] += ref[...]


def route_rows_kernel(other, first_ref, second_ref, out_ref):
    n = 2 * out_ref.shape[0]
    per_piece = first_ref.shape[0] // n
    width = out_ref.shape[1]
    side = first_ref.shape[-1]
    column = lax.broadcasted_iota(jnp.int32, (side, side), 1)
    for q in range(n // 2):
        base = (shifted(2 * q, n) ^ other) * per_piece
        for b in range(per_piece):
            turned = jnp.where(column < side // 2, first_ref[base + b], second_ref[base + b]).T
            block = turned[:width]
            for v in range(width, side, width):
                block = block + turned[v:v + width]
            out_ref[q, :, b * side:(b + 1) * side] = block


def route_cols_kernel(total_ref, *outs):
    width, share = outs[0].shape
    side = total_ref.shape[-1]
    for s, out in enumerate(outs):
        base = (lax.axis_index("row") ^ s) * (share // side)
        for b in range(share // side):
            out[:, b * side:(b + 1) * side] = total_ref[base + b]


def add_kernel(kept_ref, came_ref, *outs):
    for q, out in enumerate(outs):
        out[...] = kept_ref[q] + came_ref[q]


def sum_kernel(*refs):
    *ins, basis_ref, residual_ref = refs
    vec = basis_ref.shape[0]
    total = ins[0][...]
    for ref in ins[1:]:
        total = total + ref[...]
    basis_ref[...] = total[:vec]
    residual_ref[...] = total[vec:]


def exchange(x, axis, offset):
    return lax.ppermute(x, axis, [(a, a ^ offset) for a in range(lax.axis_size(axis))])


def shift(x, steps):
    n = lax.axis_size("col")
    return lax.ppermute(x, "col", [(a, (a + steps) % n) for a in range(n)])


def local(ham_tiles, tile_list, tile_count, basis_block, residual_block):
    slots, side = ham_tiles.shape[2], ham_tiles.shape[-1]
    vec, share = basis_block.shape
    width = 2 * vec
    per_piece = share // side
    n_row, n_col = lax.axis_size("row"), lax.axis_size("col")
    row_blocks, col_blocks = n_col * per_piece, n_row * per_piece
    tiles = ham_tiles[0, 0]
    listing = tile_list[0, 0].T
    def cost(part):
        return pl.CostEstimate(
            flops=int(part * slots * 2 * side * side * width * 24),
            bytes_accessed=int(part * slots * side * side * 4),
            transcendentals=0,
        )

    stacked = lax.pad(basis_block, 0.0, ((0, vec, 0), (0, 0, 0))) + lax.pad(
        residual_block, 0.0, ((vec, 0, 0), (0, 0, 0))
    )
    own = pl.pallas_call(
        pass_kernel,
        out_shape=f32(width, share),
        in_specs=[VMEM],
        out_specs=VMEM,
        compiler_params=pltpu.CompilerParams(vmem_limit_bytes=2 * MIB),
        cost_estimate=cost(4.0),
        name="own_share",
    )(stacked)
    col_pieces = [own] + [exchange(own, "row", s) for s in range(1, n_row)]
    line = [own] + [shift(own, s) for s in reversed(range(2, n_col, 2))][::-1]
    params = pltpu.CompilerParams(vmem_limit_bytes=16 * MIB)
    total, second = pl.pallas_call(
        functools.partial(forward_kernel, per_piece),
        out_shape=[f32(row_blocks, side, side)] * 2,
        in_specs=[ANY, SMEM, VMEM] + [VMEM] * n_row,
        out_specs=[VMEM] * 2,
        scratch_shapes=[
            pltpu.VMEM((2, col_blocks + per_piece + 1, side, side), jnp.bfloat16),
            pltpu.SMEM(listing.shape, jnp.int32),
            pltpu.SemaphoreType.DMA(()),
        ],
        compiler_params=params,
        cost_estimate=cost(1.0),
        name="forward_product",
    )(listing, tile_count, tiles, *col_pieces)
    *line, total = lax.optimization_barrier((*line[::-1], total))
    panel = small(gather_kernel, f32(n_col // 2, width, share), "gather_line", *line)
    came = exchange(panel, "col", 1)
    pieces = f32(n_col // 2, width, share)
    leaving = small(functools.partial(route_rows_kernel, 1), pieces, "route_leaving", total, second)
    from_core = exchange(leaving, "col", 1)
    leaving, total = lax.optimization_barrier((leaving, total))
    kept = small(functools.partial(route_rows_kernel, 0), pieces, "route_kept", total, second)
    piece = f32(width, share)
    line = small(add_kernel, [piece] * (n_col // 2), "add_cores", kept, from_core)
    total = pl.pallas_call(
        functools.partial(transposed_kernel, per_piece),
        out_shape=f32(col_blocks, width, side),
        in_specs=[ANY, SMEM, VMEM, VMEM, VMEM, ANY],
        out_specs=VMEM,
        scratch_shapes=[
            pltpu.VMEM((1, row_blocks + per_piece + 1, 2 * width, side), jnp.bfloat16),
            pltpu.SMEM(listing.shape, jnp.int32),
            pltpu.SemaphoreType.DMA(()),
        ]
        + [pltpu.VMEM((col_blocks, width, side), jnp.float32)] * 3,
        compiler_params=params,
        cost_estimate=cost(1.0),
        name="transposed_product",
    )(listing, tile_count, tiles, panel, came, line[0])
    lines = [line[0]] + [shift(line[q], 2 * q) for q in range(1, n_col // 2)]
    *lines, total = lax.optimization_barrier((*lines, total))
    away = small(route_cols_kernel, [piece] * n_row, "route_columns", total)
    cols = [away[0]] + [exchange(away[s], "row", s) for s in reversed(range(1, n_row))]
    h_basis, h_residual = small(sum_kernel, [f32(vec, share)] * 2, "sum_pieces", *lines, *cols)
    return (h_basis, h_residual)


def solution(mesh):
    placed = (
        P("row", "col", None, None, None),
        P("row", "col", None, None),
        P("row", "col"),
        P(None, ("row", "col")),
        P(None, ("row", "col")),
    )
    return jax.shard_map(
        local,
        mesh=mesh,
        in_specs=placed,
        out_specs=(P(None, ("row", "col")), P(None, ("row", "col"))),
        check_vma=False,
    )
```

```python
import functools

import jax
import jax.numpy as jnp
from jax import lax
from jax.experimental import pallas as pl
from jax.experimental.pallas import tpu as pltpu
from jax.sharding import PartitionSpec as P

FORWARD_GROUP = 64
TRANSPOSED_GROUP = 160
MIB = 1024 * 1024
VMEM = pl.BlockSpec(memory_space=pltpu.VMEM)
SMEM = pl.BlockSpec(memory_space=pltpu.SMEM)
ANY = pl.BlockSpec(memory_space=pl.ANY)


def small(kernel, out_shape, name, *args, in_specs=None):
    single = not isinstance(out_shape, list)
    return pl.pallas_call(
        kernel,
        out_shape=out_shape,
        in_specs=in_specs or [VMEM] * len(args),
        out_specs=VMEM if single else [VMEM] * len(out_shape),
        compiler_params=pltpu.CompilerParams(vmem_limit_bytes=2 * MIB),
        name=name,
    )(*args)


def f32(*shape):
    return jax.ShapeDtypeStruct(shape, jnp.float32)


def pass_kernel(in_ref, out_ref):
    out_ref[...] = in_ref[...]


def gather_kernel(*refs):
    *ins, out_ref = refs
    for q, ref in enumerate(reversed(ins)):
        out_ref[q] = ref[...]


def split(x):
    high = x.astype(jnp.bfloat16)
    low = (x - high.astype(jnp.float32)).astype(jnp.bfloat16)
    return high, low


def turned_vectors(x, vecs_ref, at, weight=1.0):
    width, side = x.shape
    high = x.astype(jnp.bfloat16).astype(jnp.float32)
    both = jnp.concatenate([high, x - high] * (side // (2 * width)), axis=0).T * weight
    column = lax.broadcasted_iota(jnp.int32, both.shape, 1)
    vecs_ref[0, at] = jnp.where(column < side // 2, both, 0.0).astype(jnp.bfloat16)
    vecs_ref[1, at] = jnp.where(column < side // 2, 0.0, both).astype(jnp.bfloat16)


def plain_vectors(x, vecs_ref, at, weight=1.0):
    high = x.astype(jnp.bfloat16).astype(jnp.float32)
    vecs_ref[0, at] = (jnp.concatenate([high, x - high], axis=0) * weight).astype(jnp.bfloat16)


def prepare(store, origins, pieces, vecs_ref):
    side = vecs_ref.shape[-1]
    per_piece = pieces[0].shape[1] // side
    blocks = len(pieces) * per_piece
    for s, (origin, piece) in enumerate(zip(origins, pieces)):
        for b in range(per_piece):
            x = piece[:, b * side:(b + 1) * side]
            store(x, vecs_ref, origin * per_piece + b)
            if s == 0:
                store(x, vecs_ref, blocks + b, 0.5)
    for form in range(vecs_ref.shape[0]):
        vecs_ref[form, blocks + per_piece] = jnp.zeros_like(vecs_ref[0, 0])


def shifted(steps, n):
    return lax.rem(lax.axis_index("col") + steps % n, n)


def find_slot(forward, per_piece, t, places_ref, count, vecs_ref):
    blocks = vecs_ref.shape[1] - per_piece - 1
    row_base, col_base = lax.axis_index("row") * per_piece, lax.axis_index("col") * per_piece
    i, j = places_ref[0, t], places_ref[1, t]
    diagonal = (i - j == col_base - row_base) & (j >= row_base) & (j < row_base + per_piece)
    source, at, base = (j, i, row_base) if forward else (i, j, col_base)
    source = jnp.where(diagonal, source + (blocks - base), source)
    return jnp.where(t < count, source, blocks + per_piece), at


def forward_kernel(per_piece, list_ref, count_ref, held_ref, *refs):
    *pieces, first_ref, second_ref, vecs_ref, places_ref, list_sem = refs
    list_copy = pltpu.make_async_copy(list_ref, places_ref, list_sem)
    list_copy.start()
    row_at = lax.axis_index("row")
    prepare(turned_vectors, [row_at ^ s for s in range(len(pieces))], pieces, vecs_ref)
    for total_ref in (first_ref, second_ref):
        total_ref[...] = jnp.zeros_like(total_ref)
    list_copy.wait()
    count = count_ref[0, 0]
    side = held_ref.shape[-1]

    @pl.loop(0, (count + FORWARD_GROUP - 1) // FORWARD_GROUP)
    def _(g):
        for u in range(0, FORWARD_GROUP, 2):
            slots = [g * FORWARD_GROUP + u + h for h in range(2)]
            found = [find_slot(True, per_piece, t, places_ref, count, vecs_ref) for t in slots]
            rows = [jnp.concatenate(split(held_ref[t]), axis=1) for t in slots]
            both = vecs_ref[0, found[0][0]] + vecs_ref[1, found[1][0]]
            out = jnp.dot(
                jnp.concatenate(rows, axis=0),
                jnp.concatenate([both, both], axis=0),
                preferred_element_type=jnp.float32,
            )
            for h, total_ref in enumerate((first_ref, second_ref)):
                total_ref[found[h][1]] += out[side * h:side * (h + 1)]


def transposed_kernel(
    per_piece, list_ref, count_ref, held_ref, own_ref, came_ref, _, total_ref, vecs_ref, places_ref, list_sem, *others
):
    list_copy = pltpu.make_async_copy(list_ref, places_ref, list_sem)
    list_copy.start()
    half = own_ref.shape[0]
    origins = [shifted(-2 * q, 2 * half) for q in range(half)]
    prepare(
        plain_vectors,
        origins + [origin ^ 1 for origin in origins],
        [ref.at[q] for ref in (own_ref, came_ref) for q in range(half)],
        vecs_ref,
    )
    totals = [total_ref, *others]
    for ref in totals:
        ref[...] = jnp.zeros_like(ref)
    list_copy.wait()
    count = count_ref[0, 0]
    width, side = total_ref.shape[1:]

    @pl.loop(0, (count + TRANSPOSED_GROUP - 1) // TRANSPOSED_GROUP)
    def _(g):
        for u in range(TRANSPOSED_GROUP):
            t = g * TRANSPOSED_GROUP + u
            source, at = find_slot(False, per_piece, t, places_ref, count, vecs_ref)
            out = jnp.dot(
                vecs_ref[0, source],
                jnp.concatenate(split(held_ref[t]), axis=1),
                preferred_element_type=jnp.float32,
            )
            totals[u % len(totals)][at] += out[:width, :side] + out[width:, :side] + out[:width, side:]

    for ref in others:
        total_ref[...] += ref[...]


def route_rows_kernel(other, first_ref, second_ref, out_ref):
    n = 2 * out_ref.shape[0]
    per_piece = first_ref.shape[0] // n
    width = out_ref.shape[1]
    side = first_ref.shape[-1]
    column = lax.broadcasted_iota(jnp.int32, (side, side), 1)
    for q in range(n // 2):
        base = (shifted(2 * q, n) ^ other) * per_piece
        for b in range(per_piece):
            turned = jnp.where(column < side // 2, first_ref[base + b], second_ref[base + b]).T
            block = turned[:width]
            for v in range(width, side, width):
                block = block + turned[v:v + width]
            out_ref[q, :, b * side:(b + 1) * side] = block


def route_cols_kernel(total_ref, *outs):
    width, share = outs[0].shape
    side = total_ref.shape[-1]
    for s, out in enumerate(outs):
        base = (lax.axis_index("row") ^ s) * (share // side)
        for b in range(share // side):
            out[:, b * side:(b + 1) * side] = total_ref[base + b]


def add_kernel(kept_ref, came_ref, *outs):
    for q, out in enumerate(outs):
        out[...] = kept_ref[q] + came_ref[q]


def line_kernel(*refs):
    *ins, out_ref = refs
    total = ins[0][...]
    for ref in ins[1:]:
        total = total + ref[...]
    out_ref[...] = total


def sum_kernel(*refs):
    *ins, basis_ref, residual_ref = refs
    vec = basis_ref.shape[0]
    total = ins[0][...]
    for ref in ins[1:]:
        total = total + ref[...]
    basis_ref[...] = total[:vec]
    residual_ref[...] = total[vec:]


def exchange(x, axis, offset):
    return lax.ppermute(x, axis, [(a, a ^ offset) for a in range(lax.axis_size(axis))])


def shift(x, steps):
    n = lax.axis_size("col")
    return lax.ppermute(x, "col", [(a, (a + steps) % n) for a in range(n)])


def local(ham_tiles, tile_list, tile_count, basis_block, residual_block):
    slots, side = ham_tiles.shape[2], ham_tiles.shape[-1]
    vec, share = basis_block.shape
    width = 2 * vec
    per_piece = share // side
    n_row, n_col = lax.axis_size("row"), lax.axis_size("col")
    row_blocks, col_blocks = n_col * per_piece, n_row * per_piece
    tiles = ham_tiles[0, 0]
    listing = tile_list[0, 0].T
    def cost(part):
        return pl.CostEstimate(
            flops=int(part * slots * 2 * side * side * width * 24),
            bytes_accessed=int(part * slots * side * side * 4),
            transcendentals=0,
        )

    stacked = lax.pad(basis_block, 0.0, ((0, vec, 0), (0, 0, 0))) + lax.pad(
        residual_block, 0.0, ((vec, 0, 0), (0, 0, 0))
    )
    own = pl.pallas_call(
        pass_kernel,
        out_shape=f32(width, share),
        in_specs=[VMEM],
        out_specs=VMEM,
        compiler_params=pltpu.CompilerParams(vmem_limit_bytes=2 * MIB),
        cost_estimate=cost(4.0),
        name="own_share",
    )(stacked)
    col_pieces = [own] + [exchange(own, "row", s) for s in range(1, n_row)]
    line = [own] + [shift(own, s) for s in reversed(range(2, n_col, 2))][::-1]
    params = pltpu.CompilerParams(vmem_limit_bytes=16 * MIB)
    total, second = pl.pallas_call(
        functools.partial(forward_kernel, per_piece),
        out_shape=[f32(row_blocks, side, side)] * 2,
        in_specs=[ANY, SMEM, VMEM] + [VMEM] * n_row,
        out_specs=[VMEM] * 2,
        scratch_shapes=[
            pltpu.VMEM((2, col_blocks + per_piece + 1, side, side), jnp.bfloat16),
            pltpu.SMEM(listing.shape, jnp.int32),
            pltpu.SemaphoreType.DMA(()),
        ],
        compiler_params=params,
        cost_estimate=cost(1.0),
        name="forward_product",
    )(listing, tile_count, tiles, *col_pieces)
    *line, total = lax.optimization_barrier((*line[::-1], total))
    panel = small(gather_kernel, f32(n_col // 2, width, share), "gather_line", *line)
    came = exchange(panel, "col", 1)
    pieces = f32(n_col // 2, width, share)
    leaving = small(functools.partial(route_rows_kernel, 1), pieces, "route_leaving", total, second)
    from_core = exchange(leaving, "col", 1)
    leaving, total = lax.optimization_barrier((leaving, total))
    kept = small(functools.partial(route_rows_kernel, 0), pieces, "route_kept", total, second)
    piece = f32(width, share)
    line = small(add_kernel, [piece] * (n_col // 2), "add_cores", kept, from_core)
    total = pl.pallas_call(
        functools.partial(transposed_kernel, per_piece),
        out_shape=f32(col_blocks, width, side),
        in_specs=[ANY, SMEM, VMEM, VMEM, VMEM, ANY],
        out_specs=VMEM,
        scratch_shapes=[
            pltpu.VMEM((1, row_blocks + per_piece + 1, 2 * width, side), jnp.bfloat16),
            pltpu.SMEM(listing.shape, jnp.int32),
            pltpu.SemaphoreType.DMA(()),
        ]
        + [pltpu.VMEM((col_blocks, width, side), jnp.float32)] * 3,
        compiler_params=params,
        cost_estimate=cost(1.0),
        name="transposed_product",
    )(listing, tile_count, tiles, panel, came, line[0])
    lines = [line[0]] + [shift(line[q], 2 * q) for q in range(1, n_col // 2)]
    away = small(route_cols_kernel, [piece] * n_row, "route_columns", total)
    cols = [exchange(away[s], "row", s) for s in reversed(range(1, n_row))]
    along = small(line_kernel, piece, "sum_line", *lines, away[0])
    h_basis, h_residual = small(sum_kernel, [f32(vec, share)] * 2, "sum_pieces", along, *cols)
    return (h_basis, h_residual)


def solution(mesh):
    placed = (
        P("row", "col", None, None, None),
        P("row", "col", None, None),
        P("row", "col"),
        P(None, ("row", "col")),
        P(None, ("row", "col")),
    )
    return jax.shard_map(
        local,
        mesh=mesh,
        in_specs=placed,
        out_specs=(P(None, ("row", "col")), P(None, ("row", "col"))),
        check_vma=False,
    )
```

```python
import functools

import jax
import jax.numpy as jnp
from jax import lax
from jax.experimental import pallas as pl
from jax.experimental.pallas import tpu as pltpu
from jax.sharding import PartitionSpec as P

FORWARD_GROUP = 160
TRANSPOSED_GROUP = 160
MIB = 1024 * 1024
VMEM = pl.BlockSpec(memory_space=pltpu.VMEM)
SMEM = pl.BlockSpec(memory_space=pltpu.SMEM)
ANY = pl.BlockSpec(memory_space=pl.ANY)


def small(kernel, out_shape, name, *args, in_specs=None):
    single = not isinstance(out_shape, list)
    return pl.pallas_call(
        kernel,
        out_shape=out_shape,
        in_specs=in_specs or [VMEM] * len(args),
        out_specs=VMEM if single else [VMEM] * len(out_shape),
        compiler_params=pltpu.CompilerParams(vmem_limit_bytes=2 * MIB),
        name=name,
    )(*args)


def f32(*shape):
    return jax.ShapeDtypeStruct(shape, jnp.float32)


def pass_kernel(in_ref, out_ref):
    out_ref[...] = in_ref[...]


def gather_kernel(*refs):
    *ins, out_ref = refs
    for q, ref in enumerate(reversed(ins)):
        out_ref[q] = ref[...]


def split(x):
    high = x.astype(jnp.bfloat16)
    low = (x - high.astype(jnp.float32)).astype(jnp.bfloat16)
    return high, low


def turned_vectors(x, vecs_ref, at, weight=1.0):
    width, side = x.shape
    high = x.astype(jnp.bfloat16).astype(jnp.float32)
    both = jnp.concatenate([high, x - high] * (side // (2 * width)), axis=0).T * weight
    column = lax.broadcasted_iota(jnp.int32, both.shape, 1)
    vecs_ref[0, at] = jnp.where(column < side // 2, both, 0.0).astype(jnp.bfloat16)
    vecs_ref[1, at] = jnp.where(column < side // 2, 0.0, both).astype(jnp.bfloat16)


def plain_vectors(x, vecs_ref, at, weight=1.0):
    high = x.astype(jnp.bfloat16).astype(jnp.float32)
    vecs_ref[0, at] = (jnp.concatenate([high, x - high], axis=0) * weight).astype(jnp.bfloat16)


def prepare(store, origins, pieces, vecs_ref):
    side = vecs_ref.shape[-1]
    per_piece = pieces[0].shape[1] // side
    blocks = len(pieces) * per_piece
    for s, (origin, piece) in enumerate(zip(origins, pieces)):
        for b in range(per_piece):
            x = piece[:, b * side:(b + 1) * side]
            store(x, vecs_ref, origin * per_piece + b)
            if s == 0:
                store(x, vecs_ref, blocks + b, 0.5)
    for form in range(vecs_ref.shape[0]):
        vecs_ref[form, blocks + per_piece] = jnp.zeros_like(vecs_ref[0, 0])


def shifted(steps, n):
    return lax.rem(lax.axis_index("col") + steps % n, n)


def find_slot(forward, per_piece, t, places_ref, count, vecs_ref):
    blocks = vecs_ref.shape[1] - per_piece - 1
    row_base, col_base = lax.axis_index("row") * per_piece, lax.axis_index("col") * per_piece
    i, j = places_ref[0, t], places_ref[1, t]
    diagonal = (i - j == col_base - row_base) & (j >= row_base) & (j < row_base + per_piece)
    source, at, base = (j, i, row_base) if forward else (i, j, col_base)
    source = jnp.where(diagonal, source + (blocks - base), source)
    return jnp.where(t < count, source, blocks + per_piece), at


def forward_kernel(per_piece, list_ref, count_ref, held_ref, *refs):
    *pieces, first_ref, second_ref, vecs_ref, places_ref, list_sem = refs
    list_copy = pltpu.make_async_copy(list_ref, places_ref, list_sem)
    list_copy.start()
    row_at = lax.axis_index("row")
    prepare(turned_vectors, [row_at ^ s for s in range(len(pieces))], pieces, vecs_ref)
    for total_ref in (first_ref, second_ref):
        total_ref[...] = jnp.zeros_like(total_ref)
    list_copy.wait()
    count = count_ref[0, 0]
    side = held_ref.shape[-1]

    @pl.loop(0, (count + FORWARD_GROUP - 1) // FORWARD_GROUP)
    def _(g):
        for u in range(0, FORWARD_GROUP, 2):
            slots = [g * FORWARD_GROUP + u + h for h in range(2)]
            found = [find_slot(True, per_piece, t, places_ref, count, vecs_ref) for t in slots]
            rows = [jnp.concatenate(split(held_ref[t]), axis=1) for t in slots]
            both = vecs_ref[0, found[0][0]] + vecs_ref[1, found[1][0]]
            out = jnp.dot(
                jnp.concatenate(rows, axis=0),
                jnp.concatenate([both, both], axis=0),
                preferred_element_type=jnp.float32,
            )
            for h, total_ref in enumerate((first_ref, second_ref)):
                total_ref[found[h][1]] += out[side * h:side * (h + 1)]


def transposed_kernel(
    per_piece, list_ref, count_ref, held_ref, own_ref, came_ref, _, total_ref, vecs_ref, places_ref, list_sem, *others
):
    list_copy = pltpu.make_async_copy(list_ref, places_ref, list_sem)
    list_copy.start()
    half = own_ref.shape[0]
    origins = [shifted(-2 * q, 2 * half) for q in range(half)]
    prepare(
        plain_vectors,
        origins + [origin ^ 1 for origin in origins],
        [ref.at[q] for ref in (own_ref, came_ref) for q in range(half)],
        vecs_ref,
    )
    totals = [total_ref, *others]
    for ref in totals:
        ref[...] = jnp.zeros_like(ref)
    list_copy.wait()
    count = count_ref[0, 0]
    width, side = total_ref.shape[1:]

    @pl.loop(0, (count + TRANSPOSED_GROUP - 1) // TRANSPOSED_GROUP)
    def _(g):
        for u in range(TRANSPOSED_GROUP):
            t = g * TRANSPOSED_GROUP + u
            source, at = find_slot(False, per_piece, t, places_ref, count, vecs_ref)
            out = jnp.dot(
                vecs_ref[0, source],
                jnp.concatenate(split(held_ref[t]), axis=1),
                preferred_element_type=jnp.float32,
            )
            totals[u % len(totals)][at] += out[:width, :side] + out[width:, :side] + out[:width, side:]

    for ref in others:
        total_ref[...] += ref[...]


def route_rows_kernel(other, first_ref, second_ref, out_ref):
    n = 2 * out_ref.shape[0]
    per_piece = first_ref.shape[0] // n
    width = out_ref.shape[1]
    side = first_ref.shape[-1]
    column = lax.broadcasted_iota(jnp.int32, (side, side), 1)
    for q in range(n // 2):
        base = (shifted(2 * q, n) ^ other) * per_piece
        for b in range(per_piece):
            turned = jnp.where(column < side // 2, first_ref[base + b], second_ref[base + b]).T
            block = turned[:width]
            for v in range(width, side, width):
                block = block + turned[v:v + width]
            out_ref[q, :, b * side:(b + 1) * side] = block


def route_cols_kernel(total_ref, *outs):
    width, share = outs[0].shape
    side = total_ref.shape[-1]
    for s, out in enumerate(outs):
        base = (lax.axis_index("row") ^ s) * (share // side)
        for b in range(share // side):
            out[:, b * side:(b + 1) * side] = total_ref[base + b]


def add_kernel(kept_ref, came_ref, *outs):
    for q, out in enumerate(outs):
        out[...] = kept_ref[q] + came_ref[q]


def line_kernel(*refs):
    *ins, out_ref = refs
    total = ins[0][...]
    for ref in ins[1:]:
        total = total + ref[...]
    out_ref[...] = total


def sum_kernel(*refs):
    *ins, basis_ref, residual_ref = refs
    vec = basis_ref.shape[0]
    total = ins[0][...]
    for ref in ins[1:]:
        total = total + ref[...]
    basis_ref[...] = total[:vec]
    residual_ref[...] = total[vec:]


def exchange(x, axis, offset):
    return lax.ppermute(x, axis, [(a, a ^ offset) for a in range(lax.axis_size(axis))])


def shift(x, steps):
    n = lax.axis_size("col")
    return lax.ppermute(x, "col", [(a, (a + steps) % n) for a in range(n)])


def local(ham_tiles, tile_list, tile_count, basis_block, residual_block):
    slots, side = ham_tiles.shape[2], ham_tiles.shape[-1]
    vec, share = basis_block.shape
    width = 2 * vec
    per_piece = share // side
    n_row, n_col = lax.axis_size("row"), lax.axis_size("col")
    row_blocks, col_blocks = n_col * per_piece, n_row * per_piece
    tiles = ham_tiles[0, 0]
    listing = tile_list[0, 0].T
    def cost(part):
        return pl.CostEstimate(
            flops=int(part * slots * 2 * side * side * width * 24),
            bytes_accessed=int(part * slots * side * side * 4),
            transcendentals=0,
        )

    stacked = lax.pad(basis_block, 0.0, ((0, vec, 0), (0, 0, 0))) + lax.pad(
        residual_block, 0.0, ((vec, 0, 0), (0, 0, 0))
    )
    own = pl.pallas_call(
        pass_kernel,
        out_shape=f32(width, share),
        in_specs=[VMEM],
        out_specs=VMEM,
        compiler_params=pltpu.CompilerParams(vmem_limit_bytes=2 * MIB),
        cost_estimate=cost(4.0),
        name="own_share",
    )(stacked)
    col_pieces = [own] + [exchange(own, "row", s) for s in range(1, n_row)]
    line = [own] + [shift(own, s) for s in reversed(range(2, n_col, 2))][::-1]
    params = pltpu.CompilerParams(vmem_limit_bytes=16 * MIB)
    total, second = pl.pallas_call(
        functools.partial(forward_kernel, per_piece),
        out_shape=[f32(row_blocks, side, side)] * 2,
        in_specs=[ANY, SMEM, VMEM] + [VMEM] * n_row,
        out_specs=[VMEM] * 2,
        scratch_shapes=[
            pltpu.VMEM((2, col_blocks + per_piece + 1, side, side), jnp.bfloat16),
            pltpu.SMEM(listing.shape, jnp.int32),
            pltpu.SemaphoreType.DMA(()),
        ],
        compiler_params=params,
        cost_estimate=cost(1.0),
        name="forward_product",
    )(listing, tile_count, tiles, *col_pieces)
    *line, total = lax.optimization_barrier((*line[::-1], total))
    panel = small(gather_kernel, f32(n_col // 2, width, share), "gather_line", *line)
    came = exchange(panel, "col", 1)
    pieces = f32(n_col // 2, width, share)
    leaving = small(functools.partial(route_rows_kernel, 1), pieces, "route_leaving", total, second)
    from_core = exchange(leaving, "col", 1)
    leaving, total = lax.optimization_barrier((leaving, total))
    kept = small(functools.partial(route_rows_kernel, 0), pieces, "route_kept", total, second)
    piece = f32(width, share)
    line = small(add_kernel, [piece] * (n_col // 2), "add_cores", kept, from_core)
    total = pl.pallas_call(
        functools.partial(transposed_kernel, per_piece),
        out_shape=f32(col_blocks, width, side),
        in_specs=[ANY, SMEM, VMEM, VMEM, VMEM, ANY],
        out_specs=VMEM,
        scratch_shapes=[
            pltpu.VMEM((1, row_blocks + per_piece + 1, 2 * width, side), jnp.bfloat16),
            pltpu.SMEM(listing.shape, jnp.int32),
            pltpu.SemaphoreType.DMA(()),
        ]
        + [pltpu.VMEM((col_blocks, width, side), jnp.float32)] * 3,
        compiler_params=params,
        cost_estimate=cost(1.0),
        name="transposed_product",
    )(listing, tile_count, tiles, panel, came, line[0])
    lines = [line[0]] + [shift(line[q], 2 * q) for q in range(1, n_col // 2)]
    away = small(route_cols_kernel, [piece] * n_row, "route_columns", total)
    cols = [exchange(away[s], "row", s) for s in sorted(range(1, n_row), key=lambda s: (s % 2 == 0, s))]
    along = small(line_kernel, piece, "sum_line", *lines, away[0])
    h_basis, h_residual = small(sum_kernel, [f32(vec, share)] * 2, "sum_pieces", along, *cols)
    return (h_basis, h_residual)


def solution(mesh):
    placed = (
        P("row", "col", None, None, None),
        P("row", "col", None, None),
        P("row", "col"),
        P(None, ("row", "col")),
        P(None, ("row", "col")),
    )
    return jax.shard_map(
        local,
        mesh=mesh,
        in_specs=placed,
        out_specs=(P(None, ("row", "col")), P(None, ("row", "col"))),
        check_vma=False,
    )
```

```python
import functools

import jax
import jax.numpy as jnp
from jax import lax
from jax.experimental import pallas as pl
from jax.experimental.pallas import tpu as pltpu
from jax.sharding import PartitionSpec as P

FORWARD_GROUP = 160
TRANSPOSED_GROUP = 160
MIB = 1024 * 1024
VMEM = pl.BlockSpec(memory_space=pltpu.VMEM)
SMEM = pl.BlockSpec(memory_space=pltpu.SMEM)
ANY = pl.BlockSpec(memory_space=pl.ANY)


def small(kernel, out_shape, name, *args, in_specs=None):
    single = not isinstance(out_shape, list)
    return pl.pallas_call(
        kernel,
        out_shape=out_shape,
        in_specs=in_specs or [VMEM] * len(args),
        out_specs=VMEM if single else [VMEM] * len(out_shape),
        compiler_params=pltpu.CompilerParams(vmem_limit_bytes=2 * MIB),
        name=name,
    )(*args)


def f32(*shape):
    return jax.ShapeDtypeStruct(shape, jnp.float32)


def pass_kernel(in_ref, out_ref):
    out_ref[...] = in_ref[...]


def gather_kernel(*refs):
    *ins, out_ref = refs
    for q, ref in enumerate(reversed(ins)):
        out_ref[q] = ref[...]


def split(x):
    high = x.astype(jnp.bfloat16)
    low = (x - high.astype(jnp.float32)).astype(jnp.bfloat16)
    return high, low


def turned_vectors(x, vecs_ref, at, weight=1.0):
    width, side = x.shape
    high = x.astype(jnp.bfloat16).astype(jnp.float32)
    both = jnp.concatenate([high, x - high] * (side // (2 * width)), axis=0).T * weight
    column = lax.broadcasted_iota(jnp.int32, both.shape, 1)
    vecs_ref[0, at] = jnp.where(column < side // 2, both, 0.0).astype(jnp.bfloat16)
    vecs_ref[1, at] = jnp.where(column < side // 2, 0.0, both).astype(jnp.bfloat16)


def plain_vectors(x, vecs_ref, at, weight=1.0):
    high = x.astype(jnp.bfloat16).astype(jnp.float32)
    vecs_ref[0, at] = (jnp.concatenate([high, x - high], axis=0) * weight).astype(jnp.bfloat16)


def prepare(store, origins, pieces, vecs_ref):
    side = vecs_ref.shape[-1]
    per_piece = pieces[0].shape[1] // side
    blocks = len(pieces) * per_piece
    for s, (origin, piece) in enumerate(zip(origins, pieces)):
        for b in range(per_piece):
            x = piece[:, b * side:(b + 1) * side]
            store(x, vecs_ref, origin * per_piece + b)
            if s == 0:
                store(x, vecs_ref, blocks + b, 0.5)
    for form in range(vecs_ref.shape[0]):
        vecs_ref[form, blocks + per_piece] = jnp.zeros_like(vecs_ref[0, 0])


def shifted(steps, n):
    return lax.rem(lax.axis_index("col") + steps % n, n)


def find_slot(forward, per_piece, t, places_ref, count, vecs_ref):
    blocks = vecs_ref.shape[1] - per_piece - 1
    row_base, col_base = lax.axis_index("row") * per_piece, lax.axis_index("col") * per_piece
    i, j = places_ref[0, t], places_ref[1, t]
    diagonal = (i - j == col_base - row_base) & (j >= row_base) & (j < row_base + per_piece)
    source, at, base = (j, i, row_base) if forward else (i, j, col_base)
    source = jnp.where(diagonal, source + (blocks - base), source)
    return jnp.where(t < count, source, blocks + per_piece), at


def forward_kernel(per_piece, list_ref, count_ref, held_ref, *refs):
    *pieces, first_ref, second_ref, vecs_ref, places_ref, list_sem = refs
    list_copy = pltpu.make_async_copy(list_ref, places_ref, list_sem)
    list_copy.start()
    row_at = lax.axis_index("row")
    prepare(turned_vectors, [row_at ^ s for s in range(len(pieces))], pieces, vecs_ref)
    for total_ref in (first_ref, second_ref):
        total_ref[...] = jnp.zeros_like(total_ref)
    list_copy.wait()
    count = count_ref[0, 0]
    side = held_ref.shape[-1]

    @pl.loop(0, (count + FORWARD_GROUP - 1) // FORWARD_GROUP)
    def _(g):
        for u in range(0, FORWARD_GROUP, 2):
            slots = [g * FORWARD_GROUP + u + h for h in range(2)]
            found = [find_slot(True, per_piece, t, places_ref, count, vecs_ref) for t in slots]
            rows = [jnp.concatenate(split(held_ref[t]), axis=1) for t in slots]
            both = vecs_ref[0, found[0][0]] + vecs_ref[1, found[1][0]]
            out = jnp.dot(
                jnp.concatenate(rows, axis=0),
                jnp.concatenate([both, both], axis=0),
                preferred_element_type=jnp.float32,
            )
            for h, total_ref in enumerate((first_ref, second_ref)):
                total_ref[found[h][1]] += out[side * h:side * (h + 1)]


def transposed_kernel(
    per_piece, list_ref, count_ref, held_ref, own_ref, came_ref, _, total_ref, vecs_ref, places_ref, list_sem, *others
):
    list_copy = pltpu.make_async_copy(list_ref, places_ref, list_sem)
    list_copy.start()
    half = own_ref.shape[0]
    origins = [shifted(-2 * q, 2 * half) for q in range(half)]
    prepare(
        plain_vectors,
        origins + [origin ^ 1 for origin in origins],
        [ref.at[q] for ref in (own_ref, came_ref) for q in range(half)],
        vecs_ref,
    )
    totals = [total_ref, *others]
    for ref in totals:
        ref[...] = jnp.zeros_like(ref)
    list_copy.wait()
    count = count_ref[0, 0]
    width, side = total_ref.shape[1:]

    @pl.loop(0, (count + TRANSPOSED_GROUP - 1) // TRANSPOSED_GROUP)
    def _(g):
        for u in range(TRANSPOSED_GROUP):
            t = g * TRANSPOSED_GROUP + u
            source, at = find_slot(False, per_piece, t, places_ref, count, vecs_ref)
            out = jnp.dot(
                vecs_ref[0, source],
                jnp.concatenate(split(held_ref[t]), axis=1),
                preferred_element_type=jnp.float32,
            )
            totals[u % len(totals)][at] += out[:width, :side] + out[width:, :side] + out[:width, side:]

    for ref in others:
        total_ref[...] += ref[...]


def route_rows_kernel(other, first_ref, second_ref, out_ref):
    n = 2 * out_ref.shape[0]
    per_piece = first_ref.shape[0] // n
    width = out_ref.shape[1]
    side = first_ref.shape[-1]
    column = lax.broadcasted_iota(jnp.int32, (side, side), 1)
    for q in range(n // 2):
        base = (shifted(2 * q, n) ^ other) * per_piece
        for b in range(per_piece):
            turned = jnp.where(column < side // 2, first_ref[base + b], second_ref[base + b]).T
            block = turned[:width]
            for v in range(width, side, width):
                block = block + turned[v:v + width]
            out_ref[q, :, b * side:(b + 1) * side] = block


def route_cols_kernel(total_ref, *outs):
    width, share = outs[0].shape
    side = total_ref.shape[-1]
    for s, out in enumerate(outs):
        base = (lax.axis_index("row") ^ s) * (share // side)
        for b in range(share // side):
            out[:, b * side:(b + 1) * side] = total_ref[base + b]


def add_kernel(kept_ref, came_ref, *outs):
    for q, out in enumerate(outs):
        out[...] = kept_ref[q] + came_ref[q]


def line_kernel(*refs):
    *ins, out_ref = refs
    total = ins[0][...]
    for ref in ins[1:]:
        total = total + ref[...]
    out_ref[...] = total


def sum_kernel(*refs):
    *ins, basis_ref, residual_ref = refs
    vec = basis_ref.shape[0]
    total = ins[0][...]
    for ref in ins[1:]:
        total = total + ref[...]
    basis_ref[...] = total[:vec]
    residual_ref[...] = total[vec:]


def exchange(x, axis, offset):
    return lax.ppermute(x, axis, [(a, a ^ offset) for a in range(lax.axis_size(axis))])


def shift(x, steps):
    n = lax.axis_size("col")
    return lax.ppermute(x, "col", [(a, (a + steps) % n) for a in range(n)])


def local(ham_tiles, tile_list, tile_count, basis_block, residual_block):
    slots, side = ham_tiles.shape[2], ham_tiles.shape[-1]
    vec, share = basis_block.shape
    width = 2 * vec
    per_piece = share // side
    n_row, n_col = lax.axis_size("row"), lax.axis_size("col")
    row_blocks, col_blocks = n_col * per_piece, n_row * per_piece
    tiles = ham_tiles[0, 0]
    listing = tile_list[0, 0].T
    def cost(part):
        return pl.CostEstimate(
            flops=int(part * slots * 2 * side * side * width * 24),
            bytes_accessed=int(part * slots * side * side * 4),
            transcendentals=0,
        )

    stacked = lax.pad(basis_block, 0.0, ((0, vec, 0), (0, 0, 0))) + lax.pad(
        residual_block, 0.0, ((vec, 0, 0), (0, 0, 0))
    )
    own = pl.pallas_call(
        pass_kernel,
        out_shape=f32(width, share),
        in_specs=[VMEM],
        out_specs=VMEM,
        compiler_params=pltpu.CompilerParams(vmem_limit_bytes=2 * MIB),
        cost_estimate=cost(4.0),
        name="own_share",
    )(stacked)
    col_pieces = [own] + [exchange(own, "row", s) for s in range(1, n_row)]
    line = [own] + [shift(own, s) for s in reversed(range(2, n_col, 2))][::-1]
    params = pltpu.CompilerParams(vmem_limit_bytes=16 * MIB)
    total, second = pl.pallas_call(
        functools.partial(forward_kernel, per_piece),
        out_shape=[f32(row_blocks, side, side)] * 2,
        in_specs=[ANY, SMEM, VMEM] + [VMEM] * n_row,
        out_specs=[VMEM] * 2,
        scratch_shapes=[
            pltpu.VMEM((2, col_blocks + per_piece + 1, side, side), jnp.bfloat16),
            pltpu.SMEM(listing.shape, jnp.int32),
            pltpu.SemaphoreType.DMA(()),
        ],
        compiler_params=params,
        cost_estimate=cost(1.0),
        name="forward_product",
    )(listing, tile_count, tiles, *col_pieces)
    *line, total = lax.optimization_barrier((*line[::-1], total))
    panel = small(gather_kernel, f32(n_col // 2, width, share), "gather_line", *line)
    came = exchange(panel, "col", 1)
    pieces = f32(n_col // 2, width, share)
    leaving = small(functools.partial(route_rows_kernel, 1), pieces, "route_leaving", total, second)
    from_core = exchange(leaving, "col", 1)
    leaving, total = lax.optimization_barrier((leaving, total))
    kept = small(functools.partial(route_rows_kernel, 0), pieces, "route_kept", total, second)
    piece = f32(width, share)
    line = small(add_kernel, [piece] * (n_col // 2), "add_cores", kept, from_core)
    total = pl.pallas_call(
        functools.partial(transposed_kernel, per_piece),
        out_shape=f32(col_blocks, width, side),
        in_specs=[ANY, SMEM, VMEM, VMEM, VMEM, ANY],
        out_specs=VMEM,
        scratch_shapes=[
            pltpu.VMEM((1, row_blocks + per_piece + 1, 2 * width, side), jnp.bfloat16),
            pltpu.SMEM(listing.shape, jnp.int32),
            pltpu.SemaphoreType.DMA(()),
        ]
        + [pltpu.VMEM((col_blocks, width, side), jnp.float32)] * 3,
        compiler_params=params,
        cost_estimate=cost(1.0),
        name="transposed_product",
    )(listing, tile_count, tiles, panel, came, line[0])
    lines = [line[0]] + [shift(line[q], 2 * q) for q in range(1, n_col // 2)]
    away = small(route_cols_kernel, [piece] * n_row, "route_columns", total)
    cols = [exchange(away[s], "row", s) for s in reversed(range(1, n_row))]
    along = small(line_kernel, piece, "sum_line", *lines, away[0])
    h_basis, h_residual = small(sum_kernel, [f32(vec, share)] * 2, "sum_pieces", along, *cols)
    return (h_basis, h_residual)


def solution(mesh):
    placed = (
        P("row", "col", None, None, None),
        P("row", "col", None, None),
        P("row", "col"),
        P(None, ("row", "col")),
        P(None, ("row", "col")),
    )
    return jax.shard_map(
        local,
        mesh=mesh,
        in_specs=placed,
        out_specs=(P(None, ("row", "col")), P(None, ("row", "col"))),
        check_vma=False,
    )
```

```python
import functools

import jax
import jax.numpy as jnp
from jax import lax
from jax.experimental import pallas as pl
from jax.experimental.pallas import tpu as pltpu
from jax.sharding import PartitionSpec as P

FORWARD_GROUP = 80
TRANSPOSED_GROUP = 160
MIB = 1024 * 1024
VMEM = pl.BlockSpec(memory_space=pltpu.VMEM)
SMEM = pl.BlockSpec(memory_space=pltpu.SMEM)
ANY = pl.BlockSpec(memory_space=pl.ANY)


def small(kernel, out_shape, name, *args, in_specs=None):
    single = not isinstance(out_shape, list)
    return pl.pallas_call(
        kernel,
        out_shape=out_shape,
        in_specs=in_specs or [VMEM] * len(args),
        out_specs=VMEM if single else [VMEM] * len(out_shape),
        compiler_params=pltpu.CompilerParams(vmem_limit_bytes=2 * MIB),
        name=name,
    )(*args)


def f32(*shape):
    return jax.ShapeDtypeStruct(shape, jnp.float32)


def pass_kernel(in_ref, out_ref):
    out_ref[...] = in_ref[...]


def gather_kernel(*refs):
    *ins, out_ref = refs
    for q, ref in enumerate(reversed(ins)):
        out_ref[q] = ref[...]


def split(x):
    high = x.astype(jnp.bfloat16)
    low = (x - high.astype(jnp.float32)).astype(jnp.bfloat16)
    return high, low


def turned_vectors(x, vecs_ref, at, weight=1.0):
    width, side = x.shape
    high = x.astype(jnp.bfloat16).astype(jnp.float32)
    both = jnp.concatenate([high, x - high] * (side // (2 * width)), axis=0).T * weight
    column = lax.broadcasted_iota(jnp.int32, both.shape, 1)
    vecs_ref[0, at] = jnp.where(column < side // 2, both, 0.0).astype(jnp.bfloat16)
    vecs_ref[1, at] = jnp.where(column < side // 2, 0.0, both).astype(jnp.bfloat16)


def plain_vectors(x, vecs_ref, at, weight=1.0):
    high = x.astype(jnp.bfloat16).astype(jnp.float32)
    vecs_ref[0, at] = (jnp.concatenate([high, x - high], axis=0) * weight).astype(jnp.bfloat16)


def prepare(store, origins, pieces, vecs_ref):
    side = vecs_ref.shape[-1]
    per_piece = pieces[0].shape[1] // side
    blocks = len(pieces) * per_piece
    for s, (origin, piece) in enumerate(zip(origins, pieces)):
        for b in range(per_piece):
            x = piece[:, b * side:(b + 1) * side]
            store(x, vecs_ref, origin * per_piece + b)
            if s == 0:
                store(x, vecs_ref, blocks + b, 0.5)
    for form in range(vecs_ref.shape[0]):
        vecs_ref[form, blocks + per_piece] = jnp.zeros_like(vecs_ref[0, 0])


def shifted(steps, n):
    return lax.rem(lax.axis_index("col") + steps % n, n)


def find_slot(forward, per_piece, t, places_ref, count, vecs_ref):
    blocks = vecs_ref.shape[1] - per_piece - 1
    row_base, col_base = lax.axis_index("row") * per_piece, lax.axis_index("col") * per_piece
    i, j = places_ref[0, t], places_ref[1, t]
    diagonal = (i - j == col_base - row_base) & (j >= row_base) & (j < row_base + per_piece)
    source, at, base = (j, i, row_base) if forward else (i, j, col_base)
    source = jnp.where(diagonal, source + (blocks - base), source)
    return jnp.where(t < count, source, blocks + per_piece), at


def forward_kernel(per_piece, list_ref, count_ref, held_ref, *refs):
    *pieces, first_ref, second_ref, vecs_ref, places_ref, list_sem = refs
    list_copy = pltpu.make_async_copy(list_ref, places_ref, list_sem)
    list_copy.start()
    row_at = lax.axis_index("row")
    prepare(turned_vectors, [row_at ^ s for s in range(len(pieces))], pieces, vecs_ref)
    for total_ref in (first_ref, second_ref):
        total_ref[...] = jnp.zeros_like(total_ref)
    list_copy.wait()
    count = count_ref[0, 0]
    side = held_ref.shape[-1]

    @pl.loop(0, (count + FORWARD_GROUP - 1) // FORWARD_GROUP)
    def _(g):
        for u in range(0, FORWARD_GROUP, 2):
            slots = [g * FORWARD_GROUP + u + h for h in range(2)]
            found = [find_slot(True, per_piece, t, places_ref, count, vecs_ref) for t in slots]
            rows = [jnp.concatenate(split(held_ref[t]), axis=1) for t in slots]
            both = vecs_ref[0, found[0][0]] + vecs_ref[1, found[1][0]]
            out = jnp.dot(
                jnp.concatenate(rows, axis=0),
                jnp.concatenate([both, both], axis=0),
                preferred_element_type=jnp.float32,
            )
            for h, total_ref in enumerate((first_ref, second_ref)):
                total_ref[found[h][1]] += out[side * h:side * (h + 1)]


def transposed_kernel(
    per_piece, list_ref, count_ref, held_ref, own_ref, came_ref, _, total_ref, vecs_ref, places_ref, list_sem, *others
):
    list_copy = pltpu.make_async_copy(list_ref, places_ref, list_sem)
    list_copy.start()
    half = own_ref.shape[0]
    origins = [shifted(-2 * q, 2 * half) for q in range(half)]
    prepare(
        plain_vectors,
        origins + [origin ^ 1 for origin in origins],
        [ref.at[q] for ref in (own_ref, came_ref) for q in range(half)],
        vecs_ref,
    )
    totals = [total_ref, *others]
    for ref in totals:
        ref[...] = jnp.zeros_like(ref)
    list_copy.wait()
    count = count_ref[0, 0]
    width, side = total_ref.shape[1:]

    @pl.loop(0, (count + TRANSPOSED_GROUP - 1) // TRANSPOSED_GROUP)
    def _(g):
        for u in range(TRANSPOSED_GROUP):
            t = g * TRANSPOSED_GROUP + u
            source, at = find_slot(False, per_piece, t, places_ref, count, vecs_ref)
            out = jnp.dot(
                vecs_ref[0, source],
                jnp.concatenate(split(held_ref[t]), axis=1),
                preferred_element_type=jnp.float32,
            )
            totals[u % len(totals)][at] += out[:width, :side] + out[width:, :side] + out[:width, side:]

    for ref in others:
        total_ref[...] += ref[...]


def route_rows_kernel(other, first_ref, second_ref, out_ref):
    n = 2 * out_ref.shape[0]
    per_piece = first_ref.shape[0] // n
    width = out_ref.shape[1]
    side = first_ref.shape[-1]
    column = lax.broadcasted_iota(jnp.int32, (side, side), 1)
    for q in range(n // 2):
        base = (shifted(2 * q, n) ^ other) * per_piece
        for b in range(per_piece):
            turned = jnp.where(column < side // 2, first_ref[base + b], second_ref[base + b]).T
            block = turned[:width]
            for v in range(width, side, width):
                block = block + turned[v:v + width]
            out_ref[q, :, b * side:(b + 1) * side] = block


def route_cols_kernel(total_ref, *outs):
    width, share = outs[0].shape
    side = total_ref.shape[-1]
    for s, out in enumerate(outs):
        base = (lax.axis_index("row") ^ s) * (share // side)
        for b in range(share // side):
            out[:, b * side:(b + 1) * side] = total_ref[base + b]


def add_kernel(kept_ref, came_ref, *outs):
    for q, out in enumerate(outs):
        out[...] = kept_ref[q] + came_ref[q]


def line_kernel(*refs):
    *ins, out_ref = refs
    total = ins[0][...]
    for ref in ins[1:]:
        total = total + ref[...]
    out_ref[...] = total


def sum_kernel(*refs):
    *ins, basis_ref, residual_ref = refs
    vec = basis_ref.shape[0]
    total = ins[0][...]
    for ref in ins[1:]:
        total = total + ref[...]
    basis_ref[...] = total[:vec]
    residual_ref[...] = total[vec:]


def exchange(x, axis, offset):
    return lax.ppermute(x, axis, [(a, a ^ offset) for a in range(lax.axis_size(axis))])


def shift(x, steps):
    n = lax.axis_size("col")
    return lax.ppermute(x, "col", [(a, (a + steps) % n) for a in range(n)])


def local(ham_tiles, tile_list, tile_count, basis_block, residual_block):
    slots, side = ham_tiles.shape[2], ham_tiles.shape[-1]
    vec, share = basis_block.shape
    width = 2 * vec
    per_piece = share // side
    n_row, n_col = lax.axis_size("row"), lax.axis_size("col")
    row_blocks, col_blocks = n_col * per_piece, n_row * per_piece
    tiles = ham_tiles[0, 0]
    listing = tile_list[0, 0].T
    def cost(part):
        return pl.CostEstimate(
            flops=int(part * slots * 2 * side * side * width * 24),
            bytes_accessed=int(part * slots * side * side * 4),
            transcendentals=0,
        )

    stacked = lax.pad(basis_block, 0.0, ((0, vec, 0), (0, 0, 0))) + lax.pad(
        residual_block, 0.0, ((vec, 0, 0), (0, 0, 0))
    )
    own = pl.pallas_call(
        pass_kernel,
        out_shape=f32(width, share),
        in_specs=[VMEM],
        out_specs=VMEM,
        compiler_params=pltpu.CompilerParams(vmem_limit_bytes=2 * MIB),
        cost_estimate=cost(4.0),
        name="own_share",
    )(stacked)
    col_pieces = [own] + [exchange(own, "row", s) for s in range(1, n_row)]
    line = [own] + [shift(own, s) for s in reversed(range(2, n_col, 2))][::-1]
    params = pltpu.CompilerParams(vmem_limit_bytes=16 * MIB)
    total, second = pl.pallas_call(
        functools.partial(forward_kernel, per_piece),
        out_shape=[f32(row_blocks, side, side)] * 2,
        in_specs=[ANY, SMEM, VMEM] + [VMEM] * n_row,
        out_specs=[VMEM] * 2,
        scratch_shapes=[
            pltpu.VMEM((2, col_blocks + per_piece + 1, side, side), jnp.bfloat16),
            pltpu.SMEM(listing.shape, jnp.int32),
            pltpu.SemaphoreType.DMA(()),
        ],
        compiler_params=params,
        cost_estimate=cost(1.0),
        name="forward_product",
    )(listing, tile_count, tiles, *col_pieces)
    *line, total = lax.optimization_barrier((*line[::-1], total))
    panel = small(gather_kernel, f32(n_col // 2, width, share), "gather_line", *line)
    came = exchange(panel, "col", 1)
    pieces = f32(n_col // 2, width, share)
    leaving = small(functools.partial(route_rows_kernel, 1), pieces, "route_leaving", total, second)
    from_core = exchange(leaving, "col", 1)
    leaving, total = lax.optimization_barrier((leaving, total))
    kept = small(functools.partial(route_rows_kernel, 0), pieces, "route_kept", total, second)
    piece = f32(width, share)
    line = small(add_kernel, [piece] * (n_col // 2), "add_cores", kept, from_core)
    total = pl.pallas_call(
        functools.partial(transposed_kernel, per_piece),
        out_shape=f32(col_blocks, width, side),
        in_specs=[ANY, SMEM, VMEM, VMEM, VMEM, ANY],
        out_specs=VMEM,
        scratch_shapes=[
            pltpu.VMEM((1, row_blocks + per_piece + 1, 2 * width, side), jnp.bfloat16),
            pltpu.SMEM(listing.shape, jnp.int32),
            pltpu.SemaphoreType.DMA(()),
        ]
        + [pltpu.VMEM((col_blocks, width, side), jnp.float32)] * 3,
        compiler_params=params,
        cost_estimate=cost(1.0),
        name="transposed_product",
    )(listing, tile_count, tiles, panel, came, line[0])
    lines = [line[0]] + [shift(line[q], 2 * q) for q in range(1, n_col // 2)]
    away = small(route_cols_kernel, [piece] * n_row, "route_columns", total)
    cols = [exchange(away[s], "row", s) for s in reversed(range(1, n_row))]
    along = small(line_kernel, piece, "sum_line", *lines, away[0])
    h_basis, h_residual = small(sum_kernel, [f32(vec, share)] * 2, "sum_pieces", along, *cols)
    return (h_basis, h_residual)


def solution(mesh):
    placed = (
        P("row", "col", None, None, None),
        P("row", "col", None, None),
        P("row", "col"),
        P(None, ("row", "col")),
        P(None, ("row", "col")),
    )
    return jax.shard_map(
        local,
        mesh=mesh,
        in_specs=placed,
        out_specs=(P(None, ("row", "col")), P(None, ("row", "col"))),
        check_vma=False,
    )
```
